128 devices in a mesh: row: 16 (over x_lo, y, core), col: 8 (over z, x_hi).
Axes of the slice: x: 4 (x_hi: 2, x_lo: 2; x = x_hi * 2 + x_lo), y: 4, z: 4, core: 2. Of those that a mesh axis runs over, the one named last changes fastest.
Arguments:
- left_proj: bfloat16 [1024, 4096], P(('row', 'col')), may hold values from -6 to 6
- right_proj: bfloat16 [1024, 4096], P(('col', 'row')), may hold values from -6 to 6
- out_weight: bfloat16 [1024, 128], replicated, may hold values from -0.1875 to 0.1875
- out_bias: float32 [128], replicated, may hold values from -3 to 3
- pair_cotangent: bfloat16 [1024, 1024, 128], P('row', 'col'), may hold values from -6 to 6
Outputs:
- pair_update: bfloat16 [1024, 1024, 128], P('row', 'col')
- grad_left: float32 [1024, 4096], P(('row', 'col'))
- grad_right: float32 [1024, 4096], P(('col', 'row'))
- grad_weight: float32 [1024, 128], replicated
- grad_bias: float32 [128], replicated
The draws below stay inside these ranges and needn't reach their ends.
All inputs are finite; a program needn't handle non-finite values.
Results may differ from the reference program's by a relative error of at most 0.0031.
Values may be sent and summed in bfloat16 or wider, within the bound.
A program may use at most 128 MiB of HBM per device.

```python
import jax
import jax.numpy as jnp
from jax import lax

C = 32
CZ = 128
S = 128
TILE_I = 64
R = 1024
N_ROW = 16


def level_of(own_key, shape, cuts, least, high):
    def one(axis_at, blocks):
        heights = jax.random.uniform(jax.random.fold_in(jax.random.fold_in(own_key, 6), axis_at), (blocks,), jnp.float32, least / len(cuts), high / len(cuts))
        return jnp.repeat(jnp.exp(heights), shape[axis_at] // blocks).reshape((-1,) + (1,) * (len(shape) - axis_at - 1))

    gain = one(*cuts[0])
    for cut in cuts[1:]:
        gain = gain * one(*cut)
    return gain


def noise(own_key, dims, scale, limit, cuts=(), kind=jnp.bfloat16):
    entries = scale * jax.random.normal(own_key, dims, jnp.float32)
    if cuts:
        entries = entries * level_of(own_key, dims, cuts, -0.22, 0.18)
    return jnp.clip(entries, -limit, limit).astype(kind)


def setup_inputs(seed: int = 0) -> dict:
    streams_of = jax.random.split(jax.random.key(seed), 6)
    return {
        "left_proj": noise(streams_of[0], (R, S * C), 1.0, 6.0, ((0, 128),)),
        "right_proj": noise(streams_of[1], (R, S * C), 1.0, 6.0, ((0, 128),)),
        "out_weight": noise(streams_of[2], (C * C, CZ), (C * C) ** -0.5, 0.1875),
        "out_bias": noise(streams_of[3], (CZ,), 0.5, 3.0, (), jnp.float32),
        "pair_cotangent": noise(streams_of[4], (R, R, CZ), 1.0, 6.0, ((0, 16), (1, 8))),
    }


def reference(left_proj, right_proj, out_weight, out_bias, pair_cotangent):
    inv = 1.0 / S
    left_all = left_proj.reshape(N_ROW, TILE_I, S, C)
    right3 = right_proj.reshape(R, S, C).astype(jnp.float32)
    cot_all = pair_cotangent.reshape(N_ROW, TILE_I, R, CZ)
    w_t = out_weight.T

    def block(carry, xs):
        grad_w, grad_b, grad_r = carry
        left_blk, cot_blk = xs
        left_f = left_blk.astype(jnp.float32)
        outer = (jnp.einsum("isa,jsb->ijab", left_f, right3) * inv).astype(jnp.bfloat16)
        flat = outer.reshape(TILE_I * R, C * C)
        pair = (jnp.dot(flat, out_weight, preferred_element_type=jnp.float32) + out_bias).astype(jnp.bfloat16)
        cot_flat = cot_blk.reshape(TILE_I * R, CZ)
        grad_w = grad_w + jnp.dot(flat.T, cot_flat, preferred_element_type=jnp.float32)
        grad_b = grad_b + jnp.sum(cot_flat.astype(jnp.float32), axis=0)
        d_outer = jnp.dot(cot_flat, w_t, preferred_element_type=jnp.float32).astype(jnp.bfloat16)
        d_four = d_outer.reshape(TILE_I, R, C, C).astype(jnp.float32)
        grad_l = jnp.einsum("ijab,jsb->isa", d_four, right3) * inv
        grad_r = grad_r + jnp.einsum("ijab,isa->jsb", d_four, left_f) * inv
        return (grad_w, grad_b, grad_r), (pair.reshape(TILE_I, R, CZ), grad_l.reshape(TILE_I, S * C))

    init = (jnp.zeros((C * C, CZ), jnp.float32), jnp.zeros((CZ,), jnp.float32), jnp.zeros((R, S, C), jnp.float32))
    (grad_w, grad_b, grad_r), (pairs, grads_l) = lax.scan(block, init, (left_all, cot_all))
    pair_update = pairs.reshape(R, R, CZ)
    grad_left = grads_l.reshape(R, S * C)
    return pair_update, grad_left, grad_r.reshape(R, S * C), grad_w, grad_b
```

```python
import functools

import jax
import jax.numpy as jnp
from jax import lax
from jax.experimental import pallas as pl
from jax.experimental.pallas import tpu as pltpu
from jax.sharding import PartitionSpec as P

C = 32
CZ = 128
S = 128
ROWS = 16
COLS = 8
TI = 64
TJ = 128
OWN = 8
MESH = pl.DeviceIdType.MESH
NN = (((1,), (0,)), ((), ()))
NT = (((1,), (1,)), ((), ()))
F32 = jnp.float32
BF16 = jnp.bfloat16


def dot(a, b, dims=NN):
    return lax.dot_general(a, b, dims, preferred_element_type=F32)


def kernel(
    a_ref, b_ref, w_ref, bias_ref, cot_hbm,
    pair_hbm, gl_ref, gr_ref, gw_ref, gb_ref,
    cot, d, p, a_all, a_t, b_in, b_all, b_t, w_t, pair,
    l_out, l_in, r_out, r_in, w1_out, w1_in, w2_out, w2_in, w3_out, w3_in, w4_in,
    cot_sem, pair_sem, a_s, a_r, b_s, b_r, l_s, l_r, r_s, r_r,
    w1_s, w1_r, w2_s, w2_r, w3_s, w3_r, w4_s, w4_r,
):
    row = lax.axis_index("row")
    col = lax.axis_index("col")

    def to_col(k, src, dst, ss, rs):
        return pltpu.make_async_remote_copy(
            src_ref=src, dst_ref=dst, send_sem=ss.at[k], recv_sem=rs.at[k],
            device_id=(row, lax.rem(col + k + 1, COLS)), device_id_type=MESH,
        )

    def to_row(k, src, dst, ss, rs):
        return pltpu.make_async_remote_copy(
            src_ref=src, dst_ref=dst, send_sem=ss.at[k], recv_sem=rs.at[k],
            device_id=(lax.rem(row + k + 1, ROWS), col), device_id_type=MESH,
        )

    def each(n, f):
        def step(k, carry):
            f(k)
            return carry

        lax.fori_loop(0, n, step, 0)

    def cot_copy(q):
        part = pl.ds(q * 16, 16)
        return pltpu.make_async_copy(cot_hbm.at[part], cot.at[part], cot_sem.at[q])

    def pair_copy(q):
        part = pl.ds(q * 16, 16)
        return pltpu.make_async_copy(pair.at[part], pair_hbm.at[part], pair_sem.at[q])

    each(4, lambda q: cot_copy(q).start())

    barrier = pltpu.get_barrier_semaphore()

    def greet_col(k):
        pl.semaphore_signal(barrier, inc=1, device_id=(row, lax.rem(col + k + 1, COLS)), device_id_type=MESH)

    def greet_row(k):
        pl.semaphore_signal(barrier, inc=1, device_id=(lax.rem(row + k + 1, ROWS), col), device_id_type=MESH)

    each(COLS - 1, greet_col)
    each(ROWS - 1, greet_row)
    pl.semaphore_wait(barrier, COLS + ROWS - 2)

    def send_b(k):
        to_row(k, b_ref, b_in.at[row], b_s, b_r).start()

    def send_a(k):
        to_col(k, a_ref, a_all.at[col], a_s, a_r).start()

    each(ROWS - 1, send_b)
    each(COLS - 1, send_a)
    a_all[col] = a_ref[...]
    b_in[row] = b_ref[...]
    w_t[...] = w_ref[...].T

    gb_ref[...] = jnp.zeros_like(gb_ref)
    group = 4

    def d_step(g, carry):
        @pl.when(lax.rem(g, 4) == 0)
        def _():
            cot_copy(g // 4).wait()

        block = cot[pl.ds(g * group, group)].reshape(group * TJ, CZ)
        r = dot(w_ref[...], block, NT).astype(BF16)
        for q in range(group):
            d[:, pl.ds((g * group + q) * C, C), :] = r[:, q * TJ:(q + 1) * TJ].reshape(C, C, TJ)
        gb_ref[...] += jnp.sum(block.astype(F32).reshape(group * TJ // 8, 8, CZ), axis=0)
        return carry

    lax.fori_loop(0, TI // group, d_step, 0)

    def wait_b(k):
        to_row(k, b_ref, b_in.at[lax.rem(row + ROWS - 1 - k, ROWS)], b_s, b_r).wait()

    def wait_a(k):
        to_col(k, a_ref, a_all.at[lax.rem(col + COLS - 1 - k, COLS)], a_s, a_r).wait()

    each(ROWS - 1, wait_b)
    each(COLS - 1, wait_a)

    def lay_b(q, carry):
        part = b_in[:, pl.ds(q * 16, 16), :].astype(F32)
        for h in range(2):
            b_all[pl.ds((q * 2 + h) * TJ, TJ), :] = part[:, h * 8:(h + 1) * 8, :].reshape(TJ, S).astype(BF16)
        return carry

    lax.fori_loop(0, C // 2, lay_b, 0)
    for q in range(COLS):
        a_t[:, q * 256:(q + 1) * 256] = a_all[q].T

    def p_step(n, carry):
        rhs = b_all[pl.ds(n * 512, 512), :]
        for m in range(4):
            r = dot(a_all[m * 2:m * 2 + 2].reshape(512, S), rhs, NT).astype(BF16)
            for q in range(4):
                p[n * 4 + q, m * 512:(m + 1) * 512, :] = r[:, q * TJ:(q + 1) * TJ]
        return carry

    lax.fori_loop(0, C * TJ // 512, p_step, 0)

    gw_ref[...] = jnp.zeros_like(gw_ref)

    def gw_step(g, carry):
        x = jnp.concatenate(
            [p[:, pl.ds((g * 8 + q) * C, C), :].reshape(C * C, TJ) for q in range(8)], axis=1
        )
        gw_ref[...] += dot(x, cot[pl.ds(g * 8, 8)].reshape(8 * TJ, CZ))
        return carry

    lax.fori_loop(0, TI // 8, gw_step, 0)
    for q in range(COLS):
        w1_out[q, :128, :] = gw_ref[q * 128:(q + 1) * 128, :]
        w1_out[q, 128:, :] = gb_ref[...]

    def send_w1(k):
        to_col(k, w1_out.at[lax.rem(col + k + 1, COLS)], w1_in.at[col], w1_s, w1_r).start()

    each(COLS - 1, send_w1)
    w1_in[col] = w1_out[col]

    def gr_step(n, carry):
        x = jnp.concatenate([d[n * 4 + q] for q in range(4)], axis=1)
        r = dot(a_t[...], x)
        t = [r[:, q * TJ:(q + 1) * TJ].T.reshape(ROWS, 8, S) for q in range(4)]
        for h in range(2):
            both = jnp.concatenate([t[2 * h], t[2 * h + 1]], axis=1)
            r_out[:, pl.ds(n * 32 + h * 16, 16), :] = both.astype(BF16)
        return carry

    lax.fori_loop(0, C // 4, gr_step, 0)

    def send_r(k):
        to_row(k, r_out.at[lax.rem(row + k + 1, ROWS)], r_in.at[row], r_s, r_r).start()

    each(ROWS - 1, send_r)
    r_in[row] = r_out[row]

    def wait_w1(k):
        to_col(k, w1_out.at[lax.rem(col + k + 1, COLS)], w1_in.at[lax.rem(col + COLS - 1 - k, COLS)], w1_s, w1_r).wait()

    each(COLS - 1, wait_w1)
    s1 = w1_in[0]
    for q in range(1, COLS):
        s1 += w1_in[q]
    for q in range(ROWS):
        w2_out[q, :8, :] = s1[q * 8:(q + 1) * 8, :]
        w2_out[q, 8:, :] = s1[128:, :]

    def send_w2(k):
        to_row(k, w2_out.at[lax.rem(row + k + 1, ROWS)], w2_in.at[row], w2_s, w2_r).start()

    each(ROWS - 1, send_w2)
    w2_in[row] = w2_out[row]

    def gl_step(m, carry):
        x = jnp.concatenate([d[q, pl.ds(m * 512, 512), :] for q in range(C)], axis=1)
        r = (dot(x, b_all[...]) * (1.0 / S)).astype(BF16)
        for h in range(2):
            l_out[m * 2 + h] = r[h * 256:(h + 1) * 256, :]
        return carry

    lax.fori_loop(0, TI * C // 512, gl_step, 0)

    def send_l(k):
        to_col(k, l_out.at[lax.rem(col + k + 1, COLS)], l_in.at[col], l_s, l_r).start()

    each(COLS - 1, send_l)
    l_in[col] = l_out[col]

    def wait_w2(k):
        to_row(k, w2_out.at[lax.rem(row + k + 1, ROWS)], w2_in.at[lax.rem(row + ROWS - 1 - k, ROWS)], w2_s, w2_r).wait()

    each(ROWS - 1, wait_w2)
    s2 = w2_in[0]
    for q in range(1, ROWS):
        s2 += w2_in[q]
    w3_out[...] = s2[:8, :]
    gb_ref[...] = s2[8:, :]

    def send_w3(k):
        to_row(k, w3_out, w3_in.at[row], w3_s, w3_r).start()

    each(ROWS - 1, send_w3)
    w3_in[row] = w3_out[...]

    def pair_step(g, carry):
        x = jnp.concatenate(
            [p[:, pl.ds((g * 4 + q) * C, C), :].reshape(C * C, TJ) for q in range(4)], axis=1
        )
        r = dot(w_t[...], x)
        for q in range(4):
            pair[g * 4 + q] = (r[:, q * TJ:(q + 1) * TJ].T + bias_ref[...]).astype(BF16)
        return carry

    for q in range(2):
        lax.fori_loop(q * 4, q * 4 + 4, pair_step, 0)
        pair_copy(q).start()

    def wait_r(k):
        to_row(k, r_out.at[lax.rem(row + k + 1, ROWS)], r_in.at[lax.rem(row + ROWS - 1 - k, ROWS)], r_s, r_r).wait()

    each(ROWS - 1, wait_r)
    total = r_in[0].astype(F32)
    for q in range(1, ROWS):
        total += r_in[q].astype(F32)
    gr_ref[...] = total

    def wait_w3(k):
        to_row(k, w3_out, w3_in.at[lax.rem(row + ROWS - 1 - k, ROWS)], w3_s, w3_r).wait()

    each(ROWS - 1, wait_w3)

    def send_w4(k):
        to_col(k, w3_in, w4_in.at[col], w4_s, w4_r).start()

    each(COLS - 1, send_w4)
    w4_in[col] = w3_in[...]

    for q in range(2, 4):
        lax.fori_loop(q * 4, q * 4 + 4, pair_step, 0)
        pair_copy(q).start()

    def wait_l(k):
        to_col(k, l_out.at[lax.rem(col + k + 1, COLS)], l_in.at[lax.rem(col + COLS - 1 - k, COLS)], l_s, l_r).wait()

    each(COLS - 1, wait_l)
    total = l_in[0].astype(F32)
    for q in range(1, COLS):
        total += l_in[q].astype(F32)
    gl_ref[...] = total

    def wait_w4(k):
        to_col(k, w3_in, w4_in.at[lax.rem(col + COLS - 1 - k, COLS)], w4_s, w4_r).wait()

    each(COLS - 1, wait_w4)
    gw_ref[...] = w4_in[...].reshape(C * C, CZ)
    each(4, lambda q: pair_copy(q).wait())


def per_device(left_proj, right_proj, out_weight, out_bias, pair_cotangent):
    a = (left_proj * BF16(1.0 / S)).reshape(OWN, S, C).transpose(0, 2, 1).reshape(OWN * C, S)
    b = right_proj.reshape(OWN, S, C).transpose(2, 0, 1).reshape(C * OWN, S)
    w = out_weight.reshape(C, C, CZ).transpose(1, 0, 2).reshape(C * C, CZ)
    vmem = pl.BlockSpec(memory_space=pltpu.VMEM)
    hbm = pl.BlockSpec(memory_space=pl.ANY)
    dma = pltpu.SemaphoreType.DMA
    own = OWN * C
    pair, gl, gr, gw, gb = pl.pallas_call(
        kernel,
        out_shape=(
            jax.ShapeDtypeStruct((TI, TJ, CZ), BF16),
            jax.ShapeDtypeStruct((own, S), F32),
            jax.ShapeDtypeStruct((own, S), F32),
            jax.ShapeDtypeStruct((C * C, CZ), F32),
            jax.ShapeDtypeStruct((8, CZ), F32),
        ),
        in_specs=[vmem, vmem, vmem, vmem, hbm],
        out_specs=(hbm, vmem, vmem, vmem, vmem),
        scratch_shapes=[
            pltpu.VMEM((TI, TJ, CZ), BF16),
            pltpu.VMEM((C, TI * C, TJ), BF16),
            pltpu.VMEM((C, TI * C, TJ), BF16),
            pltpu.VMEM((COLS, own, S), BF16),
            pltpu.VMEM((S, TI * C), BF16),
            pltpu.VMEM((ROWS, own, S), BF16),
            pltpu.VMEM((C * TJ, S), BF16),
            pltpu.VMEM((S, C * TJ), BF16),
            pltpu.VMEM((CZ, C * C), BF16),
            pltpu.VMEM((TI, TJ, CZ), BF16),
            pltpu.VMEM((COLS, own, S), BF16),
            pltpu.VMEM((COLS, own, S), BF16),
            pltpu.VMEM((ROWS, own, S), BF16),
            pltpu.VMEM((ROWS, own, S), BF16),
            pltpu.VMEM((COLS, 136, CZ), F32),
            pltpu.VMEM((COLS, 136, CZ), F32),
            pltpu.VMEM((ROWS, 16, CZ), F32),
            pltpu.VMEM((ROWS, 16, CZ), F32),
            pltpu.VMEM((8, CZ), F32),
            pltpu.VMEM((ROWS, 8, CZ), F32),
            pltpu.VMEM((COLS, ROWS, 8, CZ), F32),
            dma((4,)), dma((4,)),
            dma((COLS - 1,)), dma((COLS - 1,)), dma((ROWS - 1,)), dma((ROWS - 1,)),
            dma((COLS - 1,)), dma((COLS - 1,)), dma((ROWS - 1,)), dma((ROWS - 1,)),
            dma((COLS - 1,)), dma((COLS - 1,)), dma((ROWS - 1,)), dma((ROWS - 1,)),
            dma((ROWS - 1,)), dma((ROWS - 1,)), dma((COLS - 1,)), dma((COLS - 1,)),
        ],
        compiler_params=pltpu.CompilerParams(
            collective_id=0, has_side_effects=True, vmem_limit_bytes=60 << 20
        ),
        name="outer_product_mean",
    )(a, b, w, out_bias.reshape(1, CZ), pair_cotangent)
    grad_left = gl.reshape(OWN, C, S).transpose(0, 2, 1).reshape(OWN, S * C)
    grad_right = gr.reshape(C, OWN, S).transpose(1, 2, 0).reshape(OWN, S * C)
    grad_weight = gw.reshape(C, C, CZ).transpose(1, 0, 2).reshape(C * C, CZ)
    return pair, grad_left, grad_right, grad_weight, jnp.sum(gb, axis=0)


def solution(mesh):
    return jax.shard_map(
        per_device,
        mesh=mesh,
        in_specs=(
            P(("row", "col"), None),
            P(("col", "row"), None),
            P(),
            P(),
            P("row", "col", None),
        ),
        out_specs=(
            P("row", "col", None),
            P(("row", "col"), None),
            P(("col", "row"), None),
            P(),
            P(),
        ),
        check_vma=False,
    )
```

```python
import functools

import jax
import jax.numpy as jnp
from jax import lax
from jax.experimental import pallas as pl
from jax.experimental.pallas import tpu as pltpu
from jax.sharding import PartitionSpec as P

C = 32
CZ = 128
S = 128
ROWS = 16
COLS = 8
TI = 64
TJ = 128
OWN = 8
MESH = pl.DeviceIdType.MESH
NN = (((1,), (0,)), ((), ()))
NT = (((1,), (1,)), ((), ()))
F32 = jnp.float32
BF16 = jnp.bfloat16


def dot(a, b, dims=NN):
    return lax.dot_general(a, b, dims, preferred_element_type=F32)


def kernel(
    a_ref, b_ref, w_ref, bias_ref, cot_hbm,
    pair_hbm, gl_ref, gr_ref, gw_ref, gb_ref,
    cot, d, p, a_all, a_t, b_in, b_all, w_t, pair,
    l_out, l_in, l_x, l_xin, r_keep, r_x, r_xin, r_out, r_in,
    w0, w0_in, w1_out, w1_in, w2_out, w2_in, w3_out, w3_in, w5,
    cot_sem, pair_sem, ax_s, ax_r, az_s, az_r, bc_s, bc_r, bx_s, bx_r, by_s, by_r,
    l_s, l_r, lx_s, lx_r, rx_s, rx_r, r_s, r_r,
    w0_s, w0_r, w1_s, w1_r, w2_s, w2_r, w3_s, w3_r, w4_s, w4_r, w5_s, w5_r,
):
    row = lax.axis_index("row")
    col = lax.axis_index("col")
    half = lax.div(row, 8)
    y = lax.rem(lax.div(row, 2), 4)
    core = lax.rem(row, 2)
    z = lax.div(col, 2)
    far = lax.rem(col, 2)
    mate = half * 8 + y * 2 + (1 - core)
    near = (1 - half) * 8 + y * 2 + core
    other = z * 2 + (1 - far)
    spot = half * 4 + y

    def row_y(n, h=None):
        return (half if h is None else h) * 8 + lax.rem(y + n + 4, 4) * 2 + core

    def col_z(n, f=None):
        return lax.rem(z + n + 4, 4) * 2 + (far if f is None else f)

    def row_spot(n):
        q = lax.rem(spot + n + 8, 8)
        return q, q * 2 + core

    def send(src, dst, ss, rs, k, r=None, c=None):
        return pltpu.make_async_remote_copy(
            src_ref=src, dst_ref=dst, send_sem=ss.at[k], recv_sem=rs.at[k],
            device_id=(row if r is None else r, col if c is None else c), device_id_type=MESH,
        )

    def each(n, f):
        def step(k, carry):
            f(k)
            return carry

        lax.fori_loop(0, n, step, 0)

    def cot_copy(q):
        part = pl.ds(q * 16, 16)
        return pltpu.make_async_copy(cot_hbm.at[part], cot.at[part], cot_sem.at[q])

    def pair_copy(q):
        part = pl.ds(q * 16, 16)
        return pltpu.make_async_copy(pair.at[part], pair_hbm.at[part], pair_sem.at[q])

    each(4, lambda q: cot_copy(q).start())

    barrier = pltpu.get_barrier_semaphore()

    def greet(r, c):
        pl.semaphore_signal(barrier, inc=1, device_id=(r, c), device_id_type=MESH)

    each(COLS - 1, lambda k: greet(row, lax.rem(col + k + 1, COLS)))
    each(7, lambda k: greet(row_spot(k + 1)[1], col))
    greet(mate, col)
    pl.semaphore_wait(barrier, 15)

    bx = send(b_ref, b_in.at[row], bx_s, bx_r, 0, r=near)
    bx.start()
    ax = send(a_ref, a_all.at[col], ax_s, ax_r, 0, c=other)
    ax.start()

    def by_own(k):
        return send(b_ref, b_in.at[row], by_s, by_r, k, r=row_y(k + 1))

    def az_own(k):
        return send(a_ref, a_all.at[col], az_s, az_r, k, c=col_z(k + 1))

    def by_near(k):
        return send(b_in.at[near], b_in.at[near], by_s, by_r, k + 3, r=row_y(k + 1))

    def az_other(k):
        return send(a_all.at[other], a_all.at[other], az_s, az_r, k + 3, c=col_z(k + 1))

    def bc_near():
        return send(b_in.at[near], b_in.at[near], bc_s, bc_r, 1, r=mate)

    def bc_y(k, h, first):
        slot = b_in.at[row_y(-1 - k, h)]
        return send(slot, slot, bc_s, bc_r, first + k, r=mate)

    bc_own = send(b_ref, b_in.at[row], bc_s, bc_r, 0, r=mate)
    each(3, lambda k: by_own(k).start())
    each(3, lambda k: az_own(k).start())
    bc_own.start()
    a_all[col] = a_ref[...]
    b_in[row] = b_ref[...]
    w_t[...] = w_ref[...].T

    def relay_x():
        send(b_ref, b_in.at[near], bx_s, bx_r, 0, r=near).wait_recv()
        each(3, lambda k: by_near(k).start())
        bc_near().start()
        send(a_ref, a_all.at[other], ax_s, ax_r, 0, c=other).wait_recv()
        each(3, lambda k: az_other(k).start())

    def relay_y(h, first, base):
        def step(k):
            slot = b_in.at[row_y(-1 - k, h)]
            send(b_ref, slot, by_s, by_r, base + k, r=row_y(k + 1)).wait_recv()
            bc_y(k, h, first).start()

        each(3, step)

    def end_a():
        def step(k):
            send(a_ref, a_all.at[col_z(-1 - k)], az_s, az_r, k, c=col_z(k + 1)).wait()
            send(a_ref, a_all.at[col_z(-1 - k, 1 - far)], az_s, az_r, k + 3, c=col_z(k + 1)).wait()

        each(3, step)
        ax.wait_send()

    def end_b():
        def from_mate(k, r):
            slot = r - core + (1 - core)
            send(b_ref, b_in.at[slot], bc_s, bc_r, k, r=mate).wait()

        from_mate(0, row)
        from_mate(1, near)
        each(3, lambda k: from_mate(k + 2, row_y(-1 - k)))
        each(3, lambda k: from_mate(k + 5, row_y(-1 - k, 1 - half)))
        bx.wait_send()
        each(6, lambda k: send(b_ref, b_in.at[row], by_s, by_r, k, r=near).wait_send())

    gb_ref[...] = jnp.zeros_like(gb_ref)
    group = 8

    def d_step(g, carry):
        @pl.when(lax.rem(g, 2) == 0)
        def _():
            cot_copy(lax.div(g, 2)).wait()

        block = cot[pl.ds(g * group, group)].reshape(group * TJ, CZ)
        r = dot(w_ref[...], block, NT).astype(BF16)
        for q in range(group):
            d[:, pl.ds((g * group + q) * C, C), :] = r[:, q * TJ:(q + 1) * TJ].reshape(C, C, TJ)
        gb_ref[...] += jnp.sum(block.astype(F32).reshape(group * TJ // 8, 8, CZ), axis=0)
        return carry

    lax.fori_loop(0, 3, d_step, 0)
    relay_x()
    lax.fori_loop(3, 6, d_step, 0)
    relay_y(half, 2, 0)
    lax.fori_loop(6, 8, d_step, 0)
    end_a()
    for q in range(COLS):
        a_t[:, q * 256:(q + 1) * 256] = a_all[q].T
    relay_y(1 - half, 5, 3)

    def rx(g):
        part = pl.ds(g * 64, 64)
        return send(r_x.at[:, part], r_xin.at[:, part], rx_s, rx_r, g, r=mate)

    def gr_step(g, carry):
        x = jnp.concatenate([d[g * 8 + q] for q in range(8)], axis=1)
        r = dot(a_t[...], x)
        t = [r[:, q * TJ:(q + 1) * TJ].T.reshape(8, 16, S) for q in range(8)]
        even = [jnp.where(core == 0, v[:, :8], v[:, 8:]) for v in t]
        odd = [jnp.where(core == 0, v[:, 8:], v[:, :8]) for v in t]
        r_keep[:, pl.ds(g * 64, 64), :] = jnp.concatenate(even, axis=1)
        for h in range(4):
            both = jnp.concatenate(odd[2 * h:2 * h + 2], axis=1)
            r_x[:, pl.ds(g * 64 + h * 16, 16), :] = both.astype(BF16)
        rx(g).start()
        return carry

    lax.fori_loop(0, C // 8, gr_step, 0)

    end_b()

    def lay_b(q, carry):
        part = b_in[:, pl.ds(q * 16, 16), :].astype(F32)
        for h in range(2):
            b_all[pl.ds((q * 2 + h) * TJ, TJ), :] = part[:, h * 8:(h + 1) * 8, :].reshape(TJ, S).astype(BF16)
        return carry

    lax.fori_loop(0, C // 2, lay_b, 0, unroll=4)

    def p_step(n, carry):
        rhs = b_all[pl.ds(n * 2048, 2048), :]
        for m in range(8):
            r = dot(a_all[m], rhs, NT).astype(BF16)
            for q in range(16):
                p[n * 16 + q, m * 256:(m + 1) * 256, :] = r[:, q * TJ:(q + 1) * TJ]
        return carry

    lax.fori_loop(0, 1, p_step, 0)

    def send_r(k):
        q, r = row_spot(k + 1)
        return send(r_out.at[q], r_in.at[spot], r_s, r_r, k, r=r)

    each(4, lambda g: rx(g).wait())

    def sum_x(q):
        r_out[q] = (r_keep[q] + r_xin[q].astype(F32)).astype(BF16)

    each(8, sum_x)
    each(7, lambda k: send_r(k).start())
    r_in[spot] = r_out[spot]

    lax.fori_loop(1, 2, p_step, 0)

    def gw_step(g, carry):
        x = jnp.concatenate(
            [p[pl.ds(g * 16, 16), q * C:(q + 1) * C, :].reshape(16 * C, TJ) for q in range(TI)], axis=1
        )
        w0[g, :512, :] = dot(x, cot[...].reshape(TI * TJ, CZ))
        return carry

    lax.fori_loop(0, 2, gw_step, 0)
    w0[0, 512:, :] = gb_ref[...]
    w0[1, 512:, :] = gb_ref[...]
    w0_copy = send(w0.at[1 - core], w0_in, w0_s, w0_r, 0, r=mate)
    w0_copy.start()

    def gl_step(m, carry):
        x = jnp.concatenate([d[q, pl.ds(m * 1024, 1024), :] for q in range(C)], axis=1)
        r = (dot(x, b_all[...]) * (1.0 / S)).astype(BF16)
        for h in range(4):
            l_out[m * 4 + h] = r[h * 256:(h + 1) * 256, :]
        return carry

    lax.fori_loop(0, 1, gl_step, 0)

    w0_copy.wait()
    for q in range(COLS):
        part = slice(q * 64, q * 64 + 64)
        w1_out[q, :64, :] = w0[core, part, :] + w0_in[part, :]
        w1_out[q, 64:, :] = w0[core, 512:, :] + w0_in[512:, :]

    def send_w1(k, slot):
        to = lax.rem(col + k + 1, COLS)
        return send(w1_out.at[to], w1_in.at[slot], w1_s, w1_r, k, c=to)

    each(COLS - 1, lambda k: send_w1(k, col).start())
    w1_in[col] = w1_out[col]

    lax.fori_loop(1, 2, gl_step, 0)

    def send_l(k):
        to = lax.rem(z + k + 1, 4)
        return send(l_out.at[pl.ds(to * 2, 2)], l_in.at[k], l_s, l_r, k, c=to * 2 + far)

    each(3, lambda k: send_l(k).start())

    each(COLS - 1, lambda k: send_w1(k, lax.rem(col + COLS - 1 - k, COLS)).wait())
    s1 = w1_in[0]
    for q in range(1, COLS):
        s1 += w1_in[q]
    for q in range(8):
        w2_out[q, :8, :] = s1[q * 8:(q + 1) * 8, :]
        w2_out[q, 8:, :] = s1[64:, :]

    def send_w2(k, slot):
        q, r = row_spot(k + 1)
        return send(w2_out.at[q], w2_in.at[slot], w2_s, w2_r, k, r=r)

    each(7, lambda k: send_w2(k, spot).start())
    w2_in[spot] = w2_out[spot]

    def pair_step(g, carry):
        x = jnp.concatenate(
            [p[:, pl.ds((g * 16 + q) * C, C), :].reshape(C * C, TJ) for q in range(16)], axis=1
        )
        r = dot(w_t[...], x)
        for q in range(16):
            pair[g * 16 + q] = (r[:, q * TJ:(q + 1) * TJ].T + bias_ref[...]).astype(BF16)
        pair_copy(g).start()
        return carry

    lax.fori_loop(0, 1, pair_step, 0)

    each(7, lambda k: send_w2(k, row_spot(-1 - k)[0]).wait())
    s2 = w2_in[0]
    for q in range(1, 8):
        s2 += w2_in[q]
    w3_out[...] = s2[:8, :]
    gb_ref[...] = s2[8:, :]

    def send_w3(k, slot):
        return send(w3_out, w3_in.at[slot], w3_s, w3_r, k, r=row_spot(k + 1)[1])

    each(7, lambda k: send_w3(k, spot).start())
    w3_in[spot] = w3_out[...]

    lax.fori_loop(1, 2, pair_step, 0)

    each(3, lambda k: send_l(k).wait())
    mine = l_out[pl.ds(z * 2 + far, 1)][0].astype(F32)
    theirs = l_out[pl.ds(z * 2 + 1 - far, 1)][0].astype(F32)
    for k in range(3):
        mine += l_in[k, far].astype(F32)
        theirs += l_in[k, 1 - far].astype(F32)
    l_x[...] = theirs.astype(BF16)
    lx = send(l_x, l_xin, lx_s, lx_r, 0, c=other)
    lx.start()
    gl_ref[...] = mine

    each(7, lambda k: send_w3(k, row_spot(-1 - k)[0]).wait())

    def send_w4(k, slot):
        return send(w3_in, w5.at[core, slot], w4_s, w4_r, k, c=lax.rem(col + k + 1, COLS))

    each(COLS - 1, lambda k: send_w4(k, col).start())
    w5[core, col] = w3_in[...]

    lax.fori_loop(2, 4, pair_step, 0)

    each(7, lambda k: send(r_out.at[0], r_in.at[row_spot(-1 - k)[0]], r_s, r_r, k, r=near).wait())
    total = r_in[0].astype(F32)
    for q in range(1, 8):
        total += r_in[q].astype(F32)
    gr_ref[...] = total

    each(COLS - 1, lambda k: send_w4(k, lax.rem(col + COLS - 1 - k, COLS)).wait())
    send(w5.at[core], w5.at[core], w5_s, w5_r, 0, r=mate).start()
    lx.wait()
    gl_ref[...] += l_xin[...].astype(F32)
    send(w5.at[core], w5.at[1 - core], w5_s, w5_r, 0, r=mate).wait()
    gw_ref[...] = w5[...].reshape(C * C, CZ)
    each(4, lambda q: pair_copy(q).wait())


def per_device(left_proj, right_proj, out_weight, out_bias, pair_cotangent):
    a = (left_proj * BF16(1.0 / S)).reshape(OWN, S, C).transpose(0, 2, 1).reshape(OWN * C, S)
    b = right_proj.reshape(OWN, S, C).transpose(2, 0, 1).reshape(C * OWN, S)
    w = out_weight.reshape(C, C, CZ).transpose(1, 0, 2).reshape(C * C, CZ)
    vmem = pl.BlockSpec(memory_space=pltpu.VMEM)
    hbm = pl.BlockSpec(memory_space=pl.ANY)
    dma = pltpu.SemaphoreType.DMA
    own = OWN * C
    pair, gl, gr, gw, gb = pl.pallas_call(
        kernel,
        out_shape=(
            jax.ShapeDtypeStruct((TI, TJ, CZ), BF16),
            jax.ShapeDtypeStruct((own, S), F32),
            jax.ShapeDtypeStruct((own, S), F32),
            jax.ShapeDtypeStruct((C * C, CZ), F32),
            jax.ShapeDtypeStruct((8, CZ), F32),
        ),
        in_specs=[vmem, vmem, vmem, vmem, hbm],
        out_specs=(hbm, vmem, vmem, vmem, vmem),
        scratch_shapes=[
            pltpu.VMEM((TI, TJ, CZ), BF16),
            pltpu.VMEM((C, TI * C, TJ), BF16),
            pltpu.VMEM((C, TI * C, TJ), BF16),
            pltpu.VMEM((COLS, own, S), BF16),
            pltpu.VMEM((S, TI * C), BF16),
            pltpu.VMEM((ROWS, own, S), BF16),
            pltpu.VMEM((C * TJ, S), BF16),
            pltpu.VMEM((CZ, C * C), BF16),
            pltpu.VMEM((TI, TJ, CZ), BF16),
            pltpu.VMEM((COLS, own, S), BF16),
            pltpu.VMEM((3, 2, own, S), BF16),
            pltpu.VMEM((own, S), BF16),
            pltpu.VMEM((own, S), BF16),
            pltpu.VMEM((8, own, S), F32),
            pltpu.VMEM((8, own, S), BF16),
            pltpu.VMEM((8, own, S), BF16),
            pltpu.VMEM((8, own, S), BF16),
            pltpu.VMEM((8, own, S), BF16),
            pltpu.VMEM((2, 520, CZ), F32),
            pltpu.VMEM((520, CZ), F32),
            pltpu.VMEM((COLS, 72, CZ), F32),
            pltpu.VMEM((COLS, 72, CZ), F32),
            pltpu.VMEM((8, 16, CZ), F32),
            pltpu.VMEM((8, 16, CZ), F32),
            pltpu.VMEM((8, CZ), F32),
            pltpu.VMEM((8, 8, CZ), F32),
            pltpu.VMEM((2, COLS, 8, 8, CZ), F32),
            dma((4,)), dma((4,)),
            dma((1,)), dma((1,)), dma((6,)), dma((6,)),
            dma((8,)), dma((8,)), dma((1,)), dma((1,)), dma((6,)), dma((6,)),
            dma((3,)), dma((3,)), dma((1,)), dma((1,)),
            dma((4,)), dma((4,)), dma((7,)), dma((7,)),
            dma((1,)), dma((1,)), dma((7,)), dma((7,)), dma((7,)), dma((7,)),
            dma((7,)), dma((7,)), dma((7,)), dma((7,)), dma((1,)), dma((1,)),
        ],
        compiler_params=pltpu.CompilerParams(
            collective_id=0, has_side_effects=True, vmem_limit_bytes=60 << 20
        ),
        name="outer_product_mean",
    )(a, b, w, out_bias.reshape(1, CZ), pair_cotangent)
    grad_left = gl.reshape(OWN, C, S).transpose(0, 2, 1).reshape(OWN, S * C)
    grad_right = gr.reshape(C, OWN, S).transpose(1, 2, 0).reshape(OWN, S * C)
    grad_weight = gw.reshape(C, C, CZ).transpose(1, 0, 2).reshape(C * C, CZ)
    return pair, grad_left, grad_right, grad_weight, jnp.sum(gb, axis=0)


def solution(mesh):
    return jax.shard_map(
        per_device,
        mesh=mesh,
        in_specs=(
            P(("row", "col"), None),
            P(("col", "row"), None),
            P(),
            P(),
            P("row", "col", None),
        ),
        out_specs=(
            P("row", "col", None),
            P(("row", "col"), None),
            P(("col", "row"), None),
            P(),
            P(),
        ),
        check_vma=False,
    )
```

```python
import functools

import jax
import jax.numpy as jnp
from jax import lax
from jax.experimental import pallas as pl
from jax.experimental.pallas import tpu as pltpu
from jax.sharding import PartitionSpec as P

C = 32
CZ = 128
S = 128
ROWS = 16
COLS = 8
TI = 64
TJ = 128
CHIPS = 64
OWN = 8
MESH = pl.DeviceIdType.MESH
NN = (((1,), (0,)), ((), ()))
NT = (((1,), (1,)), ((), ()))
F32 = jnp.float32
BF16 = jnp.bfloat16


def dot(a, b, dims=NN):
    return lax.dot_general(a, b, dims, preferred_element_type=F32)


def swap(parts):
    block = lax.broadcasted_iota(jnp.int32, (C, S), 1) // C
    out = []
    for n in range(4):
        v = None
        for m in range(4):
            r = parts[m] if m == n else pltpu.roll(parts[m], (m - n) * C % S, 1)
            v = r if v is None else jnp.where(block == m, r, v)
        out.append(v)
    return out


def prepare(left_ref, right_ref, weight_ref, a_ref, b_ref, w_ref, stage, flat):
    for n, ref in enumerate((left_ref, right_ref)):
        for q in range(C):
            stage[n, q * OWN:(q + 1) * OWN, :] = ref[:, q * S:(q + 1) * S].astype(F32)
    for n in range(2):
        for g in range(2):
            x = jnp.concatenate([stage[n, pl.ds(g * 4 + i, C, stride=OWN), :] for i in range(4)], axis=0)
            t = x.T
            parts = swap([t[m * C:(m + 1) * C] for m in range(4)])
            for i in range(4):
                if n == 0:
                    a_ref[(g * 4 + i) * C:(g * 4 + i + 1) * C, :] = (parts[i] * (1.0 / S)).astype(BF16)
                else:
                    flat[pl.ds(g * 4 + i, C, stride=OWN), :] = parts[i]
    b_ref[...] = flat[:OWN * C, :].astype(BF16)
    flat[...] = weight_ref[...].astype(F32)
    for c in range(C):
        w_ref[c * C:(c + 1) * C, :] = flat[pl.ds(c, C, stride=C), :].astype(BF16)


def finish(
    gl_ref, gr_ref, gw_ref, gb_ref, pair_in,
    left_ref, right_ref, weight_ref, bias_ref, pair_out, hold, stage, in_sem, out_sem,
):
    def part(ref, q):
        return ref.at[pl.ds(q * 16, 16)]

    load = [pltpu.make_async_copy(part(pair_in, q), part(hold, q), in_sem.at[q]) for q in range(4)]
    save = [pltpu.make_async_copy(part(hold, q), part(pair_out, q), out_sem.at[q]) for q in range(4)]
    for c in load:
        c.start()
    for n, (ref, out) in enumerate(((gl_ref, left_ref), (gr_ref, right_ref))):
        for g in range(2):
            rows = [
                ref[(g * 4 + i) * C:(g * 4 + i + 1) * C, :] if n == 0
                else ref[pl.ds(g * 4 + i, C, stride=OWN), :]
                for i in range(4)
            ]
            stage[n, g * S:(g + 1) * S, :] = jnp.concatenate(swap(rows), axis=0).T
    for q in range(4):
        load[q].wait()
        save[q].start()
    for n, out in enumerate((left_ref, right_ref)):
        for q in range(C):
            out[:, q * S:(q + 1) * S] = stage[n, pl.ds(q, OWN, stride=C), :]
    for c in range(C):
        weight_ref[pl.ds(c, C, stride=C), :] = gw_ref[c * C:(c + 1) * C, :]
    bias_ref[...] = gb_ref[:1, :]
    for c in save:
        c.wait()

def kernel(
    a_ref, b_ref, w_ref, bias_ref, cot_hbm,
    pair_hbm, gl_ref, gr_ref, gw_ref, gb_ref,
    cot, d, p, a_all, a_t, b_in, b_all, w_t, pair,
    l_out, l_in, r_keep, r_x, r_xin, r_out, r_in,
    w0, w0_in, w1_out, w1_in, w2_out, w_all,
    cot_sem, pair_sem, ax_s, ax_r, az_s, az_r, bc_s, bc_r, bx_s, bx_r, by_s, by_r,
    l_s, l_r, rx_s, rx_r, r_s, r_r,
    w0_s, w0_r, w1_s, w1_r, w2_s, w2_r, w3_s, w3_r,
):
    row = lax.axis_index("row")
    col = lax.axis_index("col")
    half = lax.div(row, 8)
    y = lax.rem(lax.div(row, 2), 4)
    core = lax.rem(row, 2)
    z = lax.div(col, 2)
    far = lax.rem(col, 2)
    mate = half * 8 + y * 2 + (1 - core)
    near = (1 - half) * 8 + y * 2 + core
    other = z * 2 + (1 - far)
    spot = half * 4 + y
    chip = spot * COLS + col

    def row_y(n, h=None):
        return (half if h is None else h) * 8 + lax.rem(y + n + 4, 4) * 2 + core

    def col_z(n, f=None):
        return lax.rem(z + n + 4, 4) * 2 + (far if f is None else f)

    def row_spot(n):
        q = lax.rem(spot + n + 8, 8)
        return q, q * 2 + core

    def chip_at(n):
        m = lax.rem(chip + n + CHIPS, CHIPS)
        return m, lax.div(m, COLS) * 2 + core, lax.rem(m, COLS)

    def send(src, dst, ss, rs, k, r=None, c=None):
        return pltpu.make_async_remote_copy(
            src_ref=src, dst_ref=dst, send_sem=ss.at[k], recv_sem=rs.at[k],
            device_id=(row if r is None else r, col if c is None else c), device_id_type=MESH,
        )

    def each(n, f):
        def step(k, carry):
            f(k)
            return carry

        lax.fori_loop(0, n, step, 0)

    def cot_copy(q):
        part = pl.ds(q * 16, 16)
        return pltpu.make_async_copy(cot_hbm.at[part], cot.at[part], cot_sem.at[q])

    def pair_copy(q):
        part = pl.ds(q * 16, 16)
        return pltpu.make_async_copy(pair.at[part], pair_hbm.at[part], pair_sem.at[q])

    each(4, lambda q: cot_copy(q).start())

    barrier = pltpu.get_barrier_semaphore()

    def greet(k):
        _, r, c = chip_at(k + 1)
        pl.semaphore_signal(barrier, inc=1, device_id=(r, c), device_id_type=MESH)

    each(CHIPS - 1, greet)
    pl.semaphore_signal(barrier, inc=1, device_id=(mate, col), device_id_type=MESH)
    pl.semaphore_wait(barrier, CHIPS)

    bx = send(b_ref, b_in.at[row], bx_s, bx_r, 0, r=near)
    bx.start()
    ax = send(a_ref, a_all.at[col], ax_s, ax_r, 0, c=other)
    ax.start()

    def by_own(k):
        return send(b_ref, b_in.at[row], by_s, by_r, k, r=row_y(k + 1))

    def az_own(k):
        return send(a_ref, a_all.at[col], az_s, az_r, k, c=col_z(k + 1))

    def by_near(k):
        return send(b_in.at[near], b_in.at[near], by_s, by_r, k + 3, r=row_y(k + 1))

    def az_other(k):
        return send(a_all.at[other], a_all.at[other], az_s, az_r, k + 3, c=col_z(k + 1))

    def bc_near():
        return send(b_in.at[near], b_in.at[near], bc_s, bc_r, 1, r=mate)

    def bc_y(k, h, first):
        slot = b_in.at[row_y(-1 - k, h)]
        return send(slot, slot, bc_s, bc_r, first + k, r=mate)

    bc_own = send(b_ref, b_in.at[row], bc_s, bc_r, 0, r=mate)
    each(3, lambda k: by_own(k).start())
    each(3, lambda k: az_own(k).start())
    bc_own.start()
    a_all[col] = a_ref[...]
    b_in[row] = b_ref[...]
    w_t[...] = w_ref[...].T

    def relay_x():
        send(b_ref, b_in.at[near], bx_s, bx_r, 0, r=near).wait_recv()
        each(3, lambda k: by_near(k).start())
        bc_near().start()
        send(a_ref, a_all.at[other], ax_s, ax_r, 0, c=other).wait_recv()
        each(3, lambda k: az_other(k).start())

    def relay_y(h, first, base):
        def step(k):
            slot = b_in.at[row_y(-1 - k, h)]
            send(b_ref, slot, by_s, by_r, base + k, r=row_y(k + 1)).wait_recv()
            bc_y(k, h, first).start()

        each(3, step)

    def end_a():
        def step(k):
            send(a_ref, a_all.at[col_z(-1 - k)], az_s, az_r, k, c=col_z(k + 1)).wait()
            send(a_ref, a_all.at[col_z(-1 - k, 1 - far)], az_s, az_r, k + 3, c=col_z(k + 1)).wait()

        each(3, step)
        ax.wait_send()

    def end_b():
        def from_mate(k, r):
            slot = r - core + (1 - core)
            send(b_ref, b_in.at[slot], bc_s, bc_r, k, r=mate).wait()

        from_mate(0, row)
        from_mate(1, near)
        each(3, lambda k: from_mate(k + 2, row_y(-1 - k)))
        each(3, lambda k: from_mate(k + 5, row_y(-1 - k, 1 - half)))
        bx.wait_send()
        each(6, lambda k: send(b_ref, b_in.at[row], by_s, by_r, k, r=near).wait_send())

    gb_ref[...] = jnp.zeros_like(gb_ref)
    group = 16

    def d_step(g, carry):
        cot_copy(g).wait()
        block = cot[pl.ds(g * group, group)].reshape(group * TJ, CZ)
        r = dot(w_ref[...], block, NT).astype(BF16)
        for q in range(group):
            d[:, pl.ds((g * group + q) * C, C), :] = r[:, q * TJ:(q + 1) * TJ].reshape(C, C, TJ)
        gb_ref[...] += jnp.sum(block.astype(F32).reshape(group * TJ // 8, 8, CZ), axis=0)
        return carry

    lax.fori_loop(0, 3, d_step, 0)
    relay_x()
    lax.fori_loop(3, 4, d_step, 0)
    relay_y(half, 2, 0)
    end_a()
    for q in range(COLS):
        a_t[:, q * 256:(q + 1) * 256] = a_all[q].T
    relay_y(1 - half, 5, 3)

    def rx(g):
        part = pl.ds(g * 64, 64)
        return send(r_x.at[:, part], r_xin.at[:, part], rx_s, rx_r, g, r=mate)

    def gr_step(g, carry):
        x = jnp.concatenate([d[g * 8 + q] for q in range(8)], axis=1)
        r = dot(a_t[...], x)
        t = [r[:, q * TJ:(q + 1) * TJ].T.reshape(8, 16, S) for q in range(8)]
        even = [jnp.where(core == 0, v[:, :8], v[:, 8:]) for v in t]
        odd = [jnp.where(core == 0, v[:, 8:], v[:, :8]) for v in t]
        r_keep[:, pl.ds(g * 64, 64), :] = jnp.concatenate(even, axis=1)
        for h in range(4):
            both = jnp.concatenate(odd[2 * h:2 * h + 2], axis=1)
            r_x[:, pl.ds(g * 64 + h * 16, 16), :] = both.astype(BF16)
        rx(g).start()
        return carry

    lax.fori_loop(0, C // 8, gr_step, 0)

    end_b()

    def lay_b(q, carry):
        part = b_in[:, pl.ds(q * 16, 16), :].astype(F32)
        for h in range(2):
            b_all[pl.ds((q * 2 + h) * TJ, TJ), :] = part[:, h * 8:(h + 1) * 8, :].reshape(TJ, S).astype(BF16)
        return carry

    lax.fori_loop(0, C // 2, lay_b, 0, unroll=4)

    def p_step(n, carry):
        rhs = b_all[pl.ds(n * 2048, 2048), :]
        for m in range(8):
            r = dot(a_all[m], rhs, NT).astype(BF16)
            for q in range(16):
                p[n * 16 + q, m * 256:(m + 1) * 256, :] = r[:, q * TJ:(q + 1) * TJ]
        return carry

    lax.fori_loop(0, 1, p_step, 0)

    def send_r(k):
        q, r = row_spot(k + 1)
        return send(r_out.at[q], r_in.at[spot], r_s, r_r, k, r=r)

    each(4, lambda g: rx(g).wait())

    def sum_x(q):
        r_out[q] = (r_keep[q] + r_xin[q].astype(F32)).astype(BF16)

    each(8, sum_x)
    each(7, lambda k: send_r(k).start())
    r_in[spot] = r_out[spot]

    lax.fori_loop(1, 2, p_step, 0)

    def gw_step(g, carry):
        x = jnp.concatenate(
            [p[pl.ds(g * 16, 16), q * C:(q + 1) * C, :].reshape(16 * C, TJ) for q in range(TI)], axis=1
        )
        w0[g, :512, :] = dot(x, cot[...].reshape(TI * TJ, CZ))
        return carry

    lax.fori_loop(0, 2, gw_step, 0)
    w0[0, 512:, :] = gb_ref[...]
    w0[1, 512:, :] = gb_ref[...]
    w0_copy = send(w0.at[1 - core], w0_in, w0_s, w0_r, 0, r=mate)
    w0_copy.start()

    def send_l(k, c, slot):
        return send(l_out.at[c], l_in.at[slot], l_s, l_r, k, c=c)

    def gl_step(m, carry):
        to = lax.rem(z + 1 + m, 4)
        x = jnp.concatenate([d[q, pl.ds(to * 512, 512), :] for q in range(C)], axis=1)
        r = (dot(x, b_all[...]) * (1.0 / S)).astype(BF16)
        for h in range(2):
            l_out[to * 2 + h] = r[h * 256:(h + 1) * 256, :]
        send_l(m * 2, to * 2 + far, col).start()
        send_l(m * 2 + 1, to * 2 + 1 - far, col).start()
        return carry

    lax.fori_loop(0, 1, gl_step, 0)

    w0_copy.wait()
    v = (w0[core, :512, :] + w0_in[:512, :]).reshape(CHIPS, 8, CZ)
    bias = jnp.sum(w0[core, 512:, :] + w0_in[512:, :], axis=0, keepdims=True)
    upper = bias.astype(BF16).astype(F32)
    place = lax.broadcasted_iota(jnp.int32, (8, CZ), 0)
    extra = jnp.where(place == 0, upper, jnp.where(place == 1, bias - upper, 0.0))
    w1_out[...] = jnp.concatenate([v, jnp.broadcast_to(extra, (CHIPS, 8, CZ))], axis=1).astype(BF16)

    def send_w1(k):
        m, r, c = chip_at(k + 1)
        return send(w1_out.at[m], w1_in.at[chip], w1_s, w1_r, k, r=r, c=c)

    each(CHIPS - 1, lambda k: send_w1(k).start())
    w1_in[chip] = w1_out[chip]

    lax.fori_loop(1, 3, gl_step, 0)

    def gl_last():
        x = jnp.concatenate([d[q, pl.ds(z * 512, 512), :] for q in range(C)], axis=1)
        r = (dot(x, b_all[...]) * (1.0 / S)).astype(BF16)
        for h in range(2):
            l_out[z * 2 + h] = r[h * 256:(h + 1) * 256, :]
        send_l(6, z * 2 + 1 - far, col).start()
        l_in[col] = l_out[col]

    gl_last()

    def pair_step(g, carry):
        x = jnp.concatenate(
            [p[:, pl.ds((g * 16 + q) * C, C), :].reshape(C * C, TJ) for q in range(16)], axis=1
        )
        r = dot(w_t[...], x)
        for q in range(16):
            pair[g * 16 + q] = (r[:, q * TJ:(q + 1) * TJ].T + bias_ref[...]).astype(BF16)
        pair_copy(g).start()
        return carry

    lax.fori_loop(0, 1, pair_step, 0)

    def wait_w1(k):
        m, r, c = chip_at(k + 1)
        send(w1_out.at[m], w1_in.at[chip_at(-1 - k)[0]], w1_s, w1_r, k, r=r, c=c).wait()

    each(CHIPS - 1, wait_w1)
    s1 = w1_in[0].astype(F32)
    for q in range(1, CHIPS):
        s1 += w1_in[q].astype(F32)
    w2_out[...] = s1[:8, :]
    gb_ref[...] = jnp.broadcast_to(s1[8:9, :] + s1[9:10, :], (8, CZ))

    def send_w2(k, slot):
        _, r, c = chip_at(k + 1)
        return send(w2_out, w_all.at[core, slot], w2_s, w2_r, k, r=r, c=c)

    each(CHIPS - 1, lambda k: send_w2(k, chip).start())
    w_all[core, chip] = w2_out[...]

    lax.fori_loop(1, 4, pair_step, 0)

    each(7, lambda k: send(r_out.at[0], r_in.at[row_spot(-1 - k)[0]], r_s, r_r, k, r=near).wait())
    total = r_in[0].astype(F32)
    for q in range(1, 8):
        total += r_in[q].astype(F32)
    gr_ref[...] = total

    def wait_l(k):
        to = lax.rem(z + 1 + k, 4) * 2
        of = lax.rem(z + 3 - k, 4) * 2
        send_l(k * 2, to + far, of + far).wait()
        send_l(k * 2 + 1, to + 1 - far, of + 1 - far).wait()

    each(3, wait_l)
    send_l(6, other, other).wait()
    total = l_in[0].astype(F32)
    for q in range(1, COLS):
        total += l_in[q].astype(F32)
    gl_ref[...] = total

    each(CHIPS - 1, lambda k: send_w2(k, chip_at(-1 - k)[0]).wait())
    send(w_all.at[core], w_all.at[core], w3_s, w3_r, 0, r=mate).start()
    gw_ref[pl.ds(core * 512, 512), :] = w_all[core].reshape(512, CZ)
    send(w_all.at[core], w_all.at[1 - core], w3_s, w3_r, 0, r=mate).wait()
    gw_ref[pl.ds((1 - core) * 512, 512), :] = w_all[1 - core].reshape(512, CZ)
    each(4, lambda q: pair_copy(q).wait())


def per_device(left_proj, right_proj, out_weight, out_bias, pair_cotangent):
    vmem = pl.BlockSpec(memory_space=pltpu.VMEM)
    hbm = pl.BlockSpec(memory_space=pl.ANY)
    dma = pltpu.SemaphoreType.DMA
    own = OWN * C
    a, b, w = pl.pallas_call(
        prepare,
        out_shape=(
            jax.ShapeDtypeStruct((own, S), BF16),
            jax.ShapeDtypeStruct((own, S), BF16),
            jax.ShapeDtypeStruct((C * C, CZ), BF16),
        ),
        scratch_shapes=[pltpu.VMEM((2, own, S), F32), pltpu.VMEM((C * C, CZ), F32)],
        name="prepare",
    )(left_proj, right_proj, out_weight)
    pair, gl, gr, gw, gb = pl.pallas_call(
        kernel,
        out_shape=(
            jax.ShapeDtypeStruct((TI, TJ, CZ), BF16),
            jax.ShapeDtypeStruct((own, S), F32),
            jax.ShapeDtypeStruct((own, S), F32),
            jax.ShapeDtypeStruct((C * C, CZ), F32),
            jax.ShapeDtypeStruct((8, CZ), F32),
        ),
        in_specs=[vmem, vmem, vmem, vmem, hbm],
        out_specs=(hbm, vmem, vmem, vmem, vmem),
        scratch_shapes=[
            pltpu.VMEM((TI, TJ, CZ), BF16),
            pltpu.VMEM((C, TI * C, TJ), BF16),
            pltpu.VMEM((C, TI * C, TJ), BF16),
            pltpu.VMEM((COLS, own, S), BF16),
            pltpu.VMEM((S, TI * C), BF16),
            pltpu.VMEM((ROWS, own, S), BF16),
            pltpu.VMEM((C * TJ, S), BF16),
            pltpu.VMEM((CZ, C * C), BF16),
            pltpu.VMEM((TI, TJ, CZ), BF16),
            pltpu.VMEM((COLS, own, S), BF16),
            pltpu.VMEM((COLS, own, S), BF16),
            pltpu.VMEM((8, own, S), F32),
            pltpu.VMEM((8, own, S), BF16),
            pltpu.VMEM((8, own, S), BF16),
            pltpu.VMEM((8, own, S), BF16),
            pltpu.VMEM((8, own, S), BF16),
            pltpu.VMEM((2, 520, CZ), F32),
            pltpu.VMEM((520, CZ), F32),
            pltpu.VMEM((CHIPS, 16, CZ), BF16),
            pltpu.VMEM((CHIPS, 16, CZ), BF16),
            pltpu.VMEM((8, CZ), F32),
            pltpu.VMEM((2, CHIPS, 8, CZ), F32),
            dma((4,)), dma((4,)),
            dma((1,)), dma((1,)), dma((6,)), dma((6,)),
            dma((8,)), dma((8,)), dma((1,)), dma((1,)), dma((6,)), dma((6,)),
            dma((7,)), dma((7,)),
            dma((4,)), dma((4,)), dma((7,)), dma((7,)),
            dma((1,)), dma((1,)), dma((CHIPS - 1,)), dma((CHIPS - 1,)),
            dma((CHIPS - 1,)), dma((CHIPS - 1,)), dma((1,)), dma((1,)),
        ],
        compiler_params=pltpu.CompilerParams(
            collective_id=0, has_side_effects=True, vmem_limit_bytes=60 << 20
        ),
        name="outer_product_mean",
    )(a, b, w, out_bias.reshape(1, CZ), pair_cotangent)
    grad_left, grad_right, grad_weight, grad_bias, pair = pl.pallas_call(
        finish,
        out_shape=(
            jax.ShapeDtypeStruct((OWN, S * C), F32),
            jax.ShapeDtypeStruct((OWN, S * C), F32),
            jax.ShapeDtypeStruct((C * C, CZ), F32),
            jax.ShapeDtypeStruct((1, CZ), F32),
            jax.ShapeDtypeStruct((TI, TJ, CZ), BF16),
        ),
        in_specs=[vmem, vmem, vmem, vmem, hbm],
        out_specs=(vmem, vmem, vmem, vmem, hbm),
        scratch_shapes=[
            pltpu.VMEM((TI, TJ, CZ), BF16), pltpu.VMEM((2, own, S), F32), dma((4,)), dma((4,)),
        ],
        name="finish",
    )(gl, gr, gw, gb, pair)
    return pair, grad_left, grad_right, grad_weight, grad_bias.reshape(CZ)


def solution(mesh):
    return jax.shard_map(
        per_device,
        mesh=mesh,
        in_specs=(
            P(("row", "col"), None),
            P(("col", "row"), None),
            P(),
            P(),
            P("row", "col", None),
        ),
        out_specs=(
            P("row", "col", None),
            P(("row", "col"), None),
            P(("col", "row"), None),
            P(),
            P(),
        ),
        check_vma=False,
    )
```

```python
import functools

import jax
import jax.numpy as jnp
from jax import lax
from jax.experimental import pallas as pl
from jax.experimental.pallas import tpu as pltpu
from jax.sharding import PartitionSpec as P

C = 32
CZ = 128
S = 128
ROWS = 16
COLS = 8
TI = 64
TJ = 128
CHIPS = 64
OWN = 8
MESH = pl.DeviceIdType.MESH
NN = (((1,), (0,)), ((), ()))
NT = (((1,), (1,)), ((), ()))
F32 = jnp.float32
BF16 = jnp.bfloat16


def dot(a, b, dims=NN):
    return lax.dot_general(a, b, dims, preferred_element_type=F32)


def swap(parts):
    block = lax.broadcasted_iota(jnp.int32, (C, S), 1) // C
    out = []
    for n in range(4):
        v = None
        for m in range(4):
            r = parts[m] if m == n else pltpu.roll(parts[m], (m - n) * C % S, 1)
            v = r if v is None else jnp.where(block == m, r, v)
        out.append(v)
    return out


def finish(*refs):
    ins, outs, sem = refs[:5], refs[5:10], refs[10]
    copies = [pltpu.make_async_copy(ins[q], outs[q], sem.at[q]) for q in range(5)]
    for c in copies:
        c.start()
    for c in copies:
        c.wait()


def kernel(
    left_ref, right_ref, weight_ref, bias_ref, cot_hbm,
    pair_hbm, gl_ref, gr_ref, gw_ref, bsum_ref,
    gb_ref, stage, flat, cot, d, p, a_all, a_t, b_in, b_all, w_ref, w_t, pair,
    l_out, l_in, r_keep, r_x, r_xin, r_out, r_in,
    w0, w0_in, w1_out, w1_in, w2_out, w_all,
    cot_sem, pair_sem, ax_s, ax_r, az_s, az_r, bc_s, bc_r, bx_s, bx_r, by_s, by_r,
    l_s, l_r, rx_s, rx_r, r_s, r_r,
    w0_s, w0_r, w1_s, w1_r, w2_s, w2_r, w3_s, w3_r,
):
    row = lax.axis_index("row")
    col = lax.axis_index("col")
    half = lax.div(row, 8)
    y = lax.rem(lax.div(row, 2), 4)
    core = lax.rem(row, 2)
    z = lax.div(col, 2)
    far = lax.rem(col, 2)
    mate = half * 8 + y * 2 + (1 - core)
    near = (1 - half) * 8 + y * 2 + core
    other = z * 2 + (1 - far)
    spot = half * 4 + y
    chip = spot * COLS + col

    def row_y(n, h=None):
        return (half if h is None else h) * 8 + lax.rem(y + n + 4, 4) * 2 + core

    def col_z(n, f=None):
        return lax.rem(z + n + 4, 4) * 2 + (far if f is None else f)

    def row_spot(n):
        q = lax.rem(spot + n + 8, 8)
        return q, q * 2 + core

    def chip_at(n):
        m = lax.rem(chip + n + CHIPS, CHIPS)
        return m, lax.div(m, COLS) * 2 + core, lax.rem(m, COLS)

    def send(src, dst, ss, rs, k, r=None, c=None):
        return pltpu.make_async_remote_copy(
            src_ref=src, dst_ref=dst, send_sem=ss.at[k], recv_sem=rs.at[k],
            device_id=(row if r is None else r, col if c is None else c), device_id_type=MESH,
        )

    def each(n, f):
        def step(k, carry):
            f(k)
            return carry

        lax.fori_loop(0, n, step, 0)

    def cot_copy(q):
        part = pl.ds(q * 16, 16)
        return pltpu.make_async_copy(cot_hbm.at[part], cot.at[part], cot_sem.at[q])

    def pair_copy(q):
        part = pl.ds(q * 16, 16)
        return pltpu.make_async_copy(pair.at[part], pair_hbm.at[part], pair_sem.at[q])

    each(4, lambda q: cot_copy(q).start())

    barrier = pltpu.get_barrier_semaphore()

    def greet(r, c):
        pl.semaphore_signal(barrier, inc=1, device_id=(r, c), device_id_type=MESH)

    each(COLS - 1, lambda k: greet(row, lax.rem(col + k + 1, COLS)))
    each(7, lambda k: greet(row_spot(k + 1)[1], col))
    greet(mate, col)

    for n, ref in enumerate((left_ref, right_ref)):
        for q in range(C):
            stage[n, q * OWN:(q + 1) * OWN, :] = ref[:, q * S:(q + 1) * S].astype(F32)
    for n in range(2):
        for g in range(2):
            x = jnp.concatenate([stage[n, pl.ds(g * 4 + i, C, stride=OWN), :] for i in range(4)], axis=0)
            t = x.T
            parts = swap([t[m * C:(m + 1) * C] for m in range(4)])
            for i in range(4):
                if n == 0:
                    a_all[col, (g * 4 + i) * C:(g * 4 + i + 1) * C, :] = (parts[i] * (1.0 / S)).astype(BF16)
                else:
                    flat[pl.ds(g * 4 + i, C, stride=OWN), :] = parts[i]
    b_in[row] = flat[:OWN * C, :].astype(BF16)
    a_ref = a_all.at[col]
    b_ref = b_in.at[row]
    pl.semaphore_wait(barrier, 15)

    bx = send(b_ref, b_in.at[row], bx_s, bx_r, 0, r=near)
    bx.start()
    ax = send(a_ref, a_all.at[col], ax_s, ax_r, 0, c=other)
    ax.start()

    def by_own(k):
        return send(b_ref, b_in.at[row], by_s, by_r, k, r=row_y(k + 1))

    def az_own(k):
        return send(a_ref, a_all.at[col], az_s, az_r, k, c=col_z(k + 1))

    def by_near(k):
        return send(b_in.at[near], b_in.at[near], by_s, by_r, k + 3, r=row_y(k + 1))

    def az_other(k):
        return send(a_all.at[other], a_all.at[other], az_s, az_r, k + 3, c=col_z(k + 1))

    def bc_near():
        return send(b_in.at[near], b_in.at[near], bc_s, bc_r, 1, r=mate)

    def bc_y(k, h, first):
        slot = b_in.at[row_y(-1 - k, h)]
        return send(slot, slot, bc_s, bc_r, first + k, r=mate)

    bc_own = send(b_ref, b_in.at[row], bc_s, bc_r, 0, r=mate)
    each(3, lambda k: by_own(k).start())
    each(3, lambda k: az_own(k).start())
    bc_own.start()
    flat[...] = weight_ref[...].astype(F32)
    for c in range(C):
        w_ref[c * C:(c + 1) * C, :] = flat[pl.ds(c, C, stride=C), :].astype(BF16)
    w_t[...] = w_ref[...].T

    def relay_x():
        send(b_ref, b_in.at[near], bx_s, bx_r, 0, r=near).wait_recv()
        each(3, lambda k: by_near(k).start())
        bc_near().start()
        send(a_ref, a_all.at[other], ax_s, ax_r, 0, c=other).wait_recv()
        each(3, lambda k: az_other(k).start())

    def relay_y(h, first, base):
        def step(k):
            slot = b_in.at[row_y(-1 - k, h)]
            send(b_ref, slot, by_s, by_r, base + k, r=row_y(k + 1)).wait_recv()
            bc_y(k, h, first).start()

        each(3, step)

    def end_a():
        def step(k):
            send(a_ref, a_all.at[col_z(-1 - k)], az_s, az_r, k, c=col_z(k + 1)).wait()
            send(a_ref, a_all.at[col_z(-1 - k, 1 - far)], az_s, az_r, k + 3, c=col_z(k + 1)).wait()

        each(3, step)
        ax.wait_send()

    def end_b():
        def from_mate(k, r):
            slot = r - core + (1 - core)
            send(b_ref, b_in.at[slot], bc_s, bc_r, k, r=mate).wait()

        from_mate(0, row)
        from_mate(1, near)
        each(3, lambda k: from_mate(k + 2, row_y(-1 - k)))
        each(3, lambda k: from_mate(k + 5, row_y(-1 - k, 1 - half)))
        bx.wait_send()
        each(6, lambda k: send(b_ref, b_in.at[row], by_s, by_r, k, r=near).wait_send())

    gb_ref[...] = jnp.zeros_like(gb_ref)
    group = 16

    def d_step(g, carry):
        cot_copy(g).wait()
        block = cot[pl.ds(g * group, group)].reshape(group * TJ, CZ)
        r = dot(w_ref[...], block, NT).astype(BF16)
        for q in range(group):
            d[:, pl.ds((g * group + q) * C, C), :] = r[:, q * TJ:(q + 1) * TJ].reshape(C, C, TJ)
        gb_ref[...] += jnp.sum(block.astype(F32).reshape(group * TJ // 8, 8, CZ), axis=0)
        return carry

    lax.fori_loop(0, 3, d_step, 0)
    relay_x()
    lax.fori_loop(3, 4, d_step, 0)
    relay_y(half, 2, 0)
    relay_y(1 - half, 5, 3)
    end_a()
    end_b()

    def lay_b(q, carry):
        part = b_in[:, pl.ds(q * 16, 16), :].astype(F32)
        for h in range(2):
            b_all[pl.ds((q * 2 + h) * TJ, TJ), :] = part[:, h * 8:(h + 1) * 8, :].reshape(TJ, S).astype(BF16)
        return carry

    lax.fori_loop(0, C // 2, lay_b, 0, unroll=4)

    def p_step(n, carry):
        rhs = b_all[pl.ds(n * 2048, 2048), :]
        for m in range(8):
            r = dot(a_all[m], rhs, NT).astype(BF16)
            for q in range(16):
                p[n * 16 + q, m * 256:(m + 1) * 256, :] = r[:, q * TJ:(q + 1) * TJ]
        return carry

    lax.fori_loop(0, 2, p_step, 0)

    def gw_step(g, carry):
        x = jnp.concatenate(
            [p[pl.ds(g * 16, 16), q * C:(q + 1) * C, :].reshape(16 * C, TJ) for q in range(TI)], axis=1
        )
        w0[g, :512, :] = dot(x, cot[...].reshape(TI * TJ, CZ))
        return carry

    lax.fori_loop(0, 2, gw_step, 0)
    w0[0, 512:, :] = gb_ref[...]
    w0[1, 512:, :] = gb_ref[...]
    w0_copy = send(w0.at[1 - core], w0_in, w0_s, w0_r, 0, r=mate)
    w0_copy.start()

    for q in range(COLS):
        a_t[:, q * 256:(q + 1) * 256] = a_all[q].T

    def rx(g):
        part = pl.ds(g * 64, 64)
        return send(r_x.at[:, part], r_xin.at[:, part], rx_s, rx_r, g, r=mate)

    def gr_step(g, carry):
        x = jnp.concatenate([d[g * 8 + q] for q in range(8)], axis=1)
        r = dot(a_t[...], x)
        t = [r[:, q * TJ:(q + 1) * TJ].T.reshape(8, 16, S) for q in range(8)]
        even = [jnp.where(core == 0, v[:, :8], v[:, 8:]) for v in t]
        odd = [jnp.where(core == 0, v[:, 8:], v[:, :8]) for v in t]
        r_keep[:, pl.ds(g * 64, 64), :] = jnp.concatenate(even, axis=1)
        for h in range(4):
            both = jnp.concatenate(odd[2 * h:2 * h + 2], axis=1)
            r_x[:, pl.ds(g * 64 + h * 16, 16), :] = both.astype(BF16)
        rx(g).start()
        return carry

    lax.fori_loop(0, 1, gr_step, 0)

    w0_copy.wait()
    v = (w0[core, :512, :] + w0_in[:512, :]).reshape(CHIPS, 8, CZ)
    bias = jnp.sum(w0[core, 512:, :] + w0_in[512:, :], axis=0, keepdims=True)
    upper = bias.astype(BF16).astype(F32)
    place = lax.broadcasted_iota(jnp.int32, (8, CZ), 0)
    extra = jnp.where(place == 0, upper, jnp.where(place == 1, bias - upper, 0.0))
    w1_out[...] = jnp.concatenate([v, jnp.broadcast_to(extra, (CHIPS, 8, CZ))], axis=1).astype(BF16)

    def send_w1(k):
        m, r, c = chip_at(k + 1)
        return send(w1_out.at[m], w1_in.at[chip], w1_s, w1_r, k, r=r, c=c)

    each(CHIPS - 1, lambda k: send_w1(k).start())
    w1_in[chip] = w1_out[chip]

    lax.fori_loop(1, 4, gr_step, 0)

    def send_l(k, c, slot):
        return send(l_out.at[c], l_in.at[slot], l_s, l_r, k, c=c)

    def gl_step(m, carry):
        to = lax.rem(z + 1 + m, 4)
        x = jnp.concatenate([d[q, pl.ds(to * 512, 512), :] for q in range(C)], axis=1)
        r = (dot(x, b_all[...]) * (1.0 / S)).astype(BF16)
        for h in range(2):
            l_out[to * 2 + h] = r[h * 256:(h + 1) * 256, :]
        send_l(m * 2, to * 2 + far, col).start()
        send_l(m * 2 + 1, to * 2 + 1 - far, col).start()
        return carry

    lax.fori_loop(0, 1, gl_step, 0)

    def send_r(k):
        q, r = row_spot(k + 1)
        return send(r_out.at[q], r_in.at[spot], r_s, r_r, k, r=r)

    each(4, lambda g: rx(g).wait())

    def sum_x(q):
        r_out[q] = (r_keep[q] + r_xin[q].astype(F32)).astype(BF16)

    each(8, sum_x)
    each(7, lambda k: send_r(k).start())
    r_in[spot] = r_out[spot]

    lax.fori_loop(1, 3, gl_step, 0)

    def gl_last():
        x = jnp.concatenate([d[q, pl.ds(z * 512, 512), :] for q in range(C)], axis=1)
        r = (dot(x, b_all[...]) * (1.0 / S)).astype(BF16)
        for h in range(2):
            l_out[z * 2 + h] = r[h * 256:(h + 1) * 256, :]
        send_l(6, z * 2 + 1 - far, col).start()
        l_in[col] = l_out[col]

    gl_last()

    def pair_step(g, carry):
        x = jnp.concatenate(
            [p[:, pl.ds((g * 16 + q) * C, C), :].reshape(C * C, TJ) for q in range(16)], axis=1
        )
        r = dot(w_t[...], x)
        for q in range(16):
            pair[g * 16 + q] = (r[:, q * TJ:(q + 1) * TJ].T + bias_ref[...]).astype(BF16)
        pair_copy(g).start()
        return carry

    lax.fori_loop(0, 2, pair_step, 0)

    def wait_w1(k):
        m, r, c = chip_at(k + 1)
        send(w1_out.at[m], w1_in.at[chip_at(-1 - k)[0]], w1_s, w1_r, k, r=r, c=c).wait()

    each(CHIPS - 1, wait_w1)
    s1 = w1_in[0].astype(F32)
    for q in range(1, CHIPS):
        s1 += w1_in[q].astype(F32)
    w2_out[...] = s1[:8, :]
    bsum_ref[...] = s1[8:9, :] + s1[9:10, :]

    def send_w2(k, slot):
        _, r, c = chip_at(k + 1)
        return send(w2_out, w_all.at[core, slot], w2_s, w2_r, k, r=r, c=c)

    each(CHIPS - 1, lambda k: send_w2(k, chip).start())
    w_all[core, chip] = w2_out[...]

    lax.fori_loop(2, 4, pair_step, 0)

    def lay_out(n, rows, out):
        for g in range(2):
            stage[n, g * S:(g + 1) * S, :] = jnp.concatenate(swap(rows[g * 4:g * 4 + 4]), axis=0).T
        for q in range(C):
            out[:, q * S:(q + 1) * S] = stage[n, pl.ds(q, OWN, stride=C), :]

    each(7, lambda k: send(r_out.at[0], r_in.at[row_spot(-1 - k)[0]], r_s, r_r, k, r=near).wait())
    total = r_in[0].astype(F32)
    for q in range(1, 8):
        total += r_in[q].astype(F32)
    flat[:OWN * C, :] = total
    lay_out(1, [flat[pl.ds(i, C, stride=OWN), :] for i in range(OWN)], gr_ref)

    def wait_l(k):
        to = lax.rem(z + 1 + k, 4) * 2
        of = lax.rem(z + 3 - k, 4) * 2
        send_l(k * 2, to + far, of + far).wait()
        send_l(k * 2 + 1, to + 1 - far, of + 1 - far).wait()

    each(3, wait_l)
    send_l(6, other, other).wait()
    total = l_in[0].astype(F32)
    for q in range(1, COLS):
        total += l_in[q].astype(F32)
    lay_out(0, [total[i * C:(i + 1) * C, :] for i in range(OWN)], gl_ref)

    each(CHIPS - 1, lambda k: send_w2(k, chip_at(-1 - k)[0]).wait())
    send(w_all.at[core], w_all.at[core], w3_s, w3_r, 0, r=mate).start()
    send(w_all.at[core], w_all.at[1 - core], w3_s, w3_r, 0, r=mate).wait()
    for c in range(C):
        gw_ref[pl.ds(c, C, stride=C), :] = w_all[c // 16, c % 16 * 4:c % 16 * 4 + 4].reshape(C, CZ)
    each(4, lambda q: pair_copy(q).wait())


def per_device(left_proj, right_proj, out_weight, out_bias, pair_cotangent):
    vmem = pl.BlockSpec(memory_space=pltpu.VMEM)
    hbm = pl.BlockSpec(memory_space=pl.ANY)
    dma = pltpu.SemaphoreType.DMA
    own = OWN * C
    pair, gl, gr, gw, gb = pl.pallas_call(
        kernel,
        out_shape=(
            jax.ShapeDtypeStruct((TI, TJ, CZ), BF16),
            jax.ShapeDtypeStruct((OWN, S * C), F32),
            jax.ShapeDtypeStruct((OWN, S * C), F32),
            jax.ShapeDtypeStruct((C * C, CZ), F32),
            jax.ShapeDtypeStruct((1, CZ), F32),
        ),
        in_specs=[vmem, vmem, vmem, vmem, hbm],
        out_specs=(hbm, vmem, vmem, vmem, vmem),
        scratch_shapes=[
            pltpu.VMEM((8, CZ), F32),
            pltpu.VMEM((2, own, S), F32),
            pltpu.VMEM((C * C, CZ), F32),
            pltpu.VMEM((TI, TJ, CZ), BF16),
            pltpu.VMEM((C, TI * C, TJ), BF16),
            pltpu.VMEM((C, TI * C, TJ), BF16),
            pltpu.VMEM((COLS, own, S), BF16),
            pltpu.VMEM((S, TI * C), BF16),
            pltpu.VMEM((ROWS, own, S), BF16),
            pltpu.VMEM((C * TJ, S), BF16),
            pltpu.VMEM((C * C, CZ), BF16),
            pltpu.VMEM((CZ, C * C), BF16),
            pltpu.VMEM((TI, TJ, CZ), BF16),
            pltpu.VMEM((COLS, own, S), BF16),
            pltpu.VMEM((COLS, own, S), BF16),
            pltpu.VMEM((8, own, S), F32),
            pltpu.VMEM((8, own, S), BF16),
            pltpu.VMEM((8, own, S), BF16),
            pltpu.VMEM((8, own, S), BF16),
            pltpu.VMEM((8, own, S), BF16),
            pltpu.VMEM((2, 520, CZ), F32),
            pltpu.VMEM((520, CZ), F32),
            pltpu.VMEM((CHIPS, 16, CZ), BF16),
            pltpu.VMEM((CHIPS, 16, CZ), BF16),
            pltpu.VMEM((8, CZ), F32),
            pltpu.VMEM((2, CHIPS, 8, CZ), F32),
            dma((4,)), dma((4,)),
            dma((1,)), dma((1,)), dma((6,)), dma((6,)),
            dma((8,)), dma((8,)), dma((1,)), dma((1,)), dma((6,)), dma((6,)),
            dma((7,)), dma((7,)),
            dma((4,)), dma((4,)), dma((7,)), dma((7,)),
            dma((1,)), dma((1,)), dma((CHIPS - 1,)), dma((CHIPS - 1,)),
            dma((CHIPS - 1,)), dma((CHIPS - 1,)), dma((1,)), dma((1,)),
        ],
        compiler_params=pltpu.CompilerParams(
            collective_id=0, has_side_effects=True, vmem_limit_bytes=56 << 20
        ),
        name="outer_product_mean",
    )(left_proj, right_proj, out_weight, out_bias.reshape(1, CZ), pair_cotangent)
    grad_left, grad_right, grad_weight, grad_bias, pair = pl.pallas_call(
        finish,
        out_shape=(
            jax.ShapeDtypeStruct((OWN, S * C), F32),
            jax.ShapeDtypeStruct((OWN, S * C), F32),
            jax.ShapeDtypeStruct((C * C, CZ), F32),
            jax.ShapeDtypeStruct((1, CZ), F32),
            jax.ShapeDtypeStruct((TI, TJ, CZ), BF16),
        ),
        in_specs=[vmem] * 5,
        out_specs=(hbm,) * 5,
        scratch_shapes=[dma((5,))],
        name="finish",
    )(gl, gr, gw, gb, pair)
    return pair, grad_left, grad_right, grad_weight, grad_bias.reshape(CZ)


def solution(mesh):
    return jax.shard_map(
        per_device,
        mesh=mesh,
        in_specs=(
            P(("row", "col"), None),
            P(("col", "row"), None),
            P(),
            P(),
            P("row", "col", None),
        ),
        out_specs=(
            P("row", "col", None),
            P(("row", "col"), None),
            P(("col", "row"), None),
            P(),
            P(),
        ),
        check_vma=False,
    )
```

```python
import functools

import jax
import jax.numpy as jnp
from jax import lax
from jax.experimental import pallas as pl
from jax.experimental.pallas import tpu as pltpu
from jax.sharding import PartitionSpec as P

C = 32
CZ = 128
S = 128
ROWS = 16
COLS = 8
TI = 64
TJ = 128
CHIPS = 64
OWN = 8
MESH = pl.DeviceIdType.MESH
NN = (((1,), (0,)), ((), ()))
NT = (((1,), (1,)), ((), ()))
F32 = jnp.float32
BF16 = jnp.bfloat16


def dot(a, b, dims=NN):
    return lax.dot_general(a, b, dims, preferred_element_type=F32)


def swap(parts):
    block = lax.broadcasted_iota(jnp.int32, (C, S), 1) // C
    out = []
    for n in range(4):
        v = None
        for m in range(4):
            r = parts[m] if m == n else pltpu.roll(parts[m], (m - n) * C % S, 1)
            v = r if v is None else jnp.where(block == m, r, v)
        out.append(v)
    return out


def finish(*refs):
    ins, outs, hold, sem = refs[:5], refs[5:10], refs[10:15], refs[15]
    load, save = [], []
    for q in range(5):
        pieces = 4 if q == 4 else 1
        for k in range(pieces):
            n = ins[q].shape[0] // pieces
            part = pl.ds(k * n, n)
            load.append(pltpu.make_async_copy(ins[q].at[part], hold[q].at[part], sem.at[0, q + k]))
            save.append(pltpu.make_async_copy(hold[q].at[part], outs[q].at[part], sem.at[1, q + k]))
    for c in load:
        c.start()
    for c, e in zip(load, save):
        c.wait()
        e.start()
    for c in save:
        c.wait()


def kernel(
    left_hbm, right_hbm, weight_hbm, bias_ref, cot_hbm,
    pair_hbm, gl_hbm, gr_hbm, gw_hbm, bsum_ref,
    left_ref, right_ref, weight_ref, gl_ref, gr_ref, gw_ref, r_acc, in_sem, out_sem,
    gb_ref, stage, flat, cot, d, p, a_all, a_t, b_in, b_all, w_ref, w_t, pair,
    l_out, l_in, r_keep, r_x, r_xin, r_out, r_in,
    w0, w0_in, w1_out, w1_in, w2_out, w_all,
    cot_sem, pair_sem, ax_s, ax_r, az_s, az_r, bc_s, bc_r, bx_s, bx_r, by_s, by_r,
    l_s, l_r, rx_s, rx_r, r_s, r_r,
    w0_s, w0_r, w1_s, w1_r, w2_s, w2_r, w3_s, w3_r,
):
    row = lax.axis_index("row")
    col = lax.axis_index("col")
    half = lax.div(row, 8)
    y = lax.rem(lax.div(row, 2), 4)
    core = lax.rem(row, 2)
    z = lax.div(col, 2)
    far = lax.rem(col, 2)
    mate = half * 8 + y * 2 + (1 - core)
    near = (1 - half) * 8 + y * 2 + core
    other = z * 2 + (1 - far)
    spot = half * 4 + y
    chip = spot * COLS + col

    def row_y(n, h=None):
        return (half if h is None else h) * 8 + lax.rem(y + n + 4, 4) * 2 + core

    def col_z(n, f=None):
        return lax.rem(z + n + 4, 4) * 2 + (far if f is None else f)

    def row_spot(n):
        q = lax.rem(spot + n + 8, 8)
        return q, q * 2 + core

    def chip_at(n):
        m = lax.rem(chip + n + CHIPS, CHIPS)
        return m, lax.div(m, COLS) * 2 + core, lax.rem(m, COLS)

    def send(src, dst, ss, rs, k, r=None, c=None):
        return pltpu.make_async_remote_copy(
            src_ref=src, dst_ref=dst, send_sem=ss.at[k], recv_sem=rs.at[k],
            device_id=(row if r is None else r, col if c is None else c), device_id_type=MESH,
        )

    def each(n, f):
        def step(k, carry):
            f(k)
            return carry

        lax.fori_loop(0, n, step, 0)

    def cot_copy(q):
        part = pl.ds(q * 16, 16)
        return pltpu.make_async_copy(cot_hbm.at[part], cot.at[part], cot_sem.at[q])

    def pair_copy(q):
        part = pl.ds(q * 16, 16)
        return pltpu.make_async_copy(pair.at[part], pair_hbm.at[part], pair_sem.at[q])

    own_in = [
        pltpu.make_async_copy(src, dst, in_sem.at[q])
        for q, (src, dst) in enumerate(
            ((left_hbm, left_ref), (right_hbm, right_ref), (weight_hbm, weight_ref))
        )
    ]
    for q in range(3):
        own_in[q].start()

    barrier = pltpu.get_barrier_semaphore()

    def greet(r, c):
        pl.semaphore_signal(barrier, inc=1, device_id=(r, c), device_id_type=MESH)

    each(COLS - 1, lambda k: greet(row, lax.rem(col + k + 1, COLS)))
    each(7, lambda k: greet(row_spot(k + 1)[1], col))
    greet(mate, col)

    each(4, lambda q: cot_copy(q).start())
    own_in[0].wait()
    own_in[1].wait()

    for n, ref in enumerate((left_ref, right_ref)):
        for q in range(C):
            stage[n, q * OWN:(q + 1) * OWN, :] = ref[:, q * S:(q + 1) * S].astype(F32)
    for n in range(2):
        for g in range(2):
            x = jnp.concatenate([stage[n, pl.ds(g * 4 + i, C, stride=OWN), :] for i in range(4)], axis=0)
            t = x.T
            parts = swap([t[m * C:(m + 1) * C] for m in range(4)])
            for i in range(4):
                if n == 0:
                    a_all[col, (g * 4 + i) * C:(g * 4 + i + 1) * C, :] = (parts[i] * (1.0 / S)).astype(BF16)
                else:
                    flat[pl.ds(g * 4 + i, C, stride=OWN), :] = parts[i]
    b_in[row] = flat[:OWN * C, :].astype(BF16)
    a_ref = a_all.at[col]
    b_ref = b_in.at[row]
    pl.semaphore_wait(barrier, 15)

    bx = send(b_ref, b_in.at[row], bx_s, bx_r, 0, r=near)
    bx.start()
    ax = send(a_ref, a_all.at[col], ax_s, ax_r, 0, c=other)
    ax.start()

    def by_own(k):
        return send(b_ref, b_in.at[row], by_s, by_r, k, r=row_y(k + 1))

    def az_own(k):
        return send(a_ref, a_all.at[col], az_s, az_r, k, c=col_z(k + 1))

    def by_near(k):
        return send(b_in.at[near], b_in.at[near], by_s, by_r, k + 3, r=row_y(k + 1))

    def az_other(k):
        return send(a_all.at[other], a_all.at[other], az_s, az_r, k + 3, c=col_z(k + 1))

    def bc_near():
        return send(b_in.at[near], b_in.at[near], bc_s, bc_r, 1, r=mate)

    def bc_y(k, h, first):
        slot = b_in.at[row_y(-1 - k, h)]
        return send(slot, slot, bc_s, bc_r, first + k, r=mate)

    bc_own = send(b_ref, b_in.at[row], bc_s, bc_r, 0, r=mate)
    each(3, lambda k: by_own(k).start())
    each(3, lambda k: az_own(k).start())
    bc_own.start()
    own_in[2].wait()
    flat[...] = weight_ref[...].astype(F32)
    for c in range(C):
        w_ref[c * C:(c + 1) * C, :] = flat[pl.ds(c, C, stride=C), :].astype(BF16)
    w_t[...] = w_ref[...].T

    def relay_x():
        send(b_ref, b_in.at[near], bx_s, bx_r, 0, r=near).wait_recv()
        each(3, lambda k: by_near(k).start())
        bc_near().start()
        send(a_ref, a_all.at[other], ax_s, ax_r, 0, c=other).wait_recv()
        each(3, lambda k: az_other(k).start())

    def relay_y(h, first, base):
        def step(k):
            slot = b_in.at[row_y(-1 - k, h)]
            send(b_ref, slot, by_s, by_r, base + k, r=row_y(k + 1)).wait_recv()
            bc_y(k, h, first).start()

        each(3, step)

    def wait_a(near_part):
        def step(k):
            f, n = (far, 0) if near_part else (1 - far, 3)
            send(a_ref, a_all.at[col_z(-1 - k, f)], az_s, az_r, k + n, c=col_z(k + 1)).wait()

        each(3, step)

    def end_b():
        def from_mate(k, r):
            slot = r - core + (1 - core)
            send(b_ref, b_in.at[slot], bc_s, bc_r, k, r=mate).wait()

        from_mate(0, row)
        from_mate(1, near)
        each(3, lambda k: from_mate(k + 2, row_y(-1 - k)))
        each(3, lambda k: from_mate(k + 5, row_y(-1 - k, 1 - half)))
        bx.wait_send()
        each(6, lambda k: send(b_ref, b_in.at[row], by_s, by_r, k, r=near).wait_send())

    gb_ref[...] = jnp.zeros_like(gb_ref)
    group = 16

    def d_step(g, carry):
        cot_copy(g).wait()
        block = cot[pl.ds(g * group, group)].reshape(group * TJ, CZ)
        r = dot(w_ref[...], block, NT).astype(BF16)
        for q in range(group):
            d[:, pl.ds((g * group + q) * C, C), :] = r[:, q * TJ:(q + 1) * TJ].reshape(C, C, TJ)
        gb_ref[...] += jnp.sum(block.astype(F32).reshape(group * TJ // 8, 8, CZ), axis=0)
        return carry

    lax.fori_loop(0, 3, d_step, 0)
    relay_x()
    lax.fori_loop(3, 4, d_step, 0)
    def rx(g):
        part = pl.ds(g * 64, 64)
        return send(r_x.at[:, part], r_xin.at[:, part], rx_s, rx_r, g, r=mate)

    def gr_part(g, f):
        x = jnp.concatenate(
            [
                jnp.concatenate(
                    [d[g * 8 + q, pl.ds((n * 2 + f) * 256, 256), :] for n in range(4)], axis=0
                )
                for q in range(8)
            ],
            axis=1,
        )
        return dot(a_t[...], x)

    def lay_a(f):
        for n in range(4):
            a_t[:, n * 256:(n + 1) * 256] = a_all[n * 2 + f].T

    def gr_first(g, carry):
        r_acc[g] = gr_part(g, far)
        return carry

    def gr_step(g, carry):
        r = r_acc[g] + gr_part(g, 1 - far)
        t = [r[:, q * TJ:(q + 1) * TJ].T.reshape(8, 16, S) for q in range(8)]
        even = [jnp.where(core == 0, v[:, :8], v[:, 8:]) for v in t]
        odd = [jnp.where(core == 0, v[:, 8:], v[:, :8]) for v in t]
        r_keep[:, pl.ds(g * 64, 64), :] = jnp.concatenate(even, axis=1)
        for h in range(4):
            both = jnp.concatenate(odd[2 * h:2 * h + 2], axis=1)
            r_x[:, pl.ds(g * 64 + h * 16, 16), :] = both.astype(BF16)
        rx(g).start()
        return carry

    relay_y(half, 2, 0)
    wait_a(True)
    lay_a(far)
    lax.fori_loop(0, C // 8, gr_first, 0)
    relay_y(1 - half, 5, 3)
    wait_a(False)
    ax.wait_send()
    lay_a(1 - far)
    lax.fori_loop(0, C // 8, gr_step, 0)
    end_b()

    def lay_b(q, carry):
        part = b_in[:, pl.ds(q * 16, 16), :].astype(F32)
        for h in range(2):
            b_all[pl.ds((q * 2 + h) * TJ, TJ), :] = part[:, h * 8:(h + 1) * 8, :].reshape(TJ, S).astype(BF16)
        return carry

    lax.fori_loop(0, C // 2, lay_b, 0, unroll=4)

    def p_step(n, carry):
        rhs = b_all[pl.ds(n * 2048, 2048), :]
        for m in range(8):
            r = dot(a_all[m], rhs, NT).astype(BF16)
            for q in range(16):
                p[n * 16 + q, m * 256:(m + 1) * 256, :] = r[:, q * TJ:(q + 1) * TJ]
        return carry

    lax.fori_loop(0, 1, p_step, 0)

    def send_r(k):
        q, r = row_spot(k + 1)
        return send(r_out.at[q], r_in.at[spot], r_s, r_r, k, r=r)

    each(4, lambda g: rx(g).wait())

    def sum_x(q):
        r_out[q] = (r_keep[q] + r_xin[q].astype(F32)).astype(BF16)

    each(8, sum_x)
    each(7, lambda k: send_r(k).start())
    r_in[spot] = r_out[spot]

    lax.fori_loop(1, 2, p_step, 0)

    def gw_step(g, carry):
        x = jnp.concatenate(
            [p[pl.ds(g * 16, 16), q * C:(q + 1) * C, :].reshape(16 * C, TJ) for q in range(TI)], axis=1
        )
        w0[g, :512, :] = dot(x, cot[...].reshape(TI * TJ, CZ))
        return carry

    lax.fori_loop(0, 2, gw_step, 0)
    w0[0, 512:, :] = gb_ref[...]
    w0[1, 512:, :] = gb_ref[...]
    w0_copy = send(w0.at[1 - core], w0_in, w0_s, w0_r, 0, r=mate)
    w0_copy.start()


    def send_l(k, c, slot):
        return send(l_out.at[c], l_in.at[slot], l_s, l_r, k, c=c)

    def gl_step(m, carry):
        to = lax.rem(z + 1 + m, 4)
        x = jnp.concatenate([d[q, pl.ds(to * 512, 512), :] for q in range(C)], axis=1)
        r = (dot(x, b_all[...]) * (1.0 / S)).astype(BF16)
        for h in range(2):
            l_out[to * 2 + h] = r[h * 256:(h + 1) * 256, :]
        send_l(m * 2, to * 2 + far, col).start()
        send_l(m * 2 + 1, to * 2 + 1 - far, col).start()
        return carry

    lax.fori_loop(0, 1, gl_step, 0)

    w0_copy.wait()
    v = (w0[core, :512, :] + w0_in[:512, :]).reshape(CHIPS, 8, CZ)
    bias = jnp.sum(w0[core, 512:, :] + w0_in[512:, :], axis=0, keepdims=True)
    upper = bias.astype(BF16).astype(F32)
    place = lax.broadcasted_iota(jnp.int32, (8, CZ), 0)
    extra = jnp.where(place == 0, upper, jnp.where(place == 1, bias - upper, 0.0))
    w1_out[...] = jnp.concatenate([v, jnp.broadcast_to(extra, (CHIPS, 8, CZ))], axis=1).astype(BF16)

    def send_w1(k):
        m, r, c = chip_at(k + 1)
        return send(w1_out.at[m], w1_in.at[chip], w1_s, w1_r, k, r=r, c=c)

    each(CHIPS - 1, lambda k: send_w1(k).start())
    w1_in[chip] = w1_out[chip]

    lax.fori_loop(1, 3, gl_step, 0)

    def gl_last():
        x = jnp.concatenate([d[q, pl.ds(z * 512, 512), :] for q in range(C)], axis=1)
        r = (dot(x, b_all[...]) * (1.0 / S)).astype(BF16)
        for h in range(2):
            l_out[z * 2 + h] = r[h * 256:(h + 1) * 256, :]
        send_l(6, z * 2 + 1 - far, col).start()
        l_in[col] = l_out[col]

    gl_last()

    def pair_step(g, carry):
        x = jnp.concatenate(
            [p[:, pl.ds((g * 16 + q) * C, C), :].reshape(C * C, TJ) for q in range(16)], axis=1
        )
        r = dot(w_t[...], x)
        for q in range(16):
            pair[g * 16 + q] = (r[:, q * TJ:(q + 1) * TJ].T + bias_ref[...]).astype(BF16)
        pair_copy(g).start()
        return carry

    lax.fori_loop(0, 2, pair_step, 0)

    def wait_w1(k):
        m, r, c = chip_at(k + 1)
        send(w1_out.at[m], w1_in.at[chip_at(-1 - k)[0]], w1_s, w1_r, k, r=r, c=c).wait()

    each(CHIPS - 1, wait_w1)
    s1 = w1_in[0].astype(F32)
    for q in range(1, CHIPS):
        s1 += w1_in[q].astype(F32)
    w2_out[...] = s1[:8, :]
    bsum_ref[...] = s1[8:9, :] + s1[9:10, :]

    def send_w2(k, slot):
        _, r, c = chip_at(k + 1)
        return send(w2_out, w_all.at[core, slot], w2_s, w2_r, k, r=r, c=c)

    each(CHIPS - 1, lambda k: send_w2(k, chip).start())
    w_all[core, chip] = w2_out[...]

    lax.fori_loop(2, 4, pair_step, 0)

    def lay_out(n, rows, out):
        for g in range(2):
            stage[n, g * S:(g + 1) * S, :] = jnp.concatenate(swap(rows[g * 4:g * 4 + 4]), axis=0).T
        for q in range(C):
            out[:, q * S:(q + 1) * S] = stage[n, pl.ds(q, OWN, stride=C), :]

    each(7, lambda k: send(r_out.at[0], r_in.at[row_spot(-1 - k)[0]], r_s, r_r, k, r=near).wait())
    total = r_in[0].astype(F32)
    for q in range(1, 8):
        total += r_in[q].astype(F32)
    flat[:OWN * C, :] = total
    lay_out(1, [flat[pl.ds(i, C, stride=OWN), :] for i in range(OWN)], gr_ref)
    gr_copy = pltpu.make_async_copy(gr_ref, gr_hbm, out_sem.at[1])
    gr_copy.start()

    def wait_l(k):
        to = lax.rem(z + 1 + k, 4) * 2
        of = lax.rem(z + 3 - k, 4) * 2
        send_l(k * 2, to + far, of + far).wait()
        send_l(k * 2 + 1, to + 1 - far, of + 1 - far).wait()

    each(3, wait_l)
    send_l(6, other, other).wait()
    total = l_in[0].astype(F32)
    for q in range(1, COLS):
        total += l_in[q].astype(F32)
    lay_out(0, [total[i * C:(i + 1) * C, :] for i in range(OWN)], gl_ref)
    gl_copy = pltpu.make_async_copy(gl_ref, gl_hbm, out_sem.at[0])
    gl_copy.start()

    each(CHIPS - 1, lambda k: send_w2(k, chip_at(-1 - k)[0]).wait())
    send(w_all.at[core], w_all.at[core], w3_s, w3_r, 0, r=mate).start()
    send(w_all.at[core], w_all.at[1 - core], w3_s, w3_r, 0, r=mate).wait()
    for c in range(C):
        gw_ref[pl.ds(c, C, stride=C), :] = w_all[c // 16, c % 16 * 4:c % 16 * 4 + 4].reshape(C, CZ)
    gw_copy = pltpu.make_async_copy(gw_ref, gw_hbm, out_sem.at[2])
    gw_copy.start()
    gl_copy.wait()
    gr_copy.wait()
    gw_copy.wait()
    each(4, lambda q: pair_copy(q).wait())


def per_device(left_proj, right_proj, out_weight, out_bias, pair_cotangent):
    vmem = pl.BlockSpec(memory_space=pltpu.VMEM)
    hbm = pl.BlockSpec(memory_space=pl.ANY)
    dma = pltpu.SemaphoreType.DMA
    own = OWN * C
    pair, gl, gr, gw, gb = pl.pallas_call(
        kernel,
        out_shape=(
            jax.ShapeDtypeStruct((TI, TJ, CZ), BF16),
            jax.ShapeDtypeStruct((OWN, S * C), F32),
            jax.ShapeDtypeStruct((OWN, S * C), F32),
            jax.ShapeDtypeStruct((C * C, CZ), F32),
            jax.ShapeDtypeStruct((1, CZ), F32),
        ),
        in_specs=[hbm, hbm, hbm, vmem, hbm],
        out_specs=(hbm, hbm, hbm, hbm, vmem),
        scratch_shapes=[
            pltpu.VMEM((OWN, S * C), BF16),
            pltpu.VMEM((OWN, S * C), BF16),
            pltpu.VMEM((C * C, CZ), BF16),
            pltpu.VMEM((OWN, S * C), F32),
            pltpu.VMEM((OWN, S * C), F32),
            pltpu.VMEM((C * C, CZ), F32),
            pltpu.VMEM((4, S, 8 * TJ), F32),
            dma((3,)),
            dma((3,)),
            pltpu.VMEM((8, CZ), F32),
            pltpu.VMEM((2, own, S), F32),
            pltpu.VMEM((C * C, CZ), F32),
            pltpu.VMEM((TI, TJ, CZ), BF16),
            pltpu.VMEM((C, TI * C, TJ), BF16),
            pltpu.VMEM((C, TI * C, TJ), BF16),
            pltpu.VMEM((COLS, own, S), BF16),
            pltpu.VMEM((S, TI * C // 2), BF16),
            pltpu.VMEM((ROWS, own, S), BF16),
            pltpu.VMEM((C * TJ, S), BF16),
            pltpu.VMEM((C * C, CZ), BF16),
            pltpu.VMEM((CZ, C * C), BF16),
            pltpu.VMEM((TI, TJ, CZ), BF16),
            pltpu.VMEM((COLS, own, S), BF16),
            pltpu.VMEM((COLS, own, S), BF16),
            pltpu.VMEM((8, own, S), F32),
            pltpu.VMEM((8, own, S), BF16),
            pltpu.VMEM((8, own, S), BF16),
            pltpu.VMEM((8, own, S), BF16),
            pltpu.VMEM((8, own, S), BF16),
            pltpu.VMEM((2, 520, CZ), F32),
            pltpu.VMEM((520, CZ), F32),
            pltpu.VMEM((CHIPS, 16, CZ), BF16),
            pltpu.VMEM((CHIPS, 16, CZ), BF16),
            pltpu.VMEM((8, CZ), F32),
            pltpu.VMEM((2, CHIPS, 8, CZ), F32),
            dma((4,)), dma((4,)),
            dma((1,)), dma((1,)), dma((6,)), dma((6,)),
            dma((8,)), dma((8,)), dma((1,)), dma((1,)), dma((6,)), dma((6,)),
            dma((7,)), dma((7,)),
            dma((4,)), dma((4,)), dma((7,)), dma((7,)),
            dma((1,)), dma((1,)), dma((CHIPS - 1,)), dma((CHIPS - 1,)),
            dma((CHIPS - 1,)), dma((CHIPS - 1,)), dma((1,)), dma((1,)),
        ],
        compiler_params=pltpu.CompilerParams(
            collective_id=0, has_side_effects=True, vmem_limit_bytes=56 << 20
        ),
        name="outer_product_mean",
    )(left_proj, right_proj, out_weight, out_bias.reshape(1, CZ), pair_cotangent)
    grad_left, grad_right, grad_weight, grad_bias, pair = pl.pallas_call(
        finish,
        out_shape=(
            jax.ShapeDtypeStruct((OWN, S * C), F32),
            jax.ShapeDtypeStruct((OWN, S * C), F32),
            jax.ShapeDtypeStruct((C * C, CZ), F32),
            jax.ShapeDtypeStruct((1, CZ), F32),
            jax.ShapeDtypeStruct((TI, TJ, CZ), BF16),
        ),
        in_specs=[hbm] * 5,
        out_specs=(hbm,) * 5,
        scratch_shapes=[
            pltpu.VMEM((OWN, S * C), F32),
            pltpu.VMEM((OWN, S * C), F32),
            pltpu.VMEM((C * C, CZ), F32),
            pltpu.VMEM((1, CZ), F32),
            pltpu.VMEM((TI, TJ, CZ), BF16),
            dma((2, 8)),
        ],
        name="finish",
    )(gl, gr, gw, gb, pair)
    return pair, grad_left, grad_right, grad_weight, grad_bias.reshape(CZ)


def solution(mesh):
    return jax.shard_map(
        per_device,
        mesh=mesh,
        in_specs=(
            P(("row", "col"), None),
            P(("col", "row"), None),
            P(),
            P(),
            P("row", "col", None),
        ),
        out_specs=(
            P("row", "col", None),
            P(("row", "col"), None),
            P(("col", "row"), None),
            P(),
            P(),
        ),
        check_vma=False,
    )
```

```python
import functools

import jax
import jax.numpy as jnp
from jax import lax
from jax.experimental import pallas as pl
from jax.experimental.pallas import tpu as pltpu
from jax.sharding import PartitionSpec as P

C = 32
CZ = 128
S = 128
ROWS = 16
COLS = 8
TI = 64
TJ = 128
CHIPS = 64
OWN = 8
MESH = pl.DeviceIdType.MESH
NN = (((1,), (0,)), ((), ()))
NT = (((1,), (1,)), ((), ()))
F32 = jnp.float32
BF16 = jnp.bfloat16


def dot(a, b, dims=NN):
    return lax.dot_general(a, b, dims, preferred_element_type=F32)


def swap(parts):
    block = lax.broadcasted_iota(jnp.int32, (C, S), 1) // C
    out = []
    for n in range(4):
        v = None
        for m in range(4):
            r = parts[m] if m == n else pltpu.roll(parts[m], (m - n) * C % S, 1)
            v = r if v is None else jnp.where(block == m, r, v)
        out.append(v)
    return out


def finish(*refs):
    ins, outs, hold, sem = refs[:5], refs[5:10], refs[10:15], refs[15]
    load, save = [], []
    for q in range(5):
        pieces = 4 if q == 4 else 1
        for k in range(pieces):
            n = ins[q].shape[0] // pieces
            part = pl.ds(k * n, n)
            load.append(pltpu.make_async_copy(ins[q].at[part], hold[q].at[part], sem.at[0, q + k]))
            save.append(pltpu.make_async_copy(hold[q].at[part], outs[q].at[part], sem.at[1, q + k]))
    for c in load:
        c.start()
    for c, e in zip(load, save):
        c.wait()
        e.start()
    for c in save:
        c.wait()


def kernel(
    left_hbm, right_hbm, weight_hbm, bias_ref, cot_hbm,
    pair_hbm, gl_hbm, gr_hbm, gw_hbm, bsum_ref,
    left_ref, right_ref, weight_ref, gl_ref, gr_ref, gw_ref, r_acc, in_sem, out_sem,
    gb_ref, stage, flat, cot, d, p, a_all, a_t, b_in, b_all, w_ref, w_t, pair,
    l_out, l_in, l_x, l_xin, r_keep, r_x, r_xin, r_out, r_in,
    w0, w0_in, w1_out, w1_in, w2_out, w_all,
    cot_sem, pair_sem, ax_s, ax_r, az_s, az_r, bc_s, bc_r, bx_s, bx_r, by_s, by_r,
    l_s, l_r, lx_s, lx_r, rx_s, rx_r, r_s, r_r,
    w0_s, w0_r, w1_s, w1_r, w2_s, w2_r, w3_s, w3_r,
):
    row = lax.axis_index("row")
    col = lax.axis_index("col")
    half = lax.div(row, 8)
    y = lax.rem(lax.div(row, 2), 4)
    core = lax.rem(row, 2)
    z = lax.div(col, 2)
    far = lax.rem(col, 2)
    mate = half * 8 + y * 2 + (1 - core)
    near = (1 - half) * 8 + y * 2 + core
    other = z * 2 + (1 - far)
    spot = half * 4 + y
    chip = spot * COLS + col

    def row_y(n, h=None):
        return (half if h is None else h) * 8 + lax.rem(y + n + 4, 4) * 2 + core

    def col_z(n, f=None):
        return lax.rem(z + n + 4, 4) * 2 + (far if f is None else f)

    def row_spot(n):
        q = lax.rem(spot + n + 8, 8)
        return q, q * 2 + core

    def chip_at(k, sign):
        def step(v):
            return lax.rem(2 + 3 * v - lax.div(v * (v - 1), 2), 4)

        def turn(v, n):
            return lax.rem(v + sign * step(n) + 4, 4)

        x2 = turn(far * 2 + half, lax.div(k, 16))
        y2 = turn(y, lax.rem(lax.div(k, 4), 4))
        z2 = turn(z, lax.rem(k, 4))
        spot2 = lax.rem(x2, 2) * 4 + y2
        col2 = z2 * 2 + lax.div(x2, 2)
        return spot2 * COLS + col2, spot2 * 2 + core, col2

    def send(src, dst, ss, rs, k, r=None, c=None):
        return pltpu.make_async_remote_copy(
            src_ref=src, dst_ref=dst, send_sem=ss.at[k], recv_sem=rs.at[k],
            device_id=(row if r is None else r, col if c is None else c), device_id_type=MESH,
        )

    def each(n, f):
        def step(k, carry):
            f(k)
            return carry

        lax.fori_loop(0, n, step, 0)

    def cot_copy(q):
        part = pl.ds(q * 16, 16)
        return pltpu.make_async_copy(cot_hbm.at[part], cot.at[part], cot_sem.at[q])

    def pair_copy(q):
        part = pl.ds(q * 16, 16)
        return pltpu.make_async_copy(pair.at[part], pair_hbm.at[part], pair_sem.at[q])

    own_in = [
        pltpu.make_async_copy(src, dst, in_sem.at[q])
        for q, (src, dst) in enumerate(
            ((left_hbm, left_ref), (right_hbm, right_ref), (weight_hbm, weight_ref))
        )
    ]
    for q in range(3):
        own_in[q].start()

    barrier = pltpu.get_barrier_semaphore()

    def greet(r, c):
        pl.semaphore_signal(barrier, inc=1, device_id=(r, c), device_id_type=MESH)

    greet(near, col)
    greet(row, other)
    each(3, lambda k: greet(row_y(k + 1), col))
    each(3, lambda k: greet(row, col_z(k + 1)))
    greet(mate, col)

    each(4, lambda q: cot_copy(q).start())
    own_in[0].wait()
    own_in[1].wait()

    for n, ref in enumerate((left_ref, right_ref)):
        for q in range(C):
            stage[n, q * OWN:(q + 1) * OWN, :] = ref[:, q * S:(q + 1) * S].astype(F32)
    for n in range(2):
        for g in range(2):
            x = jnp.concatenate([stage[n, pl.ds(g * 4 + i, C, stride=OWN), :] for i in range(4)], axis=0)
            t = x.T
            parts = swap([t[m * C:(m + 1) * C] for m in range(4)])
            for i in range(4):
                if n == 0:
                    a_all[col, (g * 4 + i) * C:(g * 4 + i + 1) * C, :] = (parts[i] * (1.0 / S)).astype(BF16)
                else:
                    flat[pl.ds(g * 4 + i, C, stride=OWN), :] = parts[i]
    b_in[row] = flat[:OWN * C, :].astype(BF16)
    a_ref = a_all.at[col]
    b_ref = b_in.at[row]
    pl.semaphore_wait(barrier, 9)

    bx = send(b_ref, b_in.at[row], bx_s, bx_r, 0, r=near)
    bx.start()
    ax = send(a_ref, a_all.at[col], ax_s, ax_r, 0, c=other)
    ax.start()

    def by_own(k):
        return send(b_ref, b_in.at[row], by_s, by_r, k, r=row_y(k + 1))

    def az_own(k):
        return send(a_ref, a_all.at[col], az_s, az_r, k, c=col_z(k + 1))

    def by_near(k):
        return send(b_in.at[near], b_in.at[near], by_s, by_r, k + 3, r=row_y(k + 1))

    def az_other(k):
        return send(a_all.at[other], a_all.at[other], az_s, az_r, k + 3, c=col_z(k + 1))

    def bc_near():
        return send(b_in.at[near], b_in.at[near], bc_s, bc_r, 1, r=mate)

    def bc_y(k, h, first):
        slot = b_in.at[row_y(-1 - k, h)]
        return send(slot, slot, bc_s, bc_r, first + k, r=mate)

    bc_own = send(b_ref, b_in.at[row], bc_s, bc_r, 0, r=mate)
    each(3, lambda k: by_own(k).start())
    each(3, lambda k: az_own(k).start())
    bc_own.start()
    own_in[2].wait()
    flat[...] = weight_ref[...].astype(F32)
    for c in range(C):
        w_ref[c * C:(c + 1) * C, :] = flat[pl.ds(c, C, stride=C), :].astype(BF16)
    w_t[...] = w_ref[...].T

    def relay_x():
        send(b_ref, b_in.at[near], bx_s, bx_r, 0, r=near).wait_recv()
        each(3, lambda k: by_near(k).start())
        bc_near().start()
        send(a_ref, a_all.at[other], ax_s, ax_r, 0, c=other).wait_recv()
        each(3, lambda k: az_other(k).start())

    def relay_y(h, first, base):
        def step(k):
            slot = b_in.at[row_y(-1 - k, h)]
            send(b_ref, slot, by_s, by_r, base + k, r=row_y(k + 1)).wait_recv()
            bc_y(k, h, first).start()

        each(3, step)

    def wait_a(near_part):
        def step(k):
            f, n = (far, 0) if near_part else (1 - far, 3)
            send(a_ref, a_all.at[col_z(-1 - k, f)], az_s, az_r, k + n, c=col_z(k + 1)).wait()

        each(3, step)

    def end_b():
        def from_mate(k, r):
            slot = r - core + (1 - core)
            send(b_ref, b_in.at[slot], bc_s, bc_r, k, r=mate).wait()

        from_mate(0, row)
        from_mate(1, near)
        each(3, lambda k: from_mate(k + 2, row_y(-1 - k)))
        each(3, lambda k: from_mate(k + 5, row_y(-1 - k, 1 - half)))
        bx.wait_send()
        each(6, lambda k: send(b_ref, b_in.at[row], by_s, by_r, k, r=near).wait_send())

    gb_ref[...] = jnp.zeros_like(gb_ref)
    group = 16

    def d_step(g, carry):
        cot_copy(g).wait()
        block = cot[pl.ds(g * group, group)].reshape(group * TJ, CZ)
        r = dot(w_ref[...], block, NT).astype(BF16)
        for q in range(group):
            d[:, pl.ds((g * group + q) * C, C), :] = r[:, q * TJ:(q + 1) * TJ].reshape(C, C, TJ)
        gb_ref[...] += jnp.sum(block.astype(F32).reshape(group * TJ // 8, 8, CZ), axis=0)
        return carry

    lax.fori_loop(0, 2, d_step, 0)
    relay_x()
    lax.fori_loop(2, 4, d_step, 0)
    def rx(g):
        part = pl.ds(g * 64, 64)
        return send(r_x.at[:, part], r_xin.at[:, part], rx_s, rx_r, g, r=mate)

    def gr_part(g, f):
        x = jnp.concatenate(
            [
                jnp.concatenate(
                    [d[g * 8 + q, pl.ds((n * 2 + f) * 256, 256), :] for n in range(4)], axis=0
                )
                for q in range(8)
            ],
            axis=1,
        )
        return dot(a_t[...], x)

    def lay_a(f):
        for n in range(4):
            a_t[:, n * 256:(n + 1) * 256] = a_all[n * 2 + f].T

    def gr_first(g, carry):
        r_acc[g] = gr_part(g, far)
        return carry

    def gr_step(g, carry):
        r = r_acc[g] + gr_part(g, 1 - far)
        t = [r[:, q * TJ:(q + 1) * TJ].T.reshape(8, 16, S) for q in range(8)]
        even = [jnp.where(core == 0, v[:, :8], v[:, 8:]) for v in t]
        odd = [jnp.where(core == 0, v[:, 8:], v[:, :8]) for v in t]
        r_keep[:, pl.ds(g * 64, 64), :] = jnp.concatenate(even, axis=1)
        for h in range(4):
            both = jnp.concatenate(odd[2 * h:2 * h + 2], axis=1)
            r_x[:, pl.ds(g * 64 + h * 16, 16), :] = both.astype(BF16)
        rx(g).start()
        return carry

    relay_y(half, 2, 0)
    wait_a(True)
    lay_a(far)
    lax.fori_loop(0, C // 8, gr_first, 0)
    relay_y(1 - half, 5, 3)
    wait_a(False)
    ax.wait_send()
    lay_a(1 - far)
    lax.fori_loop(0, C // 8, gr_step, 0)
    end_b()

    def lay_b(q, carry):
        part = b_in[:, pl.ds(q * 16, 16), :].astype(F32)
        for h in range(2):
            b_all[pl.ds((q * 2 + h) * TJ, TJ), :] = part[:, h * 8:(h + 1) * 8, :].reshape(TJ, S).astype(BF16)
        return carry

    lax.fori_loop(0, C // 2, lay_b, 0, unroll=4)

    def p_step(n, carry):
        rhs = b_all[pl.ds(n * 2048, 2048), :]
        for m in range(8):
            r = dot(a_all[m], rhs, NT).astype(BF16)
            for q in range(16):
                p[n * 16 + q, m * 256:(m + 1) * 256, :] = r[:, q * TJ:(q + 1) * TJ]
        return carry

    lax.fori_loop(0, 1, p_step, 0)

    def send_r(k):
        q, r = row_spot(k + 1)
        return send(r_out.at[q], r_in.at[spot], r_s, r_r, k, r=r)

    each(4, lambda g: rx(g).wait())

    def sum_x(q):
        r_out[q] = (r_keep[q] + r_xin[q].astype(F32)).astype(BF16)

    each(8, sum_x)
    each(7, lambda k: send_r(k).start())
    r_in[spot] = r_out[spot]

    lax.fori_loop(1, 2, p_step, 0)

    def gw_step(g, carry):
        x = jnp.concatenate(
            [p[pl.ds(g * 16, 16), q * C:(q + 1) * C, :].reshape(16 * C, TJ) for q in range(TI)], axis=1
        )
        w0[g, :512, :] = dot(x, cot[...].reshape(TI * TJ, CZ))
        return carry

    lax.fori_loop(0, 2, gw_step, 0)
    w0[0, 512:, :] = gb_ref[...]
    w0[1, 512:, :] = gb_ref[...]
    w0_copy = send(w0.at[1 - core], w0_in, w0_s, w0_r, 0, r=mate)
    w0_copy.start()


    def send_l(m, slot):
        to = lax.rem(z + 1 + m, 4)
        return send(l_out.at[pl.ds(to * 2, 2)], l_in.at[pl.ds(slot * 2, 2)], l_s, l_r, m, c=to * 2 + far)

    def gl_step(m, carry):
        to = lax.rem(z + 1 + m, 4)
        x = jnp.concatenate([d[q, pl.ds(to * 512, 512), :] for q in range(C)], axis=1)
        r = (dot(x, b_all[...]) * (1.0 / S)).astype(BF16)
        for h in range(2):
            l_out[to * 2 + h] = r[h * 256:(h + 1) * 256, :]
        send_l(m, z).start()
        return carry

    lax.fori_loop(0, 1, gl_step, 0)

    w0_copy.wait()
    v = (w0[core, :512, :] + w0_in[:512, :]).reshape(CHIPS, 8, CZ)
    bias = jnp.sum(w0[core, 512:, :] + w0_in[512:, :], axis=0, keepdims=True)
    upper = bias.astype(BF16).astype(F32)
    place = lax.broadcasted_iota(jnp.int32, (8, CZ), 0)
    extra = jnp.where(place == 0, upper, jnp.where(place == 1, bias - upper, 0.0))
    w1_out[...] = jnp.concatenate([v, jnp.broadcast_to(extra, (CHIPS, 8, CZ))], axis=1).astype(BF16)

    def send_w1(k):
        m, r, c = chip_at(k, 1)
        return send(w1_out.at[m], w1_in.at[chip], w1_s, w1_r, k, r=r, c=c)

    each(7, lambda k: send(r_out.at[0], r_in.at[row_spot(-1 - k)[0]], r_s, r_r, k, r=near).wait())
    each(CHIPS - 1, lambda k: send_w1(k).start())
    w1_in[chip] = w1_out[chip]

    lax.fori_loop(1, 3, gl_step, 0)

    def gl_last():
        x = jnp.concatenate([d[q, pl.ds(z * 512, 512), :] for q in range(C)], axis=1)
        r = (dot(x, b_all[...]) * (1.0 / S)).astype(BF16)
        for h in range(2):
            l_out[z * 2 + h] = r[h * 256:(h + 1) * 256, :]
        l_in[pl.ds(z * 2, 2)] = l_out[pl.ds(z * 2, 2)]

    gl_last()

    def pair_step(g, carry):
        x = jnp.concatenate(
            [p[:, pl.ds((g * 16 + q) * C, C), :].reshape(C * C, TJ) for q in range(16)], axis=1
        )
        r = dot(w_t[...], x)
        for q in range(16):
            pair[g * 16 + q] = (r[:, q * TJ:(q + 1) * TJ].T + bias_ref[...]).astype(BF16)
        pair_copy(g).start()
        return carry

    lax.fori_loop(0, 2, pair_step, 0)

    def wait_w1(k):
        m, r, c = chip_at(k, 1)
        send(w1_out.at[m], w1_in.at[chip_at(k, -1)[0]], w1_s, w1_r, k, r=r, c=c).wait()

    each(CHIPS - 1, wait_w1)
    s1 = w1_in[0].astype(F32)
    for q in range(1, CHIPS):
        s1 += w1_in[q].astype(F32)
    w2_out[...] = s1[:8, :]
    bsum_ref[...] = s1[8:9, :] + s1[9:10, :]

    def send_w2(k, slot):
        _, r, c = chip_at(k, 1)
        return send(w2_out, w_all.at[core, slot], w2_s, w2_r, k, r=r, c=c)

    each(CHIPS - 1, lambda k: send_w2(k, chip).start())
    w_all[core, chip] = w2_out[...]

    lax.fori_loop(2, 4, pair_step, 0)

    def lay_out(n, rows, out):
        for g in range(2):
            stage[n, g * S:(g + 1) * S, :] = jnp.concatenate(swap(rows[g * 4:g * 4 + 4]), axis=0).T
        for q in range(C):
            out[:, q * S:(q + 1) * S] = stage[n, pl.ds(q, OWN, stride=C), :]

    total = r_in[0].astype(F32)
    for q in range(1, 8):
        total += r_in[q].astype(F32)
    flat[:OWN * C, :] = total
    lay_out(1, [flat[pl.ds(i, C, stride=OWN), :] for i in range(OWN)], gr_ref)
    gr_copy = pltpu.make_async_copy(gr_ref, gr_hbm, out_sem.at[1])
    gr_copy.start()

    each(3, lambda m: send_l(m, lax.rem(z + 3 - m, 4)).wait())
    theirs = l_in[1 - far].astype(F32)
    for q in range(1, 4):
        theirs += l_in[2 * q + 1 - far].astype(F32)
    l_x[...] = theirs.astype(BF16)
    lx = send(l_x, l_xin, lx_s, lx_r, 0, c=other)
    lx.start()
    total = l_in[far].astype(F32)
    for q in range(1, 4):
        total += l_in[2 * q + far].astype(F32)
    stage[0] = total

    lx.wait()
    total = stage[0] + l_xin[...].astype(F32)
    lay_out(0, [total[i * C:(i + 1) * C, :] for i in range(OWN)], gl_ref)
    gl_copy = pltpu.make_async_copy(gl_ref, gl_hbm, out_sem.at[0])
    gl_copy.start()

    each(CHIPS - 1, lambda k: send_w2(k, chip_at(k, -1)[0]).wait())
    send(w_all.at[core], w_all.at[core], w3_s, w3_r, 0, r=mate).start()
    send(w_all.at[core], w_all.at[1 - core], w3_s, w3_r, 0, r=mate).wait()
    for c in range(C):
        gw_ref[pl.ds(c, C, stride=C), :] = w_all[c // 16, c % 16 * 4:c % 16 * 4 + 4].reshape(C, CZ)
    gw_copy = pltpu.make_async_copy(gw_ref, gw_hbm, out_sem.at[2])
    gw_copy.start()
    gl_copy.wait()
    gr_copy.wait()
    gw_copy.wait()
    each(4, lambda q: pair_copy(q).wait())


def per_device(left_proj, right_proj, out_weight, out_bias, pair_cotangent):
    vmem = pl.BlockSpec(memory_space=pltpu.VMEM)
    hbm = pl.BlockSpec(memory_space=pl.ANY)
    dma = pltpu.SemaphoreType.DMA
    own = OWN * C
    pair, gl, gr, gw, gb = pl.pallas_call(
        kernel,
        out_shape=(
            jax.ShapeDtypeStruct((TI, TJ, CZ), BF16),
            jax.ShapeDtypeStruct((OWN, S * C), F32),
            jax.ShapeDtypeStruct((OWN, S * C), F32),
            jax.ShapeDtypeStruct((C * C, CZ), F32),
            jax.ShapeDtypeStruct((1, CZ), F32),
        ),
        in_specs=[hbm, hbm, hbm, vmem, hbm],
        out_specs=(hbm, hbm, hbm, hbm, vmem),
        scratch_shapes=[
            pltpu.VMEM((OWN, S * C), BF16),
            pltpu.VMEM((OWN, S * C), BF16),
            pltpu.VMEM((C * C, CZ), BF16),
            pltpu.VMEM((OWN, S * C), F32),
            pltpu.VMEM((OWN, S * C), F32),
            pltpu.VMEM((C * C, CZ), F32),
            pltpu.VMEM((4, S, 8 * TJ), F32),
            dma((3,)),
            dma((3,)),
            pltpu.VMEM((8, CZ), F32),
            pltpu.VMEM((2, own, S), F32),
            pltpu.VMEM((C * C, CZ), F32),
            pltpu.VMEM((TI, TJ, CZ), BF16),
            pltpu.VMEM((C, TI * C, TJ), BF16),
            pltpu.VMEM((C, TI * C, TJ), BF16),
            pltpu.VMEM((COLS, own, S), BF16),
            pltpu.VMEM((S, TI * C // 2), BF16),
            pltpu.VMEM((ROWS, own, S), BF16),
            pltpu.VMEM((C * TJ, S), BF16),
            pltpu.VMEM((C * C, CZ), BF16),
            pltpu.VMEM((CZ, C * C), BF16),
            pltpu.VMEM((TI, TJ, CZ), BF16),
            pltpu.VMEM((COLS, own, S), BF16),
            pltpu.VMEM((COLS, own, S), BF16),
            pltpu.VMEM((own, S), BF16),
            pltpu.VMEM((own, S), BF16),
            pltpu.VMEM((8, own, S), F32),
            pltpu.VMEM((8, own, S), BF16),
            pltpu.VMEM((8, own, S), BF16),
            pltpu.VMEM((8, own, S), BF16),
            pltpu.VMEM((8, own, S), BF16),
            pltpu.VMEM((2, 520, CZ), F32),
            pltpu.VMEM((520, CZ), F32),
            pltpu.VMEM((CHIPS, 16, CZ), BF16),
            pltpu.VMEM((CHIPS, 16, CZ), BF16),
            pltpu.VMEM((8, CZ), F32),
            pltpu.VMEM((2, CHIPS, 8, CZ), F32),
            dma((4,)), dma((4,)),
            dma((1,)), dma((1,)), dma((6,)), dma((6,)),
            dma((8,)), dma((8,)), dma((1,)), dma((1,)), dma((6,)), dma((6,)),
            dma((3,)), dma((3,)), dma((1,)), dma((1,)),
            dma((4,)), dma((4,)), dma((7,)), dma((7,)),
            dma((1,)), dma((1,)), dma((CHIPS - 1,)), dma((CHIPS - 1,)),
            dma((CHIPS - 1,)), dma((CHIPS - 1,)), dma((1,)), dma((1,)),
        ],
        compiler_params=pltpu.CompilerParams(
            collective_id=0, has_side_effects=True, vmem_limit_bytes=56 << 20
        ),
        name="outer_product_mean",
    )(left_proj, right_proj, out_weight, out_bias.reshape(1, CZ), pair_cotangent)
    grad_left, grad_right, grad_weight, grad_bias, pair = pl.pallas_call(
        finish,
        out_shape=(
            jax.ShapeDtypeStruct((OWN, S * C), F32),
            jax.ShapeDtypeStruct((OWN, S * C), F32),
            jax.ShapeDtypeStruct((C * C, CZ), F32),
            jax.ShapeDtypeStruct((1, CZ), F32),
            jax.ShapeDtypeStruct((TI, TJ, CZ), BF16),
        ),
        in_specs=[hbm] * 5,
        out_specs=(hbm,) * 5,
        scratch_shapes=[
            pltpu.VMEM((OWN, S * C), F32),
            pltpu.VMEM((OWN, S * C), F32),
            pltpu.VMEM((C * C, CZ), F32),
            pltpu.VMEM((1, CZ), F32),
            pltpu.VMEM((TI, TJ, CZ), BF16),
            dma((2, 8)),
        ],
        name="finish",
    )(gl, gr, gw, gb, pair)
    return pair, grad_left, grad_right, grad_weight, grad_bias.reshape(CZ)


def solution(mesh):
    return jax.shard_map(
        per_device,
        mesh=mesh,
        in_specs=(
            P(("row", "col"), None),
            P(("col", "row"), None),
            P(),
            P(),
            P("row", "col", None),
        ),
        out_specs=(
            P("row", "col", None),
            P(("row", "col"), None),
            P(("col", "row"), None),
            P(),
            P(),
        ),
        check_vma=False,
    )
```

```python
import functools

import jax
import jax.numpy as jnp
from jax import lax
from jax.experimental import pallas as pl
from jax.experimental.pallas import tpu as pltpu
from jax.sharding import PartitionSpec as P

C = 32
CZ = 128
S = 128
ROWS = 16
COLS = 8
TI = 64
TJ = 128
CHIPS = 64
OWN = 8
MESH = pl.DeviceIdType.MESH
NN = (((1,), (0,)), ((), ()))
NT = (((1,), (1,)), ((), ()))
F32 = jnp.float32
BF16 = jnp.bfloat16


STEPS = sorted(
    ((n // 16, n // 4 % 4, n % 4) for n in range(1, CHIPS)),
    key=lambda t: (-sum(min(v, 4 - v) for v in t), t),
)


def dot(a, b, dims=NN):
    return lax.dot_general(a, b, dims, preferred_element_type=F32)


def swap(parts):
    block = lax.broadcasted_iota(jnp.int32, (C, S), 1) // C
    out = []
    for n in range(4):
        v = None
        for m in range(4):
            r = parts[m] if m == n else pltpu.roll(parts[m], (m - n) * C % S, 1)
            v = r if v is None else jnp.where(block == m, r, v)
        out.append(v)
    return out


def finish(*refs):
    ins, outs, hold, sem = refs[:5], refs[5:10], refs[10:15], refs[15]
    load, save = [], []
    for q in range(5):
        pieces = 4 if q == 4 else 1
        for k in range(pieces):
            n = ins[q].shape[0] // pieces
            part = pl.ds(k * n, n)
            load.append(pltpu.make_async_copy(ins[q].at[part], hold[q].at[part], sem.at[0, q + k]))
            save.append(pltpu.make_async_copy(hold[q].at[part], outs[q].at[part], sem.at[1, q + k]))
    for c in load:
        c.start()
    for c, e in zip(load, save):
        c.wait()
        e.start()
    for c in save:
        c.wait()


def kernel(
    left_hbm, right_hbm, weight_hbm, bias_ref, cot_hbm,
    pair_hbm, gl_hbm, gr_hbm, gw_hbm, bsum_ref,
    left_ref, right_ref, weight_ref, gl_ref, gr_ref, gw_ref, r_acc, in_sem, out_sem,
    gb_ref, stage, flat, cot, d, p, a_all, a_t, b_in, b_all, w_ref, w_t, pair,
    l_out, l_in, l_x, l_xin, r_keep, r_x, r_xin, r_out, r_in,
    w0, w0_in, w1_out, w1_in, w2_out, w_all,
    cot_sem, pair_sem, ax_s, ax_r, az_s, az_r, bc_s, bc_r, bx_s, bx_r, by_s, by_r,
    l_s, l_r, lx_s, lx_r, rx_s, rx_r, r_s, r_r,
    w0_s, w0_r, w1_s, w1_r, w2_s, w2_r, w3_s, w3_r,
):
    row = lax.axis_index("row")
    col = lax.axis_index("col")
    half = lax.div(row, 8)
    y = lax.rem(lax.div(row, 2), 4)
    core = lax.rem(row, 2)
    z = lax.div(col, 2)
    far = lax.rem(col, 2)
    mate = half * 8 + y * 2 + (1 - core)
    near = (1 - half) * 8 + y * 2 + core
    other = z * 2 + (1 - far)
    spot = half * 4 + y
    chip = spot * COLS + col

    def row_y(n, h=None):
        return (half if h is None else h) * 8 + lax.rem(y + n + 4, 4) * 2 + core

    def col_z(n, f=None):
        return lax.rem(z + n + 4, 4) * 2 + (far if f is None else f)

    def row_spot(n):
        q = lax.rem(spot + n + 8, 8)
        return q, q * 2 + core

    x = far * 2 + half
    xs, ys, zs = ([lax.rem(v + n, 4) for n in range(4)] for v in (x, y, z))
    row_x = [lax.rem(v, 2) * 8 + core for v in xs]
    col_x = [lax.div(v, 2) for v in xs]

    def chip_at(k):
        dx, dy, dz = STEPS[k]
        r = row_x[dx] + ys[dy] * 2
        c = col_x[dx] + zs[dz] * 2
        return lax.div(r, 2) * COLS + c, r, c

    def send(src, dst, ss, rs, k, r=None, c=None):
        return pltpu.make_async_remote_copy(
            src_ref=src, dst_ref=dst, send_sem=ss.at[k], recv_sem=rs.at[k],
            device_id=(row if r is None else r, col if c is None else c), device_id_type=MESH,
        )

    def each(n, f):
        def step(k, carry):
            f(k)
            return carry

        lax.fori_loop(0, n, step, 0)

    def cot_copy(q):
        part = pl.ds(q * 16, 16)
        return pltpu.make_async_copy(cot_hbm.at[part], cot.at[part], cot_sem.at[q])

    def pair_copy(q):
        part = pl.ds(q * 16, 16)
        return pltpu.make_async_copy(pair.at[part], pair_hbm.at[part], pair_sem.at[q])

    own_in = [
        pltpu.make_async_copy(src, dst, in_sem.at[q])
        for q, (src, dst) in enumerate(
            ((left_hbm, left_ref), (right_hbm, right_ref), (weight_hbm, weight_ref))
        )
    ]
    for q in range(3):
        own_in[q].start()

    barrier = pltpu.get_barrier_semaphore()

    def greet(r, c):
        pl.semaphore_signal(barrier, inc=1, device_id=(r, c), device_id_type=MESH)

    greet(near, col)
    greet(row, other)
    each(3, lambda k: greet(row_y(k + 1), col))
    each(3, lambda k: greet(row, col_z(k + 1)))
    greet(mate, col)

    each(4, lambda q: cot_copy(q).start())
    own_in[0].wait()
    own_in[1].wait()

    for n, ref in enumerate((left_ref, right_ref)):
        for q in range(C):
            stage[n, q * OWN:(q + 1) * OWN, :] = ref[:, q * S:(q + 1) * S].astype(F32)
    for n in range(2):
        for g in range(2):
            x = jnp.concatenate([stage[n, pl.ds(g * 4 + i, C, stride=OWN), :] for i in range(4)], axis=0)
            t = x.T
            parts = swap([t[m * C:(m + 1) * C] for m in range(4)])
            for i in range(4):
                if n == 0:
                    a_all[col, (g * 4 + i) * C:(g * 4 + i + 1) * C, :] = (parts[i] * (1.0 / S)).astype(BF16)
                else:
                    flat[pl.ds(g * 4 + i, C, stride=OWN), :] = parts[i]
    b_in[row] = flat[:OWN * C, :].astype(BF16)
    a_ref = a_all.at[col]
    b_ref = b_in.at[row]
    pl.semaphore_wait(barrier, 9)

    bx = send(b_ref, b_in.at[row], bx_s, bx_r, 0, r=near)
    bx.start()
    ax = send(a_ref, a_all.at[col], ax_s, ax_r, 0, c=other)
    ax.start()

    def by_own(k):
        return send(b_ref, b_in.at[row], by_s, by_r, k, r=row_y(k + 1))

    def az_own(k):
        return send(a_ref, a_all.at[col], az_s, az_r, k, c=col_z(k + 1))

    def by_near(k):
        return send(b_in.at[near], b_in.at[near], by_s, by_r, k + 3, r=row_y(k + 1))

    def az_other(k):
        return send(a_all.at[other], a_all.at[other], az_s, az_r, k + 3, c=col_z(k + 1))

    def bc_near():
        return send(b_in.at[near], b_in.at[near], bc_s, bc_r, 1, r=mate)

    def bc_y(k, h, first):
        slot = b_in.at[row_y(-1 - k, h)]
        return send(slot, slot, bc_s, bc_r, first + k, r=mate)

    bc_own = send(b_ref, b_in.at[row], bc_s, bc_r, 0, r=mate)
    each(3, lambda k: by_own(k).start())
    each(3, lambda k: az_own(k).start())
    bc_own.start()
    own_in[2].wait()
    flat[...] = weight_ref[...].astype(F32)
    for c in range(C):
        w_ref[c * C:(c + 1) * C, :] = flat[pl.ds(c, C, stride=C), :].astype(BF16)
    w_t[...] = w_ref[...].T

    def relay_x():
        send(b_ref, b_in.at[near], bx_s, bx_r, 0, r=near).wait_recv()
        each(3, lambda k: by_near(k).start())
        bc_near().start()
        send(a_ref, a_all.at[other], ax_s, ax_r, 0, c=other).wait_recv()
        each(3, lambda k: az_other(k).start())

    def relay_y(h, first, base):
        def step(k):
            slot = b_in.at[row_y(-1 - k, h)]
            send(b_ref, slot, by_s, by_r, base + k, r=row_y(k + 1)).wait_recv()
            bc_y(k, h, first).start()

        each(3, step)

    def wait_a(near_part):
        def step(k):
            f, n = (far, 0) if near_part else (1 - far, 3)
            send(a_ref, a_all.at[col_z(-1 - k, f)], az_s, az_r, k + n, c=col_z(k + 1)).wait()

        each(3, step)

    def end_b():
        def from_mate(k, r):
            slot = r - core + (1 - core)
            send(b_ref, b_in.at[slot], bc_s, bc_r, k, r=mate).wait()

        from_mate(0, row)
        from_mate(1, near)
        each(3, lambda k: from_mate(k + 2, row_y(-1 - k)))
        each(3, lambda k: from_mate(k + 5, row_y(-1 - k, 1 - half)))
        bx.wait_send()
        each(6, lambda k: send(b_ref, b_in.at[row], by_s, by_r, k, r=near).wait_send())

    gb_ref[...] = jnp.zeros_like(gb_ref)
    group = 16

    def d_step(g, carry):
        cot_copy(g).wait()
        block = cot[pl.ds(g * group, group)].reshape(group * TJ, CZ)
        r = dot(w_ref[...], block, NT).astype(BF16)
        for q in range(group):
            d[:, pl.ds((g * group + q) * C, C), :] = r[:, q * TJ:(q + 1) * TJ].reshape(C, C, TJ)
        gb_ref[...] += jnp.sum(block.astype(F32).reshape(group * TJ // 8, 8, CZ), axis=0)
        return carry

    lax.fori_loop(0, 2, d_step, 0)
    relay_x()
    lax.fori_loop(2, 4, d_step, 0)
    def rx(g):
        part = pl.ds(g * 64, 64)
        return send(r_x.at[:, part], r_xin.at[:, part], rx_s, rx_r, g, r=mate)

    def gr_part(g, f):
        x = jnp.concatenate(
            [
                jnp.concatenate(
                    [d[g * 8 + q, pl.ds((n * 2 + f) * 256, 256), :] for n in range(4)], axis=0
                )
                for q in range(8)
            ],
            axis=1,
        )
        return dot(a_t[...], x)

    def lay_a(f):
        for n in range(4):
            a_t[:, n * 256:(n + 1) * 256] = a_all[n * 2 + f].T

    def gr_first(g, carry):
        r_acc[g] = gr_part(g, far)
        return carry

    def gr_step(g, carry):
        r = r_acc[g] + gr_part(g, 1 - far)
        t = [r[:, q * TJ:(q + 1) * TJ].T.reshape(8, 16, S) for q in range(8)]
        even = [jnp.where(core == 0, v[:, :8], v[:, 8:]) for v in t]
        odd = [jnp.where(core == 0, v[:, 8:], v[:, :8]) for v in t]
        r_keep[:, pl.ds(g * 64, 64), :] = jnp.concatenate(even, axis=1)
        for h in range(4):
            both = jnp.concatenate(odd[2 * h:2 * h + 2], axis=1)
            r_x[:, pl.ds(g * 64 + h * 16, 16), :] = both.astype(BF16)
        rx(g).start()
        return carry

    relay_y(half, 2, 0)
    wait_a(True)
    lay_a(far)
    lax.fori_loop(0, C // 8, gr_first, 0)
    relay_y(1 - half, 5, 3)
    wait_a(False)
    ax.wait_send()
    lay_a(1 - far)
    lax.fori_loop(0, C // 8, gr_step, 0)
    end_b()

    def lay_b(q, carry):
        part = b_in[:, pl.ds(q * 16, 16), :].astype(F32)
        for h in range(2):
            b_all[pl.ds((q * 2 + h) * TJ, TJ), :] = part[:, h * 8:(h + 1) * 8, :].reshape(TJ, S).astype(BF16)
        return carry

    lax.fori_loop(0, C // 2, lay_b, 0, unroll=4)

    def p_step(n, carry):
        rhs = b_all[pl.ds(n * 1024, 1024), :]
        for m in range(8):
            r = dot(a_all[m], rhs, NT).astype(BF16)
            for q in range(8):
                p[n * 8 + q, m * 256:(m + 1) * 256, :] = r[:, q * TJ:(q + 1) * TJ]
        return carry

    lax.fori_loop(0, 1, p_step, 0)

    def send_r(k):
        q, r = row_spot(k + 1)
        return send(r_out.at[q], r_in.at[spot], r_s, r_r, k, r=r)

    each(4, lambda g: rx(g).wait())

    def sum_x(q):
        r_out[q] = (r_keep[q] + r_xin[q].astype(F32)).astype(BF16)

    each(8, sum_x)
    each(7, lambda k: send_r(k).start())
    r_in[spot] = r_out[spot]

    lax.fori_loop(1, 4, p_step, 0)

    w0[0, 512:, :] = gb_ref[...]
    w0[1, 512:, :] = gb_ref[...]
    w0_copy = send(w0.at[1 - core], w0_in, w0_s, w0_r, 0, r=mate)

    def gw_step(n, carry):
        g = lax.rem(n + 1 + core, 2)
        x = jnp.concatenate(
            [p[pl.ds(g * 16, 16), q * C:(q + 1) * C, :].reshape(16 * C, TJ) for q in range(TI)], axis=1
        )
        w0[g, :512, :] = dot(x, cot[...].reshape(TI * TJ, CZ))
        return carry

    lax.fori_loop(0, 1, gw_step, 0)
    w0_copy.start()
    lax.fori_loop(1, 2, gw_step, 0)


    def send_l(m, slot):
        to = lax.rem(z + 1 + m, 4)
        return send(l_out.at[pl.ds(to * 2, 2)], l_in.at[pl.ds(slot * 2, 2)], l_s, l_r, m, c=to * 2 + far)

    def gl_step(m, carry):
        to = lax.rem(z + 1 + m, 4)
        x = jnp.concatenate([d[q, pl.ds(to * 512, 512), :] for q in range(C)], axis=1)
        r = (dot(x, b_all[...]) * (1.0 / S)).astype(BF16)
        for h in range(2):
            l_out[to * 2 + h] = r[h * 256:(h + 1) * 256, :]
        send_l(m, z).start()
        return carry

    w0_copy.wait()
    v = (w0[core, :512, :] + w0_in[:512, :]).reshape(CHIPS, 8, CZ)
    bias = jnp.sum(w0[core, 512:, :] + w0_in[512:, :], axis=0, keepdims=True)
    upper = bias.astype(BF16).astype(F32)
    place = lax.broadcasted_iota(jnp.int32, (8, CZ), 0)
    extra = jnp.where(place == 0, upper, jnp.where(place == 1, bias - upper, 0.0))
    w1_out[...] = jnp.concatenate([v, jnp.broadcast_to(extra, (CHIPS, 8, CZ))], axis=1).astype(BF16)

    def send_w1(k):
        m, r, c = chip_at(k)
        return send(w1_out.at[m], w1_in.at[chip], w1_s, w1_r, k, r=r, c=c)

    each(7, lambda k: send(r_out.at[0], r_in.at[row_spot(-1 - k)[0]], r_s, r_r, k, r=near).wait())
    for k in range(CHIPS - 1):
        send_w1(k).start()
    w1_in[chip] = w1_out[chip]

    lax.fori_loop(0, 3, gl_step, 0)

    def gl_last():
        x = jnp.concatenate([d[q, pl.ds(z * 512, 512), :] for q in range(C)], axis=1)
        r = (dot(x, b_all[...]) * (1.0 / S)).astype(BF16)
        for h in range(2):
            l_out[z * 2 + h] = r[h * 256:(h + 1) * 256, :]
        l_in[pl.ds(z * 2, 2)] = l_out[pl.ds(z * 2, 2)]

    gl_last()

    def pair_step(g, carry):
        x = jnp.concatenate(
            [p[:, pl.ds((g * 16 + q) * C, C), :].reshape(C * C, TJ) for q in range(16)], axis=1
        )
        r = dot(w_t[...], x)
        for q in range(16):
            pair[g * 16 + q] = (r[:, q * TJ:(q + 1) * TJ].T + bias_ref[...]).astype(BF16)
        pair_copy(g).start()
        return carry

    lax.fori_loop(0, 2, pair_step, 0)

    def wait_w1(k):
        send(w1_out.at[k], w1_in.at[k], w1_s, w1_r, k, r=near).wait()

    each(CHIPS - 1, wait_w1)
    s1 = w1_in[0].astype(F32)
    for q in range(1, CHIPS):
        s1 += w1_in[q].astype(F32)
    w2_out[...] = s1[:8, :]
    bsum_ref[...] = s1[8:9, :] + s1[9:10, :]

    def send_w2(k):
        _, r, c = chip_at(k)
        return send(w2_out, w_all.at[core, chip], w2_s, w2_r, k, r=r, c=c)

    for k in range(CHIPS - 1):
        send_w2(k).start()
    w_all[core, chip] = w2_out[...]

    lax.fori_loop(2, 4, pair_step, 0)

    def lay_out(n, rows, out):
        for g in range(2):
            stage[n, g * S:(g + 1) * S, :] = jnp.concatenate(swap(rows[g * 4:g * 4 + 4]), axis=0).T
        for q in range(C):
            out[:, q * S:(q + 1) * S] = stage[n, pl.ds(q, OWN, stride=C), :]

    total = r_in[0].astype(F32)
    for q in range(1, 8):
        total += r_in[q].astype(F32)
    flat[:OWN * C, :] = total
    lay_out(1, [flat[pl.ds(i, C, stride=OWN), :] for i in range(OWN)], gr_ref)
    gr_copy = pltpu.make_async_copy(gr_ref, gr_hbm, out_sem.at[1])
    gr_copy.start()

    each(3, lambda m: send_l(m, lax.rem(z + 3 - m, 4)).wait())
    theirs = l_in[1 - far].astype(F32)
    for q in range(1, 4):
        theirs += l_in[2 * q + 1 - far].astype(F32)
    l_x[...] = theirs.astype(BF16)
    lx = send(l_x, l_xin, lx_s, lx_r, 0, c=other)
    lx.start()
    total = l_in[far].astype(F32)
    for q in range(1, 4):
        total += l_in[2 * q + far].astype(F32)
    stage[0] = total

    lx.wait()
    total = stage[0] + l_xin[...].astype(F32)
    lay_out(0, [total[i * C:(i + 1) * C, :] for i in range(OWN)], gl_ref)
    gl_copy = pltpu.make_async_copy(gl_ref, gl_hbm, out_sem.at[0])
    gl_copy.start()

    each(CHIPS - 1, lambda k: send(w2_out, w_all.at[core, k], w2_s, w2_r, k, r=near).wait())
    send(w_all.at[core], w_all.at[core], w3_s, w3_r, 0, r=mate).start()
    send(w_all.at[core], w_all.at[1 - core], w3_s, w3_r, 0, r=mate).wait()
    for c in range(C):
        gw_ref[pl.ds(c, C, stride=C), :] = w_all[c // 16, c % 16 * 4:c % 16 * 4 + 4].reshape(C, CZ)
    gw_copy = pltpu.make_async_copy(gw_ref, gw_hbm, out_sem.at[2])
    gw_copy.start()
    gl_copy.wait()
    gr_copy.wait()
    gw_copy.wait()
    each(4, lambda q: pair_copy(q).wait())


def per_device(left_proj, right_proj, out_weight, out_bias, pair_cotangent):
    vmem = pl.BlockSpec(memory_space=pltpu.VMEM)
    hbm = pl.BlockSpec(memory_space=pl.ANY)
    dma = pltpu.SemaphoreType.DMA
    own = OWN * C
    pair, gl, gr, gw, gb = pl.pallas_call(
        kernel,
        out_shape=(
            jax.ShapeDtypeStruct((TI, TJ, CZ), BF16),
            jax.ShapeDtypeStruct((OWN, S * C), F32),
            jax.ShapeDtypeStruct((OWN, S * C), F32),
            jax.ShapeDtypeStruct((C * C, CZ), F32),
            jax.ShapeDtypeStruct((1, CZ), F32),
        ),
        in_specs=[hbm, hbm, hbm, vmem, hbm],
        out_specs=(hbm, hbm, hbm, hbm, vmem),
        scratch_shapes=[
            pltpu.VMEM((OWN, S * C), BF16),
            pltpu.VMEM((OWN, S * C), BF16),
            pltpu.VMEM((C * C, CZ), BF16),
            pltpu.VMEM((OWN, S * C), F32),
            pltpu.VMEM((OWN, S * C), F32),
            pltpu.VMEM((C * C, CZ), F32),
            pltpu.VMEM((4, S, 8 * TJ), F32),
            dma((3,)),
            dma((3,)),
            pltpu.VMEM((8, CZ), F32),
            pltpu.VMEM((2, own, S), F32),
            pltpu.VMEM((C * C, CZ), F32),
            pltpu.VMEM((TI, TJ, CZ), BF16),
            pltpu.VMEM((C, TI * C, TJ), BF16),
            pltpu.VMEM((C, TI * C, TJ), BF16),
            pltpu.VMEM((COLS, own, S), BF16),
            pltpu.VMEM((S, TI * C // 2), BF16),
            pltpu.VMEM((ROWS, own, S), BF16),
            pltpu.VMEM((C * TJ, S), BF16),
            pltpu.VMEM((C * C, CZ), BF16),
            pltpu.VMEM((CZ, C * C), BF16),
            pltpu.VMEM((TI, TJ, CZ), BF16),
            pltpu.VMEM((COLS, own, S), BF16),
            pltpu.VMEM((COLS, own, S), BF16),
            pltpu.VMEM((own, S), BF16),
            pltpu.VMEM((own, S), BF16),
            pltpu.VMEM((8, own, S), F32),
            pltpu.VMEM((8, own, S), BF16),
            pltpu.VMEM((8, own, S), BF16),
            pltpu.VMEM((8, own, S), BF16),
            pltpu.VMEM((8, own, S), BF16),
            pltpu.VMEM((2, 520, CZ), F32),
            pltpu.VMEM((520, CZ), F32),
            pltpu.VMEM((CHIPS, 16, CZ), BF16),
            pltpu.VMEM((CHIPS, 16, CZ), BF16),
            pltpu.VMEM((8, CZ), F32),
            pltpu.VMEM((2, CHIPS, 8, CZ), F32),
            dma((4,)), dma((4,)),
            dma((1,)), dma((1,)), dma((6,)), dma((6,)),
            dma((8,)), dma((8,)), dma((1,)), dma((1,)), dma((6,)), dma((6,)),
            dma((3,)), dma((3,)), dma((1,)), dma((1,)),
            dma((4,)), dma((4,)), dma((7,)), dma((7,)),
            dma((1,)), dma((1,)), dma((CHIPS - 1,)), dma((CHIPS - 1,)),
            dma((CHIPS - 1,)), dma((CHIPS - 1,)), dma((1,)), dma((1,)),
        ],
        compiler_params=pltpu.CompilerParams(
            collective_id=0, has_side_effects=True, vmem_limit_bytes=56 << 20
        ),
        name="outer_product_mean",
    )(left_proj, right_proj, out_weight, out_bias.reshape(1, CZ), pair_cotangent)
    grad_left, grad_right, grad_weight, grad_bias, pair = pl.pallas_call(
        finish,
        out_shape=(
            jax.ShapeDtypeStruct((OWN, S * C), F32),
            jax.ShapeDtypeStruct((OWN, S * C), F32),
            jax.ShapeDtypeStruct((C * C, CZ), F32),
            jax.ShapeDtypeStruct((1, CZ), F32),
            jax.ShapeDtypeStruct((TI, TJ, CZ), BF16),
        ),
        in_specs=[hbm] * 5,
        out_specs=(hbm,) * 5,
        scratch_shapes=[
            pltpu.VMEM((OWN, S * C), F32),
            pltpu.VMEM((OWN, S * C), F32),
            pltpu.VMEM((C * C, CZ), F32),
            pltpu.VMEM((1, CZ), F32),
            pltpu.VMEM((TI, TJ, CZ), BF16),
            dma((2, 8)),
        ],
        name="finish",
    )(gl, gr, gw, gb, pair)
    return pair, grad_left, grad_right, grad_weight, grad_bias.reshape(CZ)


def solution(mesh):
    return jax.shard_map(
        per_device,
        mesh=mesh,
        in_specs=(
            P(("row", "col"), None),
            P(("col", "row"), None),
            P(),
            P(),
            P("row", "col", None),
        ),
        out_specs=(
            P("row", "col", None),
            P(("row", "col"), None),
            P(("col", "row"), None),
            P(),
            P(),
        ),
        check_vma=False,
    )
```

```python
import functools

import jax
import jax.numpy as jnp
from jax import lax
from jax.experimental import pallas as pl
from jax.experimental.pallas import tpu as pltpu
from jax.sharding import PartitionSpec as P

C = 32
CZ = 128
S = 128
ROWS = 16
COLS = 8
TI = 64
TJ = 128
CHIPS = 64
OWN = 8
MESH = pl.DeviceIdType.MESH
NN = (((1,), (0,)), ((), ()))
NT = (((1,), (1,)), ((), ()))
F32 = jnp.float32
BF16 = jnp.bfloat16


STEPS = sorted(
    ((n // 16, n // 4 % 4, n % 4) for n in range(1, CHIPS)),
    key=lambda t: tuple((2, 1, 3, 0).index(v) for v in t),
)


def dot(a, b, dims=NN):
    return lax.dot_general(a, b, dims, preferred_element_type=F32)


def swap(parts):
    block = lax.broadcasted_iota(jnp.int32, (C, S), 1) // C
    out = []
    for n in range(4):
        v = None
        for m in range(4):
            r = parts[m] if m == n else pltpu.roll(parts[m], (m - n) * C % S, 1)
            v = r if v is None else jnp.where(block == m, r, v)
        out.append(v)
    return out


def finish(*refs):
    ins, outs, hold, sem = refs[:5], refs[5:10], refs[10:15], refs[15]
    load, save = [], []
    for q in range(5):
        pieces = 4 if q == 4 else 1
        for k in range(pieces):
            n = ins[q].shape[0] // pieces
            part = pl.ds(k * n, n)
            load.append(pltpu.make_async_copy(ins[q].at[part], hold[q].at[part], sem.at[0, q + k]))
            save.append(pltpu.make_async_copy(hold[q].at[part], outs[q].at[part], sem.at[1, q + k]))
    for c in load:
        c.start()
    for c, e in zip(load, save):
        c.wait()
        e.start()
    for c in save:
        c.wait()


def kernel(
    left_hbm, right_hbm, weight_hbm, bias_ref, cot_hbm,
    pair_hbm, gl_hbm, gr_hbm, gw_hbm, bsum_ref,
    left_ref, right_ref, weight_ref, gl_ref, gr_ref, gw_ref, r_acc, in_sem, out_sem,
    gb_ref, stage, flat, cot, d, p, a_all, a_t, b_in, b_all, w_ref, w_t, pair,
    l_out, l_in, l_x, l_xin, r_keep, r_x, r_xin, r_out, r_in,
    w0, w0_in, w1_out, w1_in, w2_out, w_all,
    cot_sem, pair_sem, ax_s, ax_r, az_s, az_r, bc_s, bc_r, bx_s, bx_r, by_s, by_r,
    l_s, l_r, lx_s, lx_r, rx_s, rx_r, r_s, r_r,
    w0_s, w0_r, w1_s, w1_r, w2_s, w2_r, w3_s, w3_r,
):
    row = lax.axis_index("row")
    col = lax.axis_index("col")
    half = lax.div(row, 8)
    y = lax.rem(lax.div(row, 2), 4)
    core = lax.rem(row, 2)
    z = lax.div(col, 2)
    far = lax.rem(col, 2)
    mate = half * 8 + y * 2 + (1 - core)
    near = (1 - half) * 8 + y * 2 + core
    other = z * 2 + (1 - far)
    spot = half * 4 + y
    chip = spot * COLS + col

    def row_y(n, h=None):
        return (half if h is None else h) * 8 + lax.rem(y + n + 4, 4) * 2 + core

    def col_z(n, f=None):
        return lax.rem(z + n + 4, 4) * 2 + (far if f is None else f)

    def row_spot(n):
        q = lax.rem(spot + n + 8, 8)
        return q, q * 2 + core

    x = far * 2 + half
    xs, ys, zs = ([lax.rem(v + n, 4) for n in range(4)] for v in (x, y, z))
    row_x = [lax.rem(v, 2) * 8 + core for v in xs]
    col_x = [lax.div(v, 2) for v in xs]

    def chip_at(k):
        dx, dy, dz = STEPS[k]
        r = row_x[dx] + ys[dy] * 2
        c = col_x[dx] + zs[dz] * 2
        return lax.div(r, 2) * COLS + c, r, c

    def send(src, dst, ss, rs, k, r=None, c=None):
        return pltpu.make_async_remote_copy(
            src_ref=src, dst_ref=dst, send_sem=ss.at[k], recv_sem=rs.at[k],
            device_id=(row if r is None else r, col if c is None else c), device_id_type=MESH,
        )

    def each(n, f):
        def step(k, carry):
            f(k)
            return carry

        lax.fori_loop(0, n, step, 0)

    def cot_copy(q):
        part = pl.ds(q * 16, 16)
        return pltpu.make_async_copy(cot_hbm.at[part], cot.at[part], cot_sem.at[q])

    def pair_copy(q):
        part = pl.ds(q * 16, 16)
        return pltpu.make_async_copy(pair.at[part], pair_hbm.at[part], pair_sem.at[q])

    own_in = [
        pltpu.make_async_copy(src, dst, in_sem.at[q])
        for q, (src, dst) in enumerate(
            ((left_hbm, left_ref), (right_hbm, right_ref), (weight_hbm, weight_ref))
        )
    ]
    for q in range(3):
        own_in[q].start()

    barrier = pltpu.get_barrier_semaphore()

    def greet(r, c):
        pl.semaphore_signal(barrier, inc=1, device_id=(r, c), device_id_type=MESH)

    greet(near, col)
    greet(row, other)
    each(3, lambda k: greet(row_y(k + 1), col))
    each(3, lambda k: greet(row, col_z(k + 1)))
    greet(mate, col)

    each(4, lambda q: cot_copy(q).start())
    own_in[0].wait()
    own_in[1].wait()

    for n, ref in enumerate((left_ref, right_ref)):
        for q in range(C):
            stage[n, q * OWN:(q + 1) * OWN, :] = ref[:, q * S:(q + 1) * S].astype(F32)
    for n in range(2):
        for g in range(2):
            x = jnp.concatenate([stage[n, pl.ds(g * 4 + i, C, stride=OWN), :] for i in range(4)], axis=0)
            t = x.T
            parts = swap([t[m * C:(m + 1) * C] for m in range(4)])
            for i in range(4):
                if n == 0:
                    a_all[col, (g * 4 + i) * C:(g * 4 + i + 1) * C, :] = (parts[i] * (1.0 / S)).astype(BF16)
                else:
                    flat[pl.ds(g * 4 + i, C, stride=OWN), :] = parts[i]
    b_in[row] = flat[:OWN * C, :].astype(BF16)
    a_ref = a_all.at[col]
    b_ref = b_in.at[row]
    pl.semaphore_wait(barrier, 9)

    bx = send(b_ref, b_in.at[row], bx_s, bx_r, 0, r=near)
    bx.start()
    ax = send(a_ref, a_all.at[col], ax_s, ax_r, 0, c=other)
    ax.start()

    def by_own(k):
        return send(b_ref, b_in.at[row], by_s, by_r, k, r=row_y(k + 1))

    def az_own(k):
        return send(a_ref, a_all.at[col], az_s, az_r, k, c=col_z(k + 1))

    def by_near(k):
        return send(b_in.at[near], b_in.at[near], by_s, by_r, k + 3, r=row_y(k + 1))

    def az_other(k):
        return send(a_all.at[other], a_all.at[other], az_s, az_r, k + 3, c=col_z(k + 1))

    def bc_near():
        return send(b_in.at[near], b_in.at[near], bc_s, bc_r, 1, r=mate)

    def bc_y(k, h, first):
        slot = b_in.at[row_y(-1 - k, h)]
        return send(slot, slot, bc_s, bc_r, first + k, r=mate)

    bc_own = send(b_ref, b_in.at[row], bc_s, bc_r, 0, r=mate)
    each(3, lambda k: by_own(k).start())
    each(3, lambda k: az_own(k).start())
    bc_own.start()
    own_in[2].wait()
    flat[...] = weight_ref[...].astype(F32)
    for c in range(C):
        w_ref[c * C:(c + 1) * C, :] = flat[pl.ds(c, C, stride=C), :].astype(BF16)
    w_t[...] = w_ref[...].T

    def relay_x():
        send(b_ref, b_in.at[near], bx_s, bx_r, 0, r=near).wait_recv()
        each(3, lambda k: by_near(k).start())
        bc_near().start()
        send(a_ref, a_all.at[other], ax_s, ax_r, 0, c=other).wait_recv()
        each(3, lambda k: az_other(k).start())

    def relay_y(h, first, base):
        def step(k):
            slot = b_in.at[row_y(-1 - k, h)]
            send(b_ref, slot, by_s, by_r, base + k, r=row_y(k + 1)).wait_recv()
            bc_y(k, h, first).start()

        each(3, step)

    def wait_a(near_part):
        def step(k):
            f, n = (far, 0) if near_part else (1 - far, 3)
            send(a_ref, a_all.at[col_z(-1 - k, f)], az_s, az_r, k + n, c=col_z(k + 1)).wait()

        each(3, step)

    def end_b():
        def from_mate(k, r):
            slot = r - core + (1 - core)
            send(b_ref, b_in.at[slot], bc_s, bc_r, k, r=mate).wait()

        from_mate(0, row)
        from_mate(1, near)
        each(3, lambda k: from_mate(k + 2, row_y(-1 - k)))
        each(3, lambda k: from_mate(k + 5, row_y(-1 - k, 1 - half)))
        bx.wait_send()
        each(6, lambda k: send(b_ref, b_in.at[row], by_s, by_r, k, r=near).wait_send())

    gb_ref[...] = jnp.zeros_like(gb_ref)
    group = 16

    def d_step(g, carry):
        cot_copy(g).wait()
        block = cot[pl.ds(g * group, group)].reshape(group * TJ, CZ)
        r = dot(w_ref[...], block, NT).astype(BF16)
        for q in range(group):
            d[:, pl.ds((g * group + q) * C, C), :] = r[:, q * TJ:(q + 1) * TJ].reshape(C, C, TJ)
        gb_ref[...] += jnp.sum(block.astype(F32).reshape(group * TJ // 8, 8, CZ), axis=0)
        return carry

    lax.fori_loop(0, 2, d_step, 0)
    relay_x()
    lax.fori_loop(2, 4, d_step, 0)
    def rx(g):
        part = pl.ds(g * 64, 64)
        return send(r_x.at[:, part], r_xin.at[:, part], rx_s, rx_r, g, r=mate)

    def gr_part(g, f):
        x = jnp.concatenate(
            [
                jnp.concatenate(
                    [d[g * 8 + q, pl.ds((n * 2 + f) * 256, 256), :] for n in range(4)], axis=0
                )
                for q in range(8)
            ],
            axis=1,
        )
        return dot(a_t[...], x)

    def lay_a(f):
        for n in range(4):
            a_t[:, n * 256:(n + 1) * 256] = a_all[n * 2 + f].T

    def gr_first(g, carry):
        r_acc[g] = gr_part(g, far)
        return carry

    def gr_step(g, carry):
        r = r_acc[g] + gr_part(g, 1 - far)
        t = [r[:, q * TJ:(q + 1) * TJ].T.reshape(8, 16, S) for q in range(8)]
        even = [jnp.where(core == 0, v[:, :8], v[:, 8:]) for v in t]
        odd = [jnp.where(core == 0, v[:, 8:], v[:, :8]) for v in t]
        r_keep[:, pl.ds(g * 64, 64), :] = jnp.concatenate(even, axis=1)
        for h in range(4):
            both = jnp.concatenate(odd[2 * h:2 * h + 2], axis=1)
            r_x[:, pl.ds(g * 64 + h * 16, 16), :] = both.astype(BF16)
        rx(g).start()
        return carry

    relay_y(half, 2, 0)
    wait_a(True)
    lay_a(far)
    lax.fori_loop(0, C // 8, gr_first, 0)
    relay_y(1 - half, 5, 3)
    wait_a(False)
    ax.wait_send()
    lay_a(1 - far)
    lax.fori_loop(0, C // 8, gr_step, 0)
    end_b()

    def lay_b(q, carry):
        part = b_in[:, pl.ds(q * 16, 16), :].astype(F32)
        for h in range(2):
            b_all[pl.ds((q * 2 + h) * TJ, TJ), :] = part[:, h * 8:(h + 1) * 8, :].reshape(TJ, S).astype(BF16)
        return carry

    lax.fori_loop(0, C // 2, lay_b, 0, unroll=4)

    def p_step(n, carry):
        rhs = b_all[pl.ds(n * 2048, 2048), :]
        for m in range(8):
            r = dot(a_all[m], rhs, NT).astype(BF16)
            for q in range(16):
                p[n * 16 + q, m * 256:(m + 1) * 256, :] = r[:, q * TJ:(q + 1) * TJ]
        return carry

    lax.fori_loop(0, 1, p_step, 0)

    def send_r(k):
        q, r = row_spot(k + 1)
        return send(r_out.at[q], r_in.at[spot], r_s, r_r, k, r=r)

    each(4, lambda g: rx(g).wait())

    def sum_x(q):
        r_out[q] = (r_keep[q] + r_xin[q].astype(F32)).astype(BF16)

    each(8, sum_x)
    each(7, lambda k: send_r(k).start())
    r_in[spot] = r_out[spot]

    lax.fori_loop(1, 2, p_step, 0)

    def gw_step(g, carry):
        x = jnp.concatenate(
            [p[pl.ds(g * 16, 16), q * C:(q + 1) * C, :].reshape(16 * C, TJ) for q in range(TI)], axis=1
        )
        w0[g, :512, :] = dot(x, cot[...].reshape(TI * TJ, CZ))
        return carry

    lax.fori_loop(0, 2, gw_step, 0)
    w0[0, 512:, :] = gb_ref[...]
    w0[1, 512:, :] = gb_ref[...]
    w0_copy = send(w0.at[1 - core], w0_in, w0_s, w0_r, 0, r=mate)
    w0_copy.start()


    def send_l(m, slot):
        to = lax.rem(z + 1 + m, 4)
        return send(l_out.at[pl.ds(to * 2, 2)], l_in.at[pl.ds(slot * 2, 2)], l_s, l_r, m, c=to * 2 + far)

    def gl_step(m, carry):
        to = lax.rem(z + 1 + m, 4)
        x = jnp.concatenate([d[q, pl.ds(to * 512, 512), :] for q in range(C)], axis=1)
        r = (dot(x, b_all[...]) * (1.0 / S)).astype(BF16)
        for h in range(2):
            l_out[to * 2 + h] = r[h * 256:(h + 1) * 256, :]
        send_l(m, z).start()
        return carry

    lax.fori_loop(0, 1, gl_step, 0)

    w0_copy.wait()
    v = (w0[core, :512, :] + w0_in[:512, :]).reshape(CHIPS, 8, CZ)
    bias = jnp.sum(w0[core, 512:, :] + w0_in[512:, :], axis=0, keepdims=True)
    upper = bias.astype(BF16).astype(F32)
    place = lax.broadcasted_iota(jnp.int32, (8, CZ), 0)
    extra = jnp.where(place == 0, upper, jnp.where(place == 1, bias - upper, 0.0))
    w1_out[...] = jnp.concatenate([v, jnp.broadcast_to(extra, (CHIPS, 8, CZ))], axis=1).astype(BF16)

    def send_w1(k):
        m, r, c = chip_at(k)
        return send(w1_out.at[m], w1_in.at[chip], w1_s, w1_r, k, r=r, c=c)

    each(7, lambda k: send(r_out.at[0], r_in.at[row_spot(-1 - k)[0]], r_s, r_r, k, r=near).wait())
    for k in range(CHIPS - 1):
        send_w1(k).start()
    w1_in[chip] = w1_out[chip]

    lax.fori_loop(1, 3, gl_step, 0)

    def gl_last():
        x = jnp.concatenate([d[q, pl.ds(z * 512, 512), :] for q in range(C)], axis=1)
        r = (dot(x, b_all[...]) * (1.0 / S)).astype(BF16)
        for h in range(2):
            l_out[z * 2 + h] = r[h * 256:(h + 1) * 256, :]
        l_in[pl.ds(z * 2, 2)] = l_out[pl.ds(z * 2, 2)]

    gl_last()

    def pair_step(g, carry):
        x = jnp.concatenate(
            [p[:, pl.ds((g * 16 + q) * C, C), :].reshape(C * C, TJ) for q in range(16)], axis=1
        )
        r = dot(w_t[...], x)
        for q in range(16):
            pair[g * 16 + q] = (r[:, q * TJ:(q + 1) * TJ].T + bias_ref[...]).astype(BF16)
        pair_copy(g).start()
        return carry

    lax.fori_loop(0, 1, pair_step, 0)

    def wait_w1(k):
        send(w1_out.at[k], w1_in.at[k], w1_s, w1_r, k, r=near).wait()

    each(CHIPS - 1, wait_w1)
    s1 = w1_in[0].astype(F32)
    for q in range(1, CHIPS):
        s1 += w1_in[q].astype(F32)
    w2_out[...] = s1[:8, :]
    bsum_ref[...] = s1[8:9, :] + s1[9:10, :]

    def send_w2(k):
        _, r, c = chip_at(k)
        return send(w2_out, w_all.at[core, chip], w2_s, w2_r, k, r=r, c=c)

    for k in range(CHIPS - 1):
        send_w2(k).start()
    w_all[core, chip] = w2_out[...]

    lax.fori_loop(1, 4, pair_step, 0)

    def lay_out(n, rows, out):
        for g in range(2):
            stage[n, g * S:(g + 1) * S, :] = jnp.concatenate(swap(rows[g * 4:g * 4 + 4]), axis=0).T
        for q in range(C):
            out[:, q * S:(q + 1) * S] = stage[n, pl.ds(q, OWN, stride=C), :]

    total = r_in[0].astype(F32)
    for q in range(1, 8):
        total += r_in[q].astype(F32)
    flat[:OWN * C, :] = total
    lay_out(1, [flat[pl.ds(i, C, stride=OWN), :] for i in range(OWN)], gr_ref)
    gr_copy = pltpu.make_async_copy(gr_ref, gr_hbm, out_sem.at[1])
    gr_copy.start()

    each(3, lambda m: send_l(m, lax.rem(z + 3 - m, 4)).wait())
    theirs = l_in[1 - far].astype(F32)
    for q in range(1, 4):
        theirs += l_in[2 * q + 1 - far].astype(F32)
    l_x[...] = theirs.astype(BF16)
    lx = send(l_x, l_xin, lx_s, lx_r, 0, c=other)
    lx.start()
    total = l_in[far].astype(F32)
    for q in range(1, 4):
        total += l_in[2 * q + far].astype(F32)
    stage[0] = total

    lx.wait()
    total = stage[0] + l_xin[...].astype(F32)
    lay_out(0, [total[i * C:(i + 1) * C, :] for i in range(OWN)], gl_ref)
    gl_copy = pltpu.make_async_copy(gl_ref, gl_hbm, out_sem.at[0])
    gl_copy.start()

    each(CHIPS - 1, lambda k: send(w2_out, w_all.at[core, k], w2_s, w2_r, k, r=near).wait())
    send(w_all.at[core], w_all.at[core], w3_s, w3_r, 0, r=mate).start()
    send(w_all.at[core], w_all.at[1 - core], w3_s, w3_r, 0, r=mate).wait()
    for c in range(C):
        gw_ref[pl.ds(c, C, stride=C), :] = w_all[c // 16, c % 16 * 4:c % 16 * 4 + 4].reshape(C, CZ)
    gw_copy = pltpu.make_async_copy(gw_ref, gw_hbm, out_sem.at[2])
    gw_copy.start()
    gl_copy.wait()
    gr_copy.wait()
    gw_copy.wait()
    each(4, lambda q: pair_copy(q).wait())


def per_device(left_proj, right_proj, out_weight, out_bias, pair_cotangent):
    vmem = pl.BlockSpec(memory_space=pltpu.VMEM)
    hbm = pl.BlockSpec(memory_space=pl.ANY)
    dma = pltpu.SemaphoreType.DMA
    own = OWN * C
    pair, gl, gr, gw, gb = pl.pallas_call(
        kernel,
        out_shape=(
            jax.ShapeDtypeStruct((TI, TJ, CZ), BF16),
            jax.ShapeDtypeStruct((OWN, S * C), F32),
            jax.ShapeDtypeStruct((OWN, S * C), F32),
            jax.ShapeDtypeStruct((C * C, CZ), F32),
            jax.ShapeDtypeStruct((1, CZ), F32),
        ),
        in_specs=[hbm, hbm, hbm, vmem, hbm],
        out_specs=(hbm, hbm, hbm, hbm, vmem),
        scratch_shapes=[
            pltpu.VMEM((OWN, S * C), BF16),
            pltpu.VMEM((OWN, S * C), BF16),
            pltpu.VMEM((C * C, CZ), BF16),
            pltpu.VMEM((OWN, S * C), F32),
            pltpu.VMEM((OWN, S * C), F32),
            pltpu.VMEM((C * C, CZ), F32),
            pltpu.VMEM((4, S, 8 * TJ), F32),
            dma((3,)),
            dma((3,)),
            pltpu.VMEM((8, CZ), F32),
            pltpu.VMEM((2, own, S), F32),
            pltpu.VMEM((C * C, CZ), F32),
            pltpu.VMEM((TI, TJ, CZ), BF16),
            pltpu.VMEM((C, TI * C, TJ), BF16),
            pltpu.VMEM((C, TI * C, TJ), BF16),
            pltpu.VMEM((COLS, own, S), BF16),
            pltpu.VMEM((S, TI * C // 2), BF16),
            pltpu.VMEM((ROWS, own, S), BF16),
            pltpu.VMEM((C * TJ, S), BF16),
            pltpu.VMEM((C * C, CZ), BF16),
            pltpu.VMEM((CZ, C * C), BF16),
            pltpu.VMEM((TI, TJ, CZ), BF16),
            pltpu.VMEM((COLS, own, S), BF16),
            pltpu.VMEM((COLS, own, S), BF16),
            pltpu.VMEM((own, S), BF16),
            pltpu.VMEM((own, S), BF16),
            pltpu.VMEM((8, own, S), F32),
            pltpu.VMEM((8, own, S), BF16),
            pltpu.VMEM((8, own, S), BF16),
            pltpu.VMEM((8, own, S), BF16),
            pltpu.VMEM((8, own, S), BF16),
            pltpu.VMEM((2, 520, CZ), F32),
            pltpu.VMEM((520, CZ), F32),
            pltpu.VMEM((CHIPS, 16, CZ), BF16),
            pltpu.VMEM((CHIPS, 16, CZ), BF16),
            pltpu.VMEM((8, CZ), F32),
            pltpu.VMEM((2, CHIPS, 8, CZ), F32),
            dma((4,)), dma((4,)),
            dma((1,)), dma((1,)), dma((6,)), dma((6,)),
            dma((8,)), dma((8,)), dma((1,)), dma((1,)), dma((6,)), dma((6,)),
            dma((3,)), dma((3,)), dma((1,)), dma((1,)),
            dma((4,)), dma((4,)), dma((7,)), dma((7,)),
            dma((1,)), dma((1,)), dma((CHIPS - 1,)), dma((CHIPS - 1,)),
            dma((CHIPS - 1,)), dma((CHIPS - 1,)), dma((1,)), dma((1,)),
        ],
        compiler_params=pltpu.CompilerParams(
            collective_id=0, has_side_effects=True, vmem_limit_bytes=56 << 20
        ),
        name="outer_product_mean",
    )(left_proj, right_proj, out_weight, out_bias.reshape(1, CZ), pair_cotangent)
    grad_left, grad_right, grad_weight, grad_bias, pair = pl.pallas_call(
        finish,
        out_shape=(
            jax.ShapeDtypeStruct((OWN, S * C), F32),
            jax.ShapeDtypeStruct((OWN, S * C), F32),
            jax.ShapeDtypeStruct((C * C, CZ), F32),
            jax.ShapeDtypeStruct((1, CZ), F32),
            jax.ShapeDtypeStruct((TI, TJ, CZ), BF16),
        ),
        in_specs=[hbm] * 5,
        out_specs=(hbm,) * 5,
        scratch_shapes=[
            pltpu.VMEM((OWN, S * C), F32),
            pltpu.VMEM((OWN, S * C), F32),
            pltpu.VMEM((C * C, CZ), F32),
            pltpu.VMEM((1, CZ), F32),
            pltpu.VMEM((TI, TJ, CZ), BF16),
            dma((2, 8)),
        ],
        name="finish",
    )(gl, gr, gw, gb, pair)
    return pair, grad_left, grad_right, grad_weight, grad_bias.reshape(CZ)


def solution(mesh):
    return jax.shard_map(
        per_device,
        mesh=mesh,
        in_specs=(
            P(("row", "col"), None),
            P(("col", "row"), None),
            P(),
            P(),
            P("row", "col", None),
        ),
        out_specs=(
            P("row", "col", None),
            P(("row", "col"), None),
            P(("col", "row"), None),
            P(),
            P(),
        ),
        check_vma=False,
    )
```

```python
import functools

import jax
import jax.numpy as jnp
from jax import lax
from jax.experimental import pallas as pl
from jax.experimental.pallas import tpu as pltpu
from jax.sharding import PartitionSpec as P

C = 32
CZ = 128
S = 128
ROWS = 16
COLS = 8
TI = 64
TJ = 128
CHIPS = 64
OWN = 8
MESH = pl.DeviceIdType.MESH
NN = (((1,), (0,)), ((), ()))
NT = (((1,), (1,)), ((), ()))
F32 = jnp.float32
BF16 = jnp.bfloat16


STEPS = sorted(
    ((n // 16, n // 4 % 4, n % 4) for n in range(1, CHIPS)),
    key=lambda t: tuple((2, 1, 3, 0).index(v) for v in t),
)


def dot(a, b, dims=NN):
    return lax.dot_general(a, b, dims, preferred_element_type=F32)


def swap(parts):
    block = lax.broadcasted_iota(jnp.int32, (C, S), 1) // C
    out = []
    for n in range(4):
        v = None
        for m in range(4):
            r = parts[m] if m == n else pltpu.roll(parts[m], (m - n) * C % S, 1)
            v = r if v is None else jnp.where(block == m, r, v)
        out.append(v)
    return out


def finish(*refs):
    ins, outs, hold, sem = refs[:5], refs[5:10], refs[10:15], refs[15]
    load, save = [], []
    for q in range(5):
        pieces = 4 if q == 4 else 1
        for k in range(pieces):
            n = ins[q].shape[0] // pieces
            part = pl.ds(k * n, n)
            load.append(pltpu.make_async_copy(ins[q].at[part], hold[q].at[part], sem.at[0, q + k]))
            save.append(pltpu.make_async_copy(hold[q].at[part], outs[q].at[part], sem.at[1, q + k]))
    for c in load:
        c.start()
    for c, e in zip(load, save):
        c.wait()
        e.start()
    for c in save:
        c.wait()


def kernel(
    left_hbm, right_hbm, weight_hbm, bias_ref, cot_hbm,
    pair_hbm, gl_hbm, gr_hbm, gw_hbm, bsum_ref,
    left_ref, right_ref, weight_ref, gl_ref, gr_ref, gw_ref, r_acc, in_sem, out_sem,
    gb_ref, stage, flat, cot, d, p, a_all, a_t, b_in, b_all, w_ref, w_t, pair,
    l_out, l_in, l_x, l_xin, r_keep, r_x, r_xin, r_out, r_in,
    w0, w0_in, w1_out, w1_in, w2_out, w_all,
    cot_sem, pair_sem, ax_s, ax_r, az_s, az_r, bc_s, bc_r, bx_s, bx_r, by_s, by_r,
    l_s, l_r, lx_s, lx_r, rx_s, rx_r, r_s, r_r,
    w0_s, w0_r, w1_s, w1_r, w2_s, w2_r, w3_s, w3_r,
):
    row = lax.axis_index("row")
    col = lax.axis_index("col")
    half = lax.div(row, 8)
    y = lax.rem(lax.div(row, 2), 4)
    core = lax.rem(row, 2)
    z = lax.div(col, 2)
    far = lax.rem(col, 2)
    mate = half * 8 + y * 2 + (1 - core)
    near = (1 - half) * 8 + y * 2 + core
    other = z * 2 + (1 - far)
    spot = half * 4 + y
    chip = spot * COLS + col

    def row_y(n, h=None):
        return (half if h is None else h) * 8 + lax.rem(y + n + 4, 4) * 2 + core

    def col_z(n, f=None):
        return lax.rem(z + n + 4, 4) * 2 + (far if f is None else f)

    def row_spot(n):
        q = lax.rem(spot + n + 8, 8)
        return q, q * 2 + core

    x = far * 2 + half
    xs, ys, zs = ([lax.rem(v + n, 4) for n in range(4)] for v in (x, y, z))
    row_x = [lax.rem(v, 2) * 8 + core for v in xs]
    col_x = [lax.div(v, 2) for v in xs]

    def chip_at(k):
        dx, dy, dz = STEPS[k]
        r = row_x[dx] + ys[dy] * 2
        c = col_x[dx] + zs[dz] * 2
        return lax.div(r, 2) * COLS + c, r, c

    def send(src, dst, ss, rs, k, r=None, c=None):
        return pltpu.make_async_remote_copy(
            src_ref=src, dst_ref=dst, send_sem=ss.at[k], recv_sem=rs.at[k],
            device_id=(row if r is None else r, col if c is None else c), device_id_type=MESH,
        )

    def each(n, f):
        def step(k, carry):
            f(k)
            return carry

        lax.fori_loop(0, n, step, 0)

    def cot_copy(q):
        part = pl.ds(q * 16, 16)
        return pltpu.make_async_copy(cot_hbm.at[part], cot.at[part], cot_sem.at[q])

    def pair_copy(q):
        part = pl.ds(q * 16, 16)
        return pltpu.make_async_copy(pair.at[part], pair_hbm.at[part], pair_sem.at[q])

    own_in = [
        pltpu.make_async_copy(src, dst, in_sem.at[q])
        for q, (src, dst) in enumerate(
            ((left_hbm, left_ref), (right_hbm, right_ref), (weight_hbm, weight_ref))
        )
    ]
    for q in range(3):
        own_in[q].start()

    barrier = pltpu.get_barrier_semaphore()

    def greet(r, c):
        pl.semaphore_signal(barrier, inc=1, device_id=(r, c), device_id_type=MESH)

    greet(near, col)
    greet(row, other)
    each(3, lambda k: greet(row_y(k + 1), col))
    each(3, lambda k: greet(row, col_z(k + 1)))
    greet(mate, col)

    each(4, lambda q: cot_copy(q).start())
    own_in[0].wait()
    own_in[1].wait()

    for n, ref in enumerate((left_ref, right_ref)):
        for q in range(C):
            stage[n, q * OWN:(q + 1) * OWN, :] = ref[:, q * S:(q + 1) * S].astype(F32)
    for n in range(2):
        for g in range(2):
            x = jnp.concatenate([stage[n, pl.ds(g * 4 + i, C, stride=OWN), :] for i in range(4)], axis=0)
            t = x.T
            parts = swap([t[m * C:(m + 1) * C] for m in range(4)])
            for i in range(4):
                if n == 0:
                    a_all[col, (g * 4 + i) * C:(g * 4 + i + 1) * C, :] = (parts[i] * (1.0 / S)).astype(BF16)
                else:
                    flat[pl.ds(g * 4 + i, C, stride=OWN), :] = parts[i]
    b_in[row] = flat[:OWN * C, :].astype(BF16)
    a_ref = a_all.at[col]
    b_ref = b_in.at[row]
    pl.semaphore_wait(barrier, 9)

    bx = send(b_ref, b_in.at[row], bx_s, bx_r, 0, r=near)
    bx.start()
    ax = send(a_ref, a_all.at[col], ax_s, ax_r, 0, c=other)
    ax.start()

    def by_own(k):
        return send(b_ref, b_in.at[row], by_s, by_r, k, r=row_y(k + 1))

    def az_own(k):
        return send(a_ref, a_all.at[col], az_s, az_r, k, c=col_z(k + 1))

    def by_near(k):
        return send(b_in.at[near], b_in.at[near], by_s, by_r, k + 3, r=row_y(k + 1))

    def az_other(k):
        return send(a_all.at[other], a_all.at[other], az_s, az_r, k + 3, c=col_z(k + 1))

    def bc_near():
        return send(b_in.at[near], b_in.at[near], bc_s, bc_r, 1, r=mate)

    def bc_y(k, h, first):
        slot = b_in.at[row_y(-1 - k, h)]
        return send(slot, slot, bc_s, bc_r, first + k, r=mate)

    bc_own = send(b_ref, b_in.at[row], bc_s, bc_r, 0, r=mate)
    each(3, lambda k: by_own(k).start())
    each(3, lambda k: az_own(k).start())
    bc_own.start()
    own_in[2].wait()
    flat[...] = weight_ref[...].astype(F32)
    for c in range(C):
        w_ref[c * C:(c + 1) * C, :] = flat[pl.ds(c, C, stride=C), :].astype(BF16)
    w_t[...] = w_ref[...].T

    def relay_x():
        send(b_ref, b_in.at[near], bx_s, bx_r, 0, r=near).wait_recv()
        each(3, lambda k: by_near(k).start())
        bc_near().start()
        send(a_ref, a_all.at[other], ax_s, ax_r, 0, c=other).wait_recv()
        each(3, lambda k: az_other(k).start())

    def relay_y(h, first, base):
        def step(k):
            slot = b_in.at[row_y(-1 - k, h)]
            send(b_ref, slot, by_s, by_r, base + k, r=row_y(k + 1)).wait_recv()
            bc_y(k, h, first).start()

        each(3, step)

    def wait_a(near_part):
        def step(k):
            f, n = (far, 0) if near_part else (1 - far, 3)
            send(a_ref, a_all.at[col_z(-1 - k, f)], az_s, az_r, k + n, c=col_z(k + 1)).wait()

        each(3, step)

    def end_b():
        def from_mate(k, r):
            slot = r - core + (1 - core)
            send(b_ref, b_in.at[slot], bc_s, bc_r, k, r=mate).wait()

        from_mate(0, row)
        from_mate(1, near)
        each(3, lambda k: from_mate(k + 2, row_y(-1 - k)))
        each(3, lambda k: from_mate(k + 5, row_y(-1 - k, 1 - half)))
        bx.wait_send()
        each(6, lambda k: send(b_ref, b_in.at[row], by_s, by_r, k, r=near).wait_send())

    gb_ref[...] = jnp.zeros_like(gb_ref)
    group = 16

    def d_step(g, carry):
        cot_copy(g).wait()
        block = cot[pl.ds(g * group, group)].reshape(group * TJ, CZ)
        r = dot(w_ref[...], block, NT).astype(BF16)
        for q in range(group):
            d[:, pl.ds((g * group + q) * C, C), :] = r[:, q * TJ:(q + 1) * TJ].reshape(C, C, TJ)
        gb_ref[...] += jnp.sum(block.astype(F32).reshape(group * TJ // 8, 8, CZ), axis=0)
        return carry

    lax.fori_loop(0, 2, d_step, 0)
    relay_x()
    lax.fori_loop(2, 4, d_step, 0)
    def rx(g):
        part = pl.ds(g * 64, 64)
        return send(r_x.at[:, part], r_xin.at[:, part], rx_s, rx_r, g, r=mate)

    def gr_part(g, f):
        x = jnp.concatenate(
            [
                jnp.concatenate(
                    [d[g * 8 + q, pl.ds((n * 2 + f) * 256, 256), :] for n in range(4)], axis=0
                )
                for q in range(8)
            ],
            axis=1,
        )
        return dot(a_t[...], x)

    def lay_a(f):
        for n in range(4):
            a_t[:, n * 256:(n + 1) * 256] = a_all[n * 2 + f].T

    def gr_first(g, carry):
        r_acc[g] = gr_part(g, far)
        return carry

    def gr_step(g, carry):
        r = r_acc[g] + gr_part(g, 1 - far)
        t = [r[:, q * TJ:(q + 1) * TJ].T.reshape(8, 16, S) for q in range(8)]
        even = [jnp.where(core == 0, v[:, :8], v[:, 8:]) for v in t]
        odd = [jnp.where(core == 0, v[:, 8:], v[:, :8]) for v in t]
        r_keep[:, pl.ds(g * 64, 64), :] = jnp.concatenate(even, axis=1)
        for h in range(4):
            both = jnp.concatenate(odd[2 * h:2 * h + 2], axis=1)
            r_x[:, pl.ds(g * 64 + h * 16, 16), :] = both.astype(BF16)
        rx(g).start()
        return carry

    relay_y(half, 2, 0)
    wait_a(True)
    lay_a(far)
    lax.fori_loop(0, C // 8, gr_first, 0)
    relay_y(1 - half, 5, 3)
    wait_a(False)
    ax.wait_send()
    lay_a(1 - far)
    lax.fori_loop(0, C // 8, gr_step, 0)
    end_b()

    def lay_b(q, carry):
        part = b_in[:, pl.ds(q * 16, 16), :].astype(F32)
        for h in range(2):
            b_all[pl.ds((q * 2 + h) * TJ, TJ), :] = part[:, h * 8:(h + 1) * 8, :].reshape(TJ, S).astype(BF16)
        return carry

    lax.fori_loop(0, C // 2, lay_b, 0, unroll=4)

    def p_step(n, carry):
        rhs = b_all[pl.ds(n * 2048, 2048), :]
        for m in range(8):
            r = dot(a_all[m], rhs, NT).astype(BF16)
            for q in range(16):
                p[n * 16 + q, m * 256:(m + 1) * 256, :] = r[:, q * TJ:(q + 1) * TJ]
        return carry

    lax.fori_loop(0, 1, p_step, 0)

    def send_r(k):
        q, r = row_spot(k + 1)
        return send(r_out.at[q], r_in.at[spot], r_s, r_r, k, r=r)

    each(4, lambda g: rx(g).wait())

    def sum_x(q):
        r_out[q] = (r_keep[q] + r_xin[q].astype(F32)).astype(BF16)

    each(8, sum_x)
    each(7, lambda k: send_r(k).start())
    r_in[spot] = r_out[spot]

    lax.fori_loop(1, 2, p_step, 0)

    def gw_step(g, carry):
        x = jnp.concatenate(
            [p[pl.ds(g * 16, 16), q * C:(q + 1) * C, :].reshape(16 * C, TJ) for q in range(TI)], axis=1
        )
        w0[g, :512, :] = dot(x, cot[...].reshape(TI * TJ, CZ))
        return carry

    lax.fori_loop(0, 2, gw_step, 0)
    w0[0, 512:, :] = gb_ref[...]
    w0[1, 512:, :] = gb_ref[...]
    w0_copy = send(w0.at[1 - core], w0_in, w0_s, w0_r, 0, r=mate)
    w0_copy.start()


    def send_l(m, slot):
        to = lax.rem(z + 1 + m, 4)
        return send(l_out.at[pl.ds(to * 2, 2)], l_in.at[pl.ds(slot * 2, 2)], l_s, l_r, m, c=to * 2 + far)

    def gl_step(m, carry):
        to = lax.rem(z + 1 + m, 4)
        x = jnp.concatenate([d[q, pl.ds(to * 512, 512), :] for q in range(C)], axis=1)
        r = (dot(x, b_all[...]) * (1.0 / S)).astype(BF16)
        for h in range(2):
            l_out[to * 2 + h] = r[h * 256:(h + 1) * 256, :]
        send_l(m, z).start()
        return carry

    lax.fori_loop(0, 2, gl_step, 0)

    w0_copy.wait()
    v = (w0[core, :512, :] + w0_in[:512, :]).reshape(CHIPS, 8, CZ)
    bias = jnp.sum(w0[core, 512:, :] + w0_in[512:, :], axis=0, keepdims=True)
    upper = bias.astype(BF16).astype(F32)
    place = lax.broadcasted_iota(jnp.int32, (8, CZ), 0)
    extra = jnp.where(place == 0, upper, jnp.where(place == 1, bias - upper, 0.0))
    w1_out[...] = jnp.concatenate([v, jnp.broadcast_to(extra, (CHIPS, 8, CZ))], axis=1).astype(BF16)

    def send_w1(k):
        m, r, c = chip_at(k)
        return send(w1_out.at[m], w1_in.at[chip], w1_s, w1_r, k, r=r, c=c)

    each(7, lambda k: send(r_out.at[0], r_in.at[row_spot(-1 - k)[0]], r_s, r_r, k, r=near).wait())
    for k in range(CHIPS - 1):
        send_w1(k).start()
    w1_in[chip] = w1_out[chip]

    lax.fori_loop(2, 3, gl_step, 0)

    def gl_last():
        x = jnp.concatenate([d[q, pl.ds(z * 512, 512), :] for q in range(C)], axis=1)
        r = (dot(x, b_all[...]) * (1.0 / S)).astype(BF16)
        for h in range(2):
            l_out[z * 2 + h] = r[h * 256:(h + 1) * 256, :]
        l_in[pl.ds(z * 2, 2)] = l_out[pl.ds(z * 2, 2)]

    gl_last()

    def pair_step(g, carry):
        x = jnp.concatenate(
            [p[:, pl.ds((g * 16 + q) * C, C), :].reshape(C * C, TJ) for q in range(16)], axis=1
        )
        r = dot(w_t[...], x)
        for q in range(16):
            pair[g * 16 + q] = (r[:, q * TJ:(q + 1) * TJ].T + bias_ref[...]).astype(BF16)
        pair_copy(g).start()
        return carry

    lax.fori_loop(0, 1, pair_step, 0)

    def wait_w1(k):
        send(w1_out.at[k], w1_in.at[k], w1_s, w1_r, k, r=near).wait()

    each(CHIPS - 1, wait_w1)
    s1 = w1_in[0].astype(F32)
    for q in range(1, CHIPS):
        s1 += w1_in[q].astype(F32)
    w2_out[...] = s1[:8, :]
    bsum_ref[...] = s1[8:9, :] + s1[9:10, :]

    def send_w2(k):
        _, r, c = chip_at(k)
        return send(w2_out, w_all.at[core, chip], w2_s, w2_r, k, r=r, c=c)

    for k in range(CHIPS - 1):
        send_w2(k).start()
    w_all[core, chip] = w2_out[...]

    lax.fori_loop(1, 4, pair_step, 0)

    def lay_out(n, rows, out):
        for g in range(2):
            stage[n, g * S:(g + 1) * S, :] = jnp.concatenate(swap(rows[g * 4:g * 4 + 4]), axis=0).T
        for q in range(C):
            out[:, q * S:(q + 1) * S] = stage[n, pl.ds(q, OWN, stride=C), :]

    total = r_in[0].astype(F32)
    for q in range(1, 8):
        total += r_in[q].astype(F32)
    flat[:OWN * C, :] = total
    lay_out(1, [flat[pl.ds(i, C, stride=OWN), :] for i in range(OWN)], gr_ref)
    gr_copy = pltpu.make_async_copy(gr_ref, gr_hbm, out_sem.at[1])
    gr_copy.start()

    each(3, lambda m: send_l(m, lax.rem(z + 3 - m, 4)).wait())
    theirs = l_in[1 - far].astype(F32)
    for q in range(1, 4):
        theirs += l_in[2 * q + 1 - far].astype(F32)
    l_x[...] = theirs.astype(BF16)
    lx = send(l_x, l_xin, lx_s, lx_r, 0, c=other)
    lx.start()
    total = l_in[far].astype(F32)
    for q in range(1, 4):
        total += l_in[2 * q + far].astype(F32)
    stage[0] = total

    lx.wait()
    total = stage[0] + l_xin[...].astype(F32)
    lay_out(0, [total[i * C:(i + 1) * C, :] for i in range(OWN)], gl_ref)
    gl_copy = pltpu.make_async_copy(gl_ref, gl_hbm, out_sem.at[0])
    gl_copy.start()

    each(CHIPS - 1, lambda k: send(w2_out, w_all.at[core, k], w2_s, w2_r, k, r=near).wait())
    send(w_all.at[core], w_all.at[core], w3_s, w3_r, 0, r=mate).start()
    send(w_all.at[core], w_all.at[1 - core], w3_s, w3_r, 0, r=mate).wait()
    for c in range(C):
        gw_ref[pl.ds(c, C, stride=C), :] = w_all[c // 16, c % 16 * 4:c % 16 * 4 + 4].reshape(C, CZ)
    gw_copy = pltpu.make_async_copy(gw_ref, gw_hbm, out_sem.at[2])
    gw_copy.start()
    gl_copy.wait()
    gr_copy.wait()
    gw_copy.wait()
    each(4, lambda q: pair_copy(q).wait())


def per_device(left_proj, right_proj, out_weight, out_bias, pair_cotangent):
    vmem = pl.BlockSpec(memory_space=pltpu.VMEM)
    hbm = pl.BlockSpec(memory_space=pl.ANY)
    dma = pltpu.SemaphoreType.DMA
    own = OWN * C
    pair, gl, gr, gw, gb = pl.pallas_call(
        kernel,
        out_shape=(
            jax.ShapeDtypeStruct((TI, TJ, CZ), BF16),
            jax.ShapeDtypeStruct((OWN, S * C), F32),
            jax.ShapeDtypeStruct((OWN, S * C), F32),
            jax.ShapeDtypeStruct((C * C, CZ), F32),
            jax.ShapeDtypeStruct((1, CZ), F32),
        ),
        in_specs=[hbm, hbm, hbm, vmem, hbm],
        out_specs=(hbm, hbm, hbm, hbm, vmem),
        scratch_shapes=[
            pltpu.VMEM((OWN, S * C), BF16),
            pltpu.VMEM((OWN, S * C), BF16),
            pltpu.VMEM((C * C, CZ), BF16),
            pltpu.VMEM((OWN, S * C), F32),
            pltpu.VMEM((OWN, S * C), F32),
            pltpu.VMEM((C * C, CZ), F32),
            pltpu.VMEM((4, S, 8 * TJ), F32),
            dma((3,)),
            dma((3,)),
            pltpu.VMEM((8, CZ), F32),
            pltpu.VMEM((2, own, S), F32),
            pltpu.VMEM((C * C, CZ), F32),
            pltpu.VMEM((TI, TJ, CZ), BF16),
            pltpu.VMEM((C, TI * C, TJ), BF16),
            pltpu.VMEM((C, TI * C, TJ), BF16),
            pltpu.VMEM((COLS, own, S), BF16),
            pltpu.VMEM((S, TI * C // 2), BF16),
            pltpu.VMEM((ROWS, own, S), BF16),
            pltpu.VMEM((C * TJ, S), BF16),
            pltpu.VMEM((C * C, CZ), BF16),
            pltpu.VMEM((CZ, C * C), BF16),
            pltpu.VMEM((TI, TJ, CZ), BF16),
            pltpu.VMEM((COLS, own, S), BF16),
            pltpu.VMEM((COLS, own, S), BF16),
            pltpu.VMEM((own, S), BF16),
            pltpu.VMEM((own, S), BF16),
            pltpu.VMEM((8, own, S), F32),
            pltpu.VMEM((8, own, S), BF16),
            pltpu.VMEM((8, own, S), BF16),
            pltpu.VMEM((8, own, S), BF16),
            pltpu.VMEM((8, own, S), BF16),
            pltpu.VMEM((2, 520, CZ), F32),
            pltpu.VMEM((520, CZ), F32),
            pltpu.VMEM((CHIPS, 16, CZ), BF16),
            pltpu.VMEM((CHIPS, 16, CZ), BF16),
            pltpu.VMEM((8, CZ), F32),
            pltpu.VMEM((2, CHIPS, 8, CZ), F32),
            dma((4,)), dma((4,)),
            dma((1,)), dma((1,)), dma((6,)), dma((6,)),
            dma((8,)), dma((8,)), dma((1,)), dma((1,)), dma((6,)), dma((6,)),
            dma((3,)), dma((3,)), dma((1,)), dma((1,)),
            dma((4,)), dma((4,)), dma((7,)), dma((7,)),
            dma((1,)), dma((1,)), dma((CHIPS - 1,)), dma((CHIPS - 1,)),
            dma((CHIPS - 1,)), dma((CHIPS - 1,)), dma((1,)), dma((1,)),
        ],
        compiler_params=pltpu.CompilerParams(
            collective_id=0, has_side_effects=True, vmem_limit_bytes=56 << 20
        ),
        name="outer_product_mean",
    )(left_proj, right_proj, out_weight, out_bias.reshape(1, CZ), pair_cotangent)
    grad_left, grad_right, grad_weight, grad_bias, pair = pl.pallas_call(
        finish,
        out_shape=(
            jax.ShapeDtypeStruct((OWN, S * C), F32),
            jax.ShapeDtypeStruct((OWN, S * C), F32),
            jax.ShapeDtypeStruct((C * C, CZ), F32),
            jax.ShapeDtypeStruct((1, CZ), F32),
            jax.ShapeDtypeStruct((TI, TJ, CZ), BF16),
        ),
        in_specs=[hbm] * 5,
        out_specs=(hbm,) * 5,
        scratch_shapes=[
            pltpu.VMEM((OWN, S * C), F32),
            pltpu.VMEM((OWN, S * C), F32),
            pltpu.VMEM((C * C, CZ), F32),
            pltpu.VMEM((1, CZ), F32),
            pltpu.VMEM((TI, TJ, CZ), BF16),
            dma((2, 8)),
        ],
        name="finish",
    )(gl, gr, gw, gb, pair)
    return pair, grad_left, grad_right, grad_weight, grad_bias.reshape(CZ)


def solution(mesh):
    return jax.shard_map(
        per_device,
        mesh=mesh,
        in_specs=(
            P(("row", "col"), None),
            P(("col", "row"), None),
            P(),
            P(),
            P("row", "col", None),
        ),
        out_specs=(
            P("row", "col", None),
            P(("row", "col"), None),
            P(("col", "row"), None),
            P(),
            P(),
        ),
        check_vma=False,
    )
```
